32 devices in a mesh: dp: 8 (over z, x), tensor: 4 (over y, core).
Axes of the slice: x: 2, y: 2, z: 4, core: 2. Of those that a mesh axis runs over, the one named last changes fastest.
Arguments:
- tokens: bfloat16 [10976, 1280], P(('dp', 'tensor')), may hold values from -6 to 6
- grad_out: bfloat16 [10976, 1280], P(('dp', 'tensor')), may hold values from -6 to 6
- adapter_index: int32 [2], replicated, may hold values from 0 to 7
- norm1_gain: bfloat16 [1280], replicated, may hold values from 0.099609375 to 1.8984375
- norm1_shift: bfloat16 [1280], replicated, may hold values from -2.5 to 2.5
- qkv_weight: bfloat16 [1280, 3, 1280], P(None, None, 'tensor'), may hold values from -0.15625 to 0.15625
- qkv_bias: bfloat16 [3, 1280], P(None, 'tensor'), may hold values from -2.5 to 2.5
- rel_pos_h: bfloat16 [27, 80], replicated, may hold values from -1.25 to 1.25
- rel_pos_w: bfloat16 [27, 80], replicated, may hold values from -1.25 to 1.25
- proj_weight: bfloat16 [1280, 1280], P('tensor'), may hold values from -0.625 to 0.625
- proj_bias: bfloat16 [1280], replicated, may hold values from -2.5 to 2.5
- norm2_gain: bfloat16 [1280], replicated, may hold values from 0.099609375 to 1.8984375
- norm2_shift: bfloat16 [1280], replicated, may hold values from -2.5 to 2.5
- lin1_weight: bfloat16 [1280, 5120], P(None, 'tensor'), may hold values from -0.15625 to 0.15625
- lin1_bias: bfloat16 [5120], P('tensor'), may hold values from -2.5 to 2.5
- lin2_weight: bfloat16 [5120, 1280], P('tensor'), may hold values from -0.078125 to 0.078125
- lin2_bias: bfloat16 [1280], replicated, may hold values from -2.5 to 2.5
- qkv_down: bfloat16 [8, 1280, 16], replicated, may hold values from -0.15625 to 0.15625
- qkv_up: bfloat16 [8, 16, 3, 1280], P(None, None, None, 'tensor'), may hold values from -1.5 to 1.5
- proj_down: bfloat16 [8, 1280, 16], P(None, 'tensor'), may hold values from -0.625 to 0.625
- proj_up: bfloat16 [8, 16, 1280], replicated, may hold values from -1.5 to 1.5
- lin1_down: bfloat16 [8, 1280, 16], replicated, may hold values from -0.15625 to 0.15625
- lin1_up: bfloat16 [8, 16, 5120], P(None, None, 'tensor'), may hold values from -1.5 to 1.5
- lin2_down: bfloat16 [8, 5120, 16], P(None, 'tensor'), may hold values from -0.078125 to 0.078125
- lin2_up: bfloat16 [8, 16, 1280], replicated, may hold values from -1.5 to 1.5
Outputs:
- output: bfloat16 [10976, 1280], P(('dp', 'tensor'))
- grad_tokens: bfloat16 [10976, 1280], P(('dp', 'tensor'))
- grad_qkv_down: float32 [8, 1280, 16], replicated
- grad_qkv_up: float32 [8, 16, 3, 1280], P(None, None, None, 'tensor')
- grad_proj_down: float32 [8, 1280, 16], P(None, 'tensor')
- grad_proj_up: float32 [8, 16, 1280], replicated
- grad_lin1_down: float32 [8, 1280, 16], replicated
- grad_lin1_up: float32 [8, 16, 5120], P(None, None, 'tensor')
- grad_lin2_down: float32 [8, 5120, 16], P(None, 'tensor')
- grad_lin2_up: float32 [8, 16, 1280], replicated
The draws below stay inside these ranges and needn't reach their ends.
Inputs may be any that keep to these rules, and one draw needn't show every extreme that they name: `adapter_index`: one adapter for each image.
All inputs are finite; a program needn't handle non-finite values.
Results may differ from the reference program's by a relative error of at most 0.019.
Values may be sent and summed in bfloat16 or wider, within the bound.
A program may use at most 256 MiB of HBM per device.

```python
import jax
import jax.numpy as jnp
from jax import lax

D = 1280
HEADS = 16
HEAD_DIM = 80
FF = 5120
WIN = 14
SIDE = 64
RANK = 16
ADAPTERS = 8
WIN_DEV = 7
GROUP = 4
GRID = 5
IMAGES = 2
TOKENS = 10976


def level_of(stream_key, extent, cuts, low, largest):
    gain, own = 1.0, jax.random.fold_in(stream_key, 6)
    for dim, blocks in cuts:
        draws = jnp.exp(jax.random.uniform(jax.random.fold_in(own, dim), (blocks,), jnp.float32, low / len(cuts), largest / len(cuts)))
        gain = gain * jnp.repeat(draws, extent[dim] // blocks).reshape([-1 if axis == dim else 1 for axis in range(len(extent))])
    return gain


def bell_draw(rng, shape, scale, most, shards=(), kind=jnp.bfloat16):
    factor_of = level_of(rng, shape, shards, -0.22, 0.18) if shards else 1.0
    array = jax.random.normal(rng, shape, jnp.float32) * scale * factor_of
    return jnp.minimum(jnp.maximum(array, -most), most).astype(kind)


def setup_inputs(seed: int = 0) -> dict:
    streams_of = jax.random.split(jax.random.key(seed), 26)
    return {
        "tokens": bell_draw(streams_of[0], (TOKENS, D), 1.0, 6.0, ((0, 32),)),
        "grad_out": bell_draw(streams_of[1], (TOKENS, D), 1.0, 6.0, ((0, 32),)),
        "adapter_index": jax.random.randint(streams_of[2], (IMAGES,), 0, ADAPTERS).astype(jnp.int32),
        "norm1_gain": jnp.clip(1.0 + 0.18 * jax.random.normal(streams_of[3], (D,), jnp.float32), 0.099609375, 1.8984375).astype(jnp.bfloat16),
        "norm1_shift": bell_draw(streams_of[4], (D,), 0.3, 2.5),
        "qkv_weight": bell_draw(streams_of[5], (D, 3, D), D ** -0.5, 0.15625, ((2, 4),)),
        "qkv_bias": bell_draw(streams_of[6], (3, D), 0.3, 2.5, ((1, 4),)),
        "rel_pos_h": bell_draw(streams_of[7], (2 * WIN - 1, HEAD_DIM), 0.08, 1.25),
        "rel_pos_w": bell_draw(streams_of[8], (2 * WIN - 1, HEAD_DIM), 0.08, 1.25),
        "proj_weight": bell_draw(streams_of[9], (D, D), (D // 16) ** -0.5, 0.625, ((0, 4),)),
        "proj_bias": bell_draw(streams_of[10], (D,), 0.3, 2.5),
        "norm2_gain": jnp.clip(1.0 + 0.18 * jax.random.normal(streams_of[11], (D,), jnp.float32), 0.099609375, 1.8984375).astype(jnp.bfloat16),
        "norm2_shift": bell_draw(streams_of[12], (D,), 0.3, 2.5),
        "lin1_weight": bell_draw(streams_of[13], (D, FF), D ** -0.5, 0.15625, ((1, 4),)),
        "lin1_bias": bell_draw(streams_of[14], (FF,), 0.3, 2.5, ((0, 4),)),
        "lin2_weight": bell_draw(streams_of[15], (FF, D), FF ** -0.5, 0.078125, ((0, 4),)),
        "lin2_bias": bell_draw(streams_of[16], (D,), 0.3, 2.5),
        "qkv_down": bell_draw(streams_of[17], (ADAPTERS, D, RANK), D ** -0.5, 0.15625),
        "qkv_up": bell_draw(streams_of[18], (ADAPTERS, RANK, 3, D), RANK ** -0.5, 1.5, ((3, 4),)),
        "proj_down": bell_draw(streams_of[19], (ADAPTERS, D, RANK), (D // 16) ** -0.5, 0.625, ((1, 4),)),
        "proj_up": bell_draw(streams_of[20], (ADAPTERS, RANK, D), RANK ** -0.5, 1.5),
        "lin1_down": bell_draw(streams_of[21], (ADAPTERS, D, RANK), D ** -0.5, 0.15625),
        "lin1_up": bell_draw(streams_of[22], (ADAPTERS, RANK, FF), RANK ** -0.5, 1.5, ((2, 4),)),
        "lin2_down": bell_draw(streams_of[23], (ADAPTERS, FF, RANK), FF ** -0.5, 0.078125, ((1, 4),)),
        "lin2_up": bell_draw(streams_of[24], (ADAPTERS, RANK, D), RANK ** -0.5, 1.5),
    }


@jax.custom_vjp
def low(v):
    return lax.optimization_barrier(v.astype(jnp.bfloat16)).astype(jnp.float32)

@jax.custom_vjp
def low_back(v):
    return v

def low_keep(v):
    return (low(v), None)

def low_pass(kept, grad):
    return (grad,)

def back_keep(v):
    return (v, None)

def back_low(kept, grad):
    return (low(grad),)
low.defvjp(low_keep, low_pass)
low_back.defvjp(back_keep, back_low)
HIGH = lax.Precision.HIGHEST
ADAPT = 0.5
EPS = 1e-06

def exact_dot(first_op, second_op):
    return jnp.dot(first_op, second_op, precision=HIGH)

def layer_norm(values, norm_gain, norm_shift):
    row_mean = lax.optimization_barrier(jnp.mean(values, axis=-1, keepdims=True))
    centered = values - row_mean
    variance = lax.optimization_barrier(jnp.mean(centered * centered, axis=-1, keepdims=True))
    return centered * lax.rsqrt(variance + EPS) * norm_gain + norm_shift

def valid_rows():
    count_all = GROUP * WIN_DEV * WIN * WIN
    position = jnp.arange(count_all, dtype=jnp.int32)
    slot_index = position // (WIN * WIN)
    within = position % (WIN * WIN)
    image_row = slot_index // GRID * WIN + within // WIN
    image_col = slot_index % GRID * WIN + within % WIN
    inside = (slot_index < GRID * GRID) & (image_row < SIDE) & (image_col < SIDE)
    return jnp.where(inside, 1.0, 0.0).astype(jnp.float32)[:, None]

def offset_table(position_table):
    offsets = (jnp.arange(WIN, dtype=jnp.int32)[:, None] - jnp.arange(WIN, dtype=jnp.int32)[None, :] + WIN - 1).astype(jnp.int32)
    return position_table[offsets]

def to_windows(values):
    return values.reshape(-1, WIN, WIN, HEADS, HEAD_DIM).transpose(0, 3, 1, 2, 4)

def from_windows(values):
    return values.transpose(0, 2, 3, 1, 4).reshape(-1, HEADS * HEAD_DIM)

def attention(queries, key_win, value_win, table_h, table_w):
    win_count = queries.shape[0]
    tokens_win = WIN * WIN
    base_scores = jnp.einsum('nhqc,nhkc->nhqk', queries.reshape(win_count, HEADS, tokens_win, HEAD_DIM), key_win.reshape(win_count, HEADS, tokens_win, HEAD_DIM), precision=HIGH) * HEAD_DIM ** (-0.5)
    rel_rows = jnp.einsum('nhabc,akc->nhabk', queries, table_h, precision=HIGH)
    rel_cols = jnp.einsum('nhabc,bkc->nhabk', queries, table_w, precision=HIGH)
    scores = base_scores.reshape(win_count, HEADS, WIN, WIN, WIN, WIN) + rel_rows[:, :, :, :, :, None] + rel_cols[:, :, :, :, None, :]
    scores = low_back(scores.reshape(win_count, HEADS, tokens_win, tokens_win))
    probs = jax.nn.softmax(scores, axis=-1)
    attended = jnp.einsum('nhqk,nhkc->nhqc', low(probs), value_win.reshape(win_count, HEADS, tokens_win, HEAD_DIM), precision=HIGH)
    return attended.reshape(queries.shape)

def block(image_rows, valid, pick, adapters, weights, table_h, table_w):
    norm1_gain, norm1_shift, qkv_weight, qkv_bias, proj_weight, proj_bias, norm2_gain, norm2_shift, lin1_weight, lin1_bias, lin2_weight, lin2_bias = weights
    chosen = tuple((lax.dynamic_index_in_dim(table_all, pick, 0, keepdims=False) for table_all in adapters))
    qkv_down, qkv_up, proj_down, proj_up, lin1_down, lin1_up, lin2_down, lin2_up = chosen
    row_count = image_rows.shape[0]
    xn1 = low(valid * layer_norm(image_rows, norm1_gain, norm1_shift))
    qkv = exact_dot(xn1, qkv_weight.reshape(D, 3 * D)) + qkv_bias.reshape(3 * D) + ADAPT * exact_dot(exact_dot(xn1, qkv_down), qkv_up.reshape(RANK, 3 * D))
    qkv = qkv.reshape(row_count, 3, D)
    queries = to_windows(low_back(low(qkv[:, 0])))
    key_win = to_windows(low_back(low(qkv[:, 1])))
    value_win = to_windows(low_back(low(qkv[:, 2])))
    att = low_back(low(from_windows(attention(queries, key_win, value_win, table_h, table_w))))
    branch_a = low_back(exact_dot(att, proj_weight) + ADAPT * exact_dot(exact_dot(att, proj_down), proj_up) + proj_bias)
    middle = image_rows + valid * branch_a
    xn2 = low(layer_norm(middle, norm2_gain, norm2_shift))
    hidden_pre = low_back(exact_dot(xn2, lin1_weight) + lin1_bias + ADAPT * exact_dot(exact_dot(xn2, lin1_down), lin1_up))
    hidden_act = low(jax.nn.gelu(hidden_pre, approximate=False))
    branch_m = low_back(exact_dot(hidden_act, lin2_weight) + ADAPT * exact_dot(exact_dot(hidden_act, lin2_down), lin2_up) + lin2_bias)
    return middle + valid * branch_m

def reference(tokens, grad_out, adapter_index, norm1_gain, norm1_shift, qkv_weight, qkv_bias, rel_pos_h, rel_pos_w, proj_weight, proj_bias, norm2_gain, norm2_shift, lin1_weight, lin1_bias, lin2_weight, lin2_bias, qkv_down, qkv_up, proj_down, proj_up, lin1_down, lin1_up, lin2_down, lin2_up):
    weights = tuple((item.astype(jnp.float32) for item in (norm1_gain, norm1_shift, qkv_weight, qkv_bias, proj_weight, proj_bias, norm2_gain, norm2_shift, lin1_weight, lin1_bias, lin2_weight, lin2_bias)))
    adapters = tuple((item.astype(jnp.float32) for item in (qkv_down, qkv_up, proj_down, proj_up, lin1_down, lin1_up, lin2_down, lin2_up)))
    table_h = offset_table(rel_pos_h.astype(jnp.float32))
    table_w = offset_table(rel_pos_w.astype(jnp.float32))
    valid = valid_rows()
    per_image = GROUP * WIN_DEV * WIN * WIN
    inputs_all = tokens.astype(jnp.float32).reshape(-1, per_image, D)
    cotangents = grad_out.astype(jnp.float32).reshape(-1, per_image, D)

    def one_image(carry, item):
        image_rows, cotangent, pick = item

        def forward(rows_in, adapters_in):
            return block(rows_in, valid, pick, adapters_in, weights, table_h, table_w)
        result, backward = jax.vjp(forward, image_rows, adapters)
        grad_rows, grad_adapters = backward(cotangent)
        carry = jax.tree.map(lambda total, term: total + term, carry, grad_adapters)
        return (carry, (result.astype(jnp.bfloat16), grad_rows.astype(jnp.bfloat16)))
    zeros_all = tuple((jnp.zeros(item.shape, jnp.float32) for item in adapters))
    grads, (results, grad_rows) = lax.scan(one_image, zeros_all, (inputs_all, cotangents, adapter_index.astype(jnp.int32)))
    return (results.reshape(-1, D), grad_rows.reshape(-1, D), grads[0], grads[1], grads[2], grads[3], grads[4], grads[5], grads[6], grads[7])
```

```python
import functools

import jax
import jax.numpy as jnp
import numpy as np
from jax import lax
from jax.experimental import pallas as pl
from jax.experimental.pallas import tpu as pltpu
from jax.sharding import PartitionSpec as P

HEAD_DIM = 80
WIN = 14
SIDE = 64
RANK = 16
ADAPTERS = 8
WIN_DEV = 7
GROUP = 4
GRID = 5
TOK = WIN * WIN
PAD = 208
NW = 2
R = NW * PAD
D = 1280
LOC = 320
LP = 384
HID = 1280
HC = 256
PACK = 3584
EXT = 32
HALF = 0.5
EPS = 1e-6
SCALE = HEAD_DIM**-0.5
MESH = pl.DeviceIdType.MESH
BF = jnp.bfloat16
F32 = jnp.float32
SPAN = ((0, 128), (0, 256), (128, 128), (128, 256))
ERF_P = 0.3275911
ERF_A = (0.254829592, -0.284496736, 1.421413741, -1.453152027, 1.061405429)

CHUNKS = (
    [("q", 0, 320), ("q", 320, 320), ("q", 640, 320), ("p", 0, 320)]
    + [("1", 320 * i, 320) for i in range(4)]
    + [("2", 256 * i, 256) for i in range(5)]
)
NCH = len(CHUNKS)
THIRDS = {80: ((2, 2, 1), (2, 1, 2), (1, 2, 2)), 64: ((2, 1, 1), (1, 2, 1), (1, 1, 2))}


def nn(a, b):
    return jnp.dot(a, b, preferred_element_type=F32)


def nt(a, b):
    return lax.dot_general(a, b, (((1,), (1,)), ((), ())), preferred_element_type=F32)


def tn(a, b):
    return lax.dot_general(a, b, (((0,), (0,)), ((), ())), preferred_element_type=F32)


def mult(v, m=16):
    return v if isinstance(v, int) else pl.multiple_of(v, m)


class Wire:
    def __init__(self, own, land, pack_own, pack_land, sems):
        self.own, self.land, self.sems = own, land, sems
        self.pack_own, self.pack_land = pack_own, pack_land
        dp, t = lax.axis_index("dp"), lax.axis_index("tensor")
        self.q = lax.rem(dp, 4)
        self.dev = {"x": (dp ^ 1, t), "z": (dp ^ 2, t), "y": (dp, t ^ 2), "c": (dp, t ^ 1)}
        self.count = {}

    def barrier(self):
        bar = pltpu.get_barrier_semaphore()
        for d in self.dev.values():
            pl.semaphore_signal(bar, inc=1, device_id=d, device_id_type=MESH)
        pl.semaphore_wait(bar, len(self.dev))

    def copy(self, key, src, dst, dev):
        n = self.count.setdefault(key, len(self.count))
        return pltpu.make_async_remote_copy(
            src_ref=src,
            dst_ref=dst,
            send_sem=self.sems.at[0, n],
            recv_sem=self.sems.at[1, n],
            device_id=self.dev[dev],
            device_id_type=MESH,
        )

    def pack(self, what):
        return {
            "c": lambda: self.copy("pc", self.pack_own, self.pack_land.at[1], "c"),
            "y": lambda: self.copy("py", self.pack_own, self.pack_land.at[2], "y"),
            "f": lambda: self.copy("pf", self.pack_land.at[2], self.pack_land.at[3], "c"),
        }[what]()

    def parts(self, c):
        name, first, rows = CHUNKS[c]
        quarter = rows // 4
        a, b, d = (16 * v for v in THIRDS[quarter][c % 3])
        q = self.q

        def at(quart, off, n):
            return pl.ds(mult(first + quart * quarter + off), n)

        return {
            "y1": at(q, 0, quarter),
            "y2": at(q ^ 3, 0, a),
            "x1": at(q ^ 1, 0, quarter),
            "z1": at(q ^ 2, 0, quarter),
            "d": at(q ^ 3, a, b + d),
            "xs": at(q, 0, quarter),
            "x2": at(q ^ 2, a, b),
            "z2": at(q ^ 1, a + b, d),
        }

    def piece(self, c, what):
        name, first, rows = CHUNKS[c]
        own, land = self.own[name], self.land[name]
        p = self.parts(c)
        if what == "s":
            s = pl.ds(first, rows)
            return self.copy((c, what), own.at[s], land.at[1, s], "c")
        if what in ("y1", "y2"):
            return self.copy((c, what), own.at[p[what]], land.at[2, p[what]], "y")
        if what in ("x1", "z1"):
            return self.copy((c, what), land.at[2, p["xs"]], land.at[2, p["xs"]], what[0])
        if what in ("x2", "z2"):
            return self.copy((c, what), land.at[2, p[what]], land.at[2, p[what]], what[0])
        r = p[what[1:]]
        return self.copy((c, what), land.at[2, r], land.at[3, r], "c")

    def begin(self):
        self.pack("c").start()
        self.pack("y").start()
        for c in range(NCH):
            self.piece(c, "y1").start()
            self.piece(c, "y2").start()
            self.piece(c, "s").start()

    def step(self, n):
        if n == 0:
            self.pack("y").wait_recv()
            self.pack("f").start()
        if n < NCH:
            for w in ("y1", "y2"):
                self.piece(n, w).wait_recv()
            for w in ("x1", "z1", "cy1", "cy2"):
                self.piece(n, w).start()
        if 0 <= n - 1 < NCH:
            for w in ("x1", "z1"):
                self.piece(n - 1, w).wait_recv()
            for w in ("x2", "z2", "cx1", "cz1"):
                self.piece(n - 1, w).start()
        if 0 <= n - 2 < NCH:
            for w in ("x2", "z2"):
                self.piece(n - 2, w).wait_recv()
            self.piece(n - 2, "cd").start()

    def have(self, k, chunks):
        for c in chunks:
            if k == 1:
                self.piece(c, "s").wait_recv()
            if k == 3:
                for w in ("cy1", "cy2", "cx1", "cz1", "cd"):
                    self.piece(c, w).wait_recv()

    def finish(self):
        for w in "cyf":
            self.pack(w).wait_send()
        for c in range(NCH):
            for w in ("s", "y1", "y2", "x1", "z1", "x2", "z2", "cy1", "cy2", "cx1", "cz1", "cd"):
                self.piece(c, w).wait_send()


STEPS = NCH + 2


def shifted(values, shift, right):
    for bit in (1, 2, 4, 8):
        moved = pltpu.roll(values, bit if right else 128 - bit, 1)
        values = jnp.where((shift & bit) > 0, moved, values)
    return values


def join_heads(parts):
    lane = lax.broadcasted_iota(jnp.int32, (PAD, 128), 1)
    t0 = jnp.where(lane < 80, parts[0], parts[1][:, :128])
    t1 = jnp.where(
        lane < 32, parts[1][:, 128:], jnp.where(lane < 112, parts[2], parts[3][:, :128])
    )
    return (t0, t1, parts[3][:, 128:])


def head_mask(h, dtype=BF):
    base, width = SPAN[h]
    low = HEAD_DIM * h - base
    lane = lax.broadcasted_iota(jnp.int32, (1, width), 1)
    return jnp.where((lane >= low) & (lane < low + HEAD_DIM), 1.0, 0.0).astype(dtype)


def stats(v):
    mean = jnp.mean(v, axis=-1, keepdims=True)
    cen = v - mean
    inv = lax.rsqrt(jnp.mean(cen * cen, axis=-1, keepdims=True) + EPS)
    return cen * inv, inv


def norm_back(grad, xhat, inv, gain):
    e = grad * gain
    return inv * (
        e
        - jnp.mean(e, axis=-1, keepdims=True)
        - xhat * jnp.mean(e * xhat, axis=-1, keepdims=True)
    )


def row_loop(body, rows=32):
    def one(i, _):
        body(pl.ds(mult(i * rows, 32), rows))
        return 0

    lax.fori_loop(0, R // rows, one, 0)


def ticks(wire, place, index):
    for n, at in place.items():

        @pl.when(index == at)
        def _():
            wire.step(n)


def kernel(
    x_hbm, g_hbm, wq_hbm, wp_hbm, w1_hbm, w2_hbm, pack_hbm,
    vec_ref, adp_ref, valid_ref, shift_ref, rel_ref, hot_ref, back_ref, key_ref,
    out_hbm, grad_hbm, g_rep, g_bq, g_ap, g_b1, g_a2,
    x_s, g_s, wq, wp, w1, w2, pack, xn_s, q_s, k_s, v_s, att_s, p_s, mid_s, acc_a, acc_b,
    datt_s, d1t_s, up2t_s, d1_s, up2_s, d2_s, up1_s, upq_s, dqt_s, sems, local,
):
    own = {"q": wq_hbm, "p": wp_hbm, "1": w1_hbm, "2": w2_hbm}
    land = {"q": wq, "p": wp, "1": w1, "2": w2}
    wire = Wire(own, land, pack_hbm, pack, sems)
    wire.barrier()
    wire.begin()
    pairs = [
        (x_hbm, x_s), (pack_hbm, pack.at[0]), (wq_hbm, wq.at[0]), (wp_hbm, wp.at[0]),
        (g_hbm, g_s), (w1_hbm, w1.at[0]), (w2_hbm, w2.at[0]),
    ]
    loads = [pltpu.make_async_copy(a, b, local.at[i]) for i, (a, b) in enumerate(pairs)]
    for cp in loads:
        cp.start()
    lane_pad = jnp.zeros((4, R, LP - 256), BF)
    for ref in (q_s, k_s, v_s, att_s):
        ref[:, :, 256:LP] = lane_pad
    datt_s[:, 256:LP] = lane_pad[0]

    gain1, shift1, gain2, shift2 = (vec_ref[i : i + 1, :] for i in range(4))
    bias_p, bias_2 = vec_ref[4:5, :], vec_ref[5:6, :]
    a_q, a_1, b_p, b_2 = (adp_ref[i] for i in range(4))
    lane_e = lax.broadcasted_iota(jnp.int32, (R, EXT), 1)
    valid = valid_ref[...]

    loads[0].wait()

    def norm_one(rows):
        xhat, _ = stats(x_s[rows, :].astype(F32))
        xn_s[rows, :] = (valid_ref[rows, :] * (xhat * gain1 + shift1)).astype(BF)

    row_loop(norm_one)
    loads[1].wait()
    down_q = HALF * nt(xn_s[...], a_q)
    dq_ext = jnp.where(lane_e == RANK, 1.0, down_q).astype(BF)
    d1_s[...] = dq_ext
    dqt_s[...] = down_q.T.astype(BF)
    loads[2].wait()

    def heads_forward(k, _):
        @pl.when(k == 1)
        def _():
            wire.pack("c").wait_recv()
            wire.have(1, range(3))

        @pl.when(k == 2)
        def _():
            for n in range(5):
                wire.step(n)

        @pl.when(k == 3)
        def _():
            wire.pack("f").wait_recv()
            wire.have(3, range(3))

        qkv = nt(xn_s[...], wq[k]) + nn(d1_s[...], pack[k, :, 0 : 3 * LOC])
        q_s[k, :, 0:LOC] = qkv[:, 0:LOC].astype(BF)
        k_s[k, :, 0:LOC] = qkv[:, LOC : 2 * LOC].astype(BF)
        v_s[k, :, 0:LOC] = qkv[:, 2 * LOC : 3 * LOC].astype(BF)

        def window(w, _):
            rows = pl.ds(mult(w * PAD), PAD)
            shift = shift_ref[...]
            lane = lax.broadcasted_iota(jnp.int32, (PAD, 128), 1)
            fine = (lane & 32) > 0
            outs = []
            for h in range(4):
                b, n = SPAN[h]
                lanes = slice(b, b + n)
                qm = q_s[k, rows, lanes] * head_mask(h)
                scores = nt(qm, k_s[k, rows, lanes]) * SCALE
                u = shifted(nt(qm, rel_ref[h, :, lanes]), shift, False)
                rest = u - u.astype(BF).astype(F32)
                u = jnp.where(fine, pltpu.roll(rest, 32, 1), u).astype(BF)
                scores = scores + nn(u, hot_ref[...]) + key_ref[...]
                top = jnp.max(scores, axis=1, keepdims=True)
                e = jnp.exp(scores - top)
                p = (e * (1.0 / jnp.sum(e, axis=1, keepdims=True))).astype(BF)
                p_s[(k * NW + w) * 4 + h] = p
                outs.append(nn(p, v_s[k, rows, lanes]))
            for i, part in enumerate(join_heads(outs)):
                att_s[k, rows, 128 * i : 128 * i + 128] = part.astype(BF)
            return 0

        lax.fori_loop(0, NW, window, 0)
        return 0

    lax.fori_loop(0, 4, heads_forward, 0)

    loads[3].wait()
    wire.have(1, [3])
    wire.step(5)
    wire.have(3, [3])
    down_p = jnp.zeros((R, RANK), F32)
    for k in range(4):
        down_p += nt(att_s[k, :, 0:LOC], pack[k, 16:32, 2304 : 2304 + LOC])
    down_p = HALF * down_p
    dp16 = down_p.astype(BF)
    dpt = down_p.T.astype(BF)
    for n in range(5):
        cols = slice(256 * n, 256 * n + 256)
        total = nn(dp16, b_p[:RANK, cols]) + bias_p[:, cols]
        for k in range(4):
            total += nn(att_s[k, :, 0:LOC], wp[k, :, cols])
        acc_a[:, cols] = total

    def norm_two(rows):
        mid = x_s[rows, :].astype(F32) + valid_ref[rows, :] * acc_a[rows, :]
        mid_s[rows, :] = mid
        xhat, _ = stats(mid)
        xn_s[rows, :] = (xhat * gain2 + shift2).astype(BF)

    row_loop(norm_two)
    down_1 = HALF * nt(xn_s[...], a_1)
    d1_s[...] = jnp.where(lane_e == RANK, 1.0, down_1).astype(BF)
    d1t_s[...] = down_1.T.astype(BF)
    loads[4].wait()
    up2 = HALF * valid * nt(g_s[...], b_2)
    up2_s[...] = up2.astype(BF)
    up2t_s[...] = up2.T.astype(BF)
    acc_a[...] = jnp.zeros((R, D), F32)
    acc_b[...] = jnp.zeros((R, D), F32)
    d2_s[...] = jnp.zeros((R, EXT), F32)
    up1_s[...] = jnp.zeros((R, EXT), F32)
    loads[5].wait()
    loads[6].wait()

    def hidden(i, _):
        late = i - 10
        k = jnp.where(i < 5, 0, jnp.where(i < 10, 1, 2 + lax.rem(late + 10, 2)))
        c = jnp.where(i < 10, lax.rem(i, 5), (late + 10) // 2 - 5)

        @pl.when(i == 5)
        def _():
            wire.have(1, range(4, NCH))

        ticks(wire, {6: 2, 7: 6, 8: 9, 9: 10, 10: 10, 11: 12, 12: 14, 13: 16, 14: 18}, i)

        @pl.when(i == 11)
        def _():
            wire.have(3, range(4, 8))

        for j in range(5):

            @pl.when(i == 11 + 2 * j)
            def _():
                wire.have(3, [8 + j])

        cols = pl.ds(mult(c * HC, HC), HC)
        pcols = pl.ds(mult(1024 + c * HC, HC), HC)
        acols = pl.ds(mult(2304 + c * HC, HC), HC)
        pre = nn(xn_s[...], w1[k, :, cols]) + nn(d1_s[...], pack[k, :, pcols])
        gauss = jnp.exp(-0.5 * pre * pre)
        t = 1.0 / (1.0 + (ERF_P * 0.5**0.5) * jnp.abs(pre))
        poly = ERF_A[4]
        for a in ERF_A[3::-1]:
            poly = poly * t + a
        tail = (HALF * poly) * t * gauss
        phi = jnp.where(pre >= 0, 1.0 - tail, tail)
        act = (pre * phi).astype(BF)
        slope = phi + pre * gauss * 0.3989422804014327
        a2 = pack[k, :, acols]
        g_a2[k, :, cols] = nn(up2t_s[...], act)[:RANK]
        d2_s[...] += nt(act, a2)
        dact = valid * nt(g_s[...], w2[k, cols, :]) + nn(up2_s[...], a2)
        dpre = (dact * slope).astype(BF)
        g_b1[k, :, cols] = nn(d1t_s[...], dpre)[:RANK]
        up1_s[...] += nt(dpre, pack[k, :, pcols])
        for n in range(5):
            out = slice(256 * n, 256 * n + 256)
            acc_a[:, out] += nn(act, w2[k, cols, out])
            acc_b[:, out] += nt(dpre, w1[k, out, cols])
        return 0

    lax.fori_loop(0, 20, hidden, 0)

    d2 = HALF * d2_s[...]
    d2b = d2.astype(BF)
    up1 = HALF * up1_s[...]
    up1b = up1.astype(BF)
    g_rep[3] = nn((d2 * valid).T.astype(BF), g_s[...])[:RANK]
    g_rep[2] = nn(up1.T.astype(BF), xn_s[...])[:RANK]
    for n in range(5):
        cols = slice(256 * n, 256 * n + 256)
        acc_a[:, cols] += nn(d2b, b_2[:, cols])
        acc_b[:, cols] += nn(up1b, a_1[:, cols])

    def back_two(rows):
        mid = mid_s[rows, :]
        ok = valid_ref[rows, :]
        x_out = mid + ok * (acc_a[rows, :] + bias_2)
        xhat, inv = stats(mid)
        dmid = g_s[rows, :].astype(F32) + norm_back(acc_b[rows, :], xhat, inv, gain2)
        mid_s[rows, :] = dmid
        g_s[rows, :] = (ok * dmid).astype(BF)
        xn_s[rows, :] = x_out.astype(BF)

    row_loop(back_two)
    put_out = pltpu.make_async_copy(xn_s, out_hbm, local.at[7])
    put_out.start()
    upp = HALF * nt(g_s[...], b_p)
    upp16 = upp[:, :RANK].astype(BF)
    uppt = upp.T.astype(BF)
    g_rep[1] = nn(dpt, g_s[...])
    acc_a[...] = jnp.zeros((R, D), F32)
    upq_s[...] = jnp.zeros((R, EXT), F32)
    up2_s[:, 0:RANK] = upp16
    up2t_s[...] = uppt

    def heads_backward(k, _):
        datt = nt(g_s[...], wp[k]) + nn(up2_s[:, 0:RANK], pack[k, 16:32, 2304 : 2304 + LOC])
        datt_s[:, 0:LOC] = datt.astype(BF)
        g_ap[k] = nn(up2t_s[...], att_s[k, :, 0:LOC])[:RANK]

        def window(w, _):
            rows = pl.ds(mult(w * PAD), PAD)
            shift = shift_ref[...]
            dqs, dks, dvs = [], [], []
            for h in range(4):
                b, n = SPAN[h]
                lanes = slice(b, b + n)
                p = p_s[(k * NW + w) * 4 + h]
                da = datt_s[rows, lanes]
                dprob = nt(da * head_mask(h), v_s[k, rows, lanes])
                dvs.append(tn(p, da))
                pf = p.astype(F32)
                inner = jnp.sum(pf * dprob, axis=1, keepdims=True)
                ds = (pf * (dprob - inner)).astype(BF)
                du = shifted(nn(ds, back_ref[...]), shift, True).astype(BF)
                dqs.append(nn(ds, k_s[k, rows, lanes]) * SCALE + nn(du, rel_ref[h, :, lanes]))
                dks.append(tn(ds, q_s[k, rows, lanes]) * SCALE)
            for ref, parts in ((q_s, dqs), (k_s, dks), (v_s, dvs)):
                for i, part in enumerate(join_heads(parts)):
                    ref[k, rows, 128 * i : 128 * i + 128] = part.astype(BF)
            return 0

        lax.fori_loop(0, NW, window, 0)
        for j, ref in enumerate((q_s, k_s, v_s)):
            d = ref[k, :, 0:LOC]
            b = pack[k, :, j * LOC : (j + 1) * LOC]
            upq_s[...] += nt(d, b)
            g_bq[k, j] = nn(dqt_s[...], d)[:RANK]
        for n in range(5):
            cols = slice(256 * n, 256 * n + 256)
            total = acc_a[:, cols]
            for j, ref in enumerate((q_s, k_s, v_s)):
                total += nn(ref[k, :, 0:LOC], wq[k, j * LOC : (j + 1) * LOC, cols])
            acc_a[:, cols] = total
        return 0

    lax.fori_loop(0, 4, heads_backward, 0)
    put_out.wait()

    upq = HALF * upq_s[...]
    upqb = upq.astype(BF)
    upqt = upq.T.astype(BF)
    for n in range(5):
        cols = slice(256 * n, 256 * n + 256)
        acc_a[:, cols] += nn(upqb, a_q[:, cols])

    def back_one(rows):
        ok = valid_ref[rows, :]
        xhat, inv = stats(x_s[rows, :].astype(F32))
        xn_s[rows, :] = (ok * (xhat * gain1 + shift1)).astype(BF)
        back = norm_back(ok * acc_a[rows, :], xhat, inv, gain1)
        g_s[rows, :] = (mid_s[rows, :] + back).astype(BF)

    row_loop(back_one)
    put_grad = pltpu.make_async_copy(g_s, grad_hbm, local.at[8])
    put_grad.start()
    g_rep[0] = nn(upqt, xn_s[...])[:RANK]
    put_grad.wait()
    wire.finish()


def tables(rel_pos_h, rel_pos_w):
    flip = np.zeros((2, 128, 2 * WIN - 1), np.float32)
    for i in range(2 * WIN - 1):
        flip[0, i, 2 * WIN - 2 - i] = 1
        flip[1, 64 + i, 2 * WIN - 2 - i] = 1
    rel = jnp.dot(flip[0].astype(BF), rel_pos_h) + jnp.dot(flip[1].astype(BF), rel_pos_w)
    zero = lambda n: jnp.zeros((128, n), BF)
    rel = jnp.stack(
        [
            jnp.concatenate([zero(80 * h), rel, zero(LP - 80 * h - 80)], axis=1)
            for h in range(LOC // HEAD_DIM)
        ]
    )
    tok = np.arange(PAD)
    inside = tok < TOK
    row, col = tok // WIN, tok % WIN
    lane = np.arange(128)[:, None]
    hot = (
        (((lane == row) | (lane == 32 + row)) & inside)
        | (((lane == 64 + col) | (lane == 96 + col)) & inside)
    ).astype(np.float32)
    back = ((lane == row) | (lane == 64 + col)) & inside
    shift = np.where(np.arange(128)[None] < 64, 13 - row[:, None], 13 - col[:, None])
    shift = np.where(inside[:, None], shift, 0).astype(np.int32)
    key = np.where(inside, 0.0, -1e30).astype(np.float32)[None]
    return rel, jnp.asarray(hot, BF), jnp.asarray(back.T, BF), jnp.asarray(shift), jnp.asarray(key)


def call_kernel(args):
    any_ = pl.BlockSpec(memory_space=pl.ANY)
    vmem = pl.BlockSpec(memory_space=pltpu.VMEM)
    sds = jax.ShapeDtypeStruct
    V = pltpu.VMEM
    return pl.pallas_call(
        kernel,
        out_shape=(
            sds((R, D), BF),
            sds((R, D), BF),
            sds((4, RANK, D), F32),
            sds((4, 3, RANK, LOC), F32),
            sds((4, RANK, LOC), F32),
            sds((4, RANK, HID), F32),
            sds((4, RANK, HID), F32),
        ),
        in_specs=[any_] * 7 + [vmem] * 8,
        out_specs=(any_, any_) + (vmem,) * 5,
        scratch_shapes=[
            V((R, D), BF),
            V((R, D), BF),
            V((4, 3 * LOC, D), BF),
            V((4, LOC, D), BF),
            V((4, D, HID), BF),
            V((4, HID, D), BF),
            V((4, EXT, PACK), BF),
            V((R, D), BF),
            V((4, R, LP), BF),
            V((4, R, LP), BF),
            V((4, R, LP), BF),
            V((4, R, LP), BF),
            V((4 * NW * 4, PAD, PAD), BF),
            V((R, D), F32),
            V((R, D), F32),
            V((R, D), F32),
            V((R, LP), BF),
            V((EXT, R), BF),
            V((EXT, R), BF),
            V((R, EXT), BF),
            V((R, EXT), BF),
            V((R, EXT), F32),
            V((R, EXT), F32),
            V((R, EXT), F32),
            V((EXT, R), BF),
            pltpu.SemaphoreType.DMA((2, 12 * NCH + 3)),
            pltpu.SemaphoreType.DMA((9,)),
        ],
        compiler_params=pltpu.CompilerParams(
            collective_id=0, has_side_effects=True, vmem_limit_bytes=66_500_000
        ),
        name="block",
    )(*args)


def on_device(
    tokens,
    grad_out,
    adapter_index,
    norm1_gain,
    norm1_shift,
    qkv_weight,
    qkv_bias,
    rel_pos_h,
    rel_pos_w,
    proj_weight,
    proj_bias,
    norm2_gain,
    norm2_shift,
    lin1_weight,
    lin1_bias,
    lin2_weight,
    lin2_bias,
    qkv_down,
    qkv_up,
    proj_down,
    proj_up,
    lin1_down,
    lin1_up,
    lin2_down,
    lin2_up,
):
    tensor_size = lax.axis_size("tensor")
    images = adapter_index.shape[0]
    row_count = tokens.shape[0]
    t = lax.axis_index("tensor")
    dp_place = lax.axis_index("dp")
    image = dp_place // GROUP
    pick = jnp.sum(jnp.where(jnp.arange(images) == image, adapter_index, 0))

    def select(table_all):
        return lax.dynamic_index_in_dim(table_all, pick, 0, keepdims=False)

    work = NW * TOK
    gap = work - row_count
    far = gap * (tensor_size - 1)
    both = jnp.stack([tokens, grad_out])
    more = lax.ppermute(both[:, :far], "tensor", [(s, s - 1) for s in range(1, tensor_size)])
    none = jnp.zeros((2, gap, D), BF)
    both = lax.dynamic_slice_in_dim(jnp.concatenate([both, more, none], axis=1), gap * t, work, 1)
    both = jnp.pad(both.reshape(2, NW, TOK, D), ((0, 0), (0, 0), (0, PAD - TOK), (0, 0)))
    x, g = both.reshape(2, R, D)

    place = jnp.arange(R, dtype=jnp.int32)
    window = place // PAD + NW * t
    slot = dp_place % GROUP * WIN_DEV + window
    within = place % PAD
    image_row = slot // GRID * WIN + within // WIN
    image_col = slot % GRID * WIN + within % WIN
    valid = (within < TOK) & (window < WIN_DEV) & (slot < GRID * GRID)
    valid = valid & (image_row < SIDE) & (image_col < SIDE)
    valid = jnp.where(valid, 1.0, 0.0).astype(F32)[:, None]

    wq = jnp.transpose(qkv_weight, (1, 2, 0)).reshape(3 * LOC, D)
    row = lambda v: v.reshape(1, -1)
    bq = jnp.transpose(select(qkv_up), (0, 1, 2)).reshape(RANK, 3 * LOC)
    pad_rows = lambda v, n: jnp.pad(v, ((0, n - v.shape[0]), (0, 0)))
    bq = pad_rows(jnp.concatenate([bq, row(qkv_bias)]), EXT)
    b1 = pad_rows(jnp.concatenate([select(lin1_up), row(lin1_bias)]), EXT)
    low = jnp.concatenate(
        [select(lin2_down).T, jnp.pad(select(proj_down).T, ((0, 0), (0, HID - LOC)))]
    )
    pack = jnp.concatenate([bq, jnp.zeros((EXT, 1024 - 3 * LOC), BF), b1, low], axis=1)
    vecs = jnp.stack([norm1_gain, norm1_shift, norm2_gain, norm2_shift, proj_bias, lin2_bias])
    vecs = jnp.pad(vecs.astype(F32), ((0, 2), (0, 0)))
    adps = jnp.stack([select(qkv_down).T, select(lin1_down).T, select(proj_up), select(lin2_up)])
    adps = jnp.pad(adps, ((0, 0), (0, EXT - RANK), (0, 0)))
    rel, hot, back, shift, key = tables(rel_pos_h, rel_pos_w)
    out, grad, g_rep, g_bq, g_ap, g_b1, g_a2 = call_kernel(
        (x, g, wq, proj_weight, lin1_weight, lin2_weight, pack,
         vecs, adps, valid, shift, rel, hot, back, key)
    )

    ends = jnp.stack([out, grad]).reshape(2, NW, PAD, D)[:, :, :TOK].reshape(2, work, D)
    more = lax.ppermute(
        ends[:, work - far :], "tensor", [(s, s + 1) for s in range(tensor_size - 1)]
    )
    ends = jnp.concatenate([more, ends], axis=1)
    output, grad_tokens = lax.dynamic_slice_in_dim(ends, far - gap * t, row_count, 1)

    order = t ^ jnp.arange(tensor_size)
    split = jnp.concatenate(
        [v.reshape(tensor_size, -1) for v in (g_bq, g_ap, g_b1, g_a2)], axis=1
    )
    split = lax.psum_scatter(split[order], "tensor", scatter_dimension=0, tiled=False)
    mine = jnp.where(jnp.arange(images) == image, 1.0, 0.0).astype(F32)
    split = lax.psum(mine[:, None] * split[None], "dp")
    whole = lax.psum(mine[:, None, None, None] * g_rep[None], ("dp", "tensor"))
    slots = jnp.where(
        jnp.arange(ADAPTERS)[:, None] == adapter_index[None], 1.0, 0.0
    ).astype(F32)
    to_slots = lambda v: jnp.einsum("ai,i...->a...", slots, v, precision=lax.Precision.HIGHEST)
    split, whole = to_slots(split), to_slots(whole)
    sizes = np.cumsum([3 * RANK * LOC, RANK * LOC, RANK * HID])
    s_bq, s_ap, s_b1, s_a2 = jnp.split(split, sizes, axis=1)
    swap = lambda v: jnp.swapaxes(v, 1, 2)
    return (
        output,
        grad_tokens,
        swap(whole[:, 0]),
        jnp.swapaxes(s_bq.reshape(ADAPTERS, 3, RANK, LOC), 1, 2),
        swap(s_ap.reshape(ADAPTERS, RANK, LOC)),
        whole[:, 1],
        swap(whole[:, 2]),
        s_b1.reshape(ADAPTERS, RANK, HID),
        swap(s_a2.reshape(ADAPTERS, RANK, HID)),
        whole[:, 3],
    )


def solution(mesh):
    placed = (
        P(("dp", "tensor"), None),
        P(("dp", "tensor"), None),
        P(),
        P(),
        P(),
        P(None, None, "tensor"),
        P(None, "tensor"),
        P(),
        P(),
        P("tensor", None),
        P(),
        P(),
        P(),
        P(None, "tensor"),
        P("tensor"),
        P("tensor", None),
        P(),
        P(),
        P(None, None, None, "tensor"),
        P(None, "tensor", None),
        P(),
        P(),
        P(None, None, "tensor"),
        P(None, "tensor", None),
        P(),
    )
    return jax.shard_map(
        on_device,
        mesh=mesh,
        in_specs=placed,
        out_specs=(
            P(("dp", "tensor"), None),
            P(("dp", "tensor"), None),
            P(),
            P(None, None, None, "tensor"),
            P(None, "tensor", None),
            P(),
            P(),
            P(None, None, "tensor"),
            P(None, "tensor", None),
            P(),
        ),
        check_vma=False,
    )
```

```python
import functools

import jax
import jax.numpy as jnp
import numpy as np
from jax import lax
from jax.experimental import pallas as pl
from jax.experimental.pallas import tpu as pltpu
from jax.sharding import PartitionSpec as P

HEAD_DIM = 80
WIN = 14
SIDE = 64
RANK = 16
ADAPTERS = 8
WIN_DEV = 7
GROUP = 4
GRID = 5
TOK = WIN * WIN
PAD = 208
NW = 2
R = NW * PAD
D = 1280
LOC = 320
LP = 384
HID = 1280
HC = 256
PACK = 3584
ROWS = 352
EXT = 32
HALF = 0.5
EPS = 1e-6
SCALE = HEAD_DIM**-0.5
MESH = pl.DeviceIdType.MESH
BF = jnp.bfloat16
F32 = jnp.float32
SPAN = ((0, 128), (0, 256), (128, 128), (128, 256))
ERF_P = 0.3275911
ERF_A = (0.254829592, -0.284496736, 1.421413741, -1.453152027, 1.061405429)

CHUNKS = (
    [("q", 0, 320), ("q", 320, 320), ("q", 640, 320), ("p", 0, 320)]
    + [("1", 320 * i, 320) for i in range(4)]
    + [("2", 256 * i, 256) for i in range(5)]
)
NCH = len(CHUNKS)
THIRDS = {80: ((2, 2, 1), (2, 1, 2), (1, 2, 2)), 64: ((2, 1, 1), (1, 2, 1), (1, 1, 2))}


def nn(a, b):
    return jnp.dot(a, b, preferred_element_type=F32)


def nt(a, b):
    return lax.dot_general(a, b, (((1,), (1,)), ((), ())), preferred_element_type=F32)


def tn(a, b):
    return lax.dot_general(a, b, (((0,), (0,)), ((), ())), preferred_element_type=F32)


def mult(v, m=16):
    return v if isinstance(v, int) else pl.multiple_of(v, m)


class Wire:
    def __init__(self, own, land, pack_own, pack_land, sems, images):
        self.own, self.land, self.sems = own, land, sems
        self.pack_own, self.pack_land = pack_own, pack_land
        dp, t = lax.axis_index("dp"), lax.axis_index("tensor")
        self.q = lax.rem(dp, 4)
        self.t = t
        self.image = dp // GROUP
        self.levels = images.bit_length() - 1
        self.dev = {"x": (dp ^ 1, t), "z": (dp ^ 2, t), "d": (dp ^ 3, t)}
        self.dev |= {"c": (dp, t ^ 1), "y": (dp, t ^ 2), "yc": (dp, t ^ 3)}
        self.dev |= {f"i{b}": (dp ^ (GROUP << b), t) for b in range(self.levels)}
        self.near = {"next": (dp, lax.rem(t + 1, 4)), "prev": (dp, lax.rem(t + 3, 4))}
        self.count = {}

    def barrier(self):
        bar = pltpu.get_barrier_semaphore()
        for d in self.dev.values():
            pl.semaphore_signal(bar, inc=1, device_id=d, device_id_type=MESH)
        pl.semaphore_wait(bar, len(self.dev))

    def copy(self, key, src, dst, dev):
        n = self.count.setdefault(key, len(self.count))
        return pltpu.make_async_remote_copy(
            src_ref=src,
            dst_ref=dst,
            send_sem=self.sems.at[0, n],
            recv_sem=self.sems.at[1, n],
            device_id=(self.dev | self.near)[dev],
            device_id_type=MESH,
        )

    def ready(self, sem):
        for d in self.dev.values():
            pl.semaphore_signal(sem, inc=1, device_id=d, device_id_type=MESH)

    def all_ready(self, sem):
        pl.semaphore_wait(sem, len(self.dev))

    def edge(self, key, src, dst, forward, do):
        for s in range(1, 4):
            n = 16 * -(-49 * s // 16)
            at, to = (s - 1, s) if forward else (s, s - 1)

            @pl.when(self.t == (at if do != "wait" else to))
            def _():
                cp = self.copy((key, s), src(n), dst(n), "next" if forward else "prev")
                getattr(cp, {"go": "start", "wait": "wait_recv", "end": "wait_send"}[do])()

    def pack(self, what):
        return {
            "c": lambda: self.copy("pc", self.pack_own, self.pack_land.at[1], "c"),
            "y": lambda: self.copy("py", self.pack_own, self.pack_land.at[2], "y"),
            "f": lambda: self.copy("pf", self.pack_land.at[2], self.pack_land.at[3], "c"),
        }[what]()

    def parts(self, c):
        name, first, rows = CHUNKS[c]
        quarter = rows // 4
        a, b, d = (16 * v for v in THIRDS[quarter][c % 3])
        q = self.q

        def at(quart, off, n):
            return pl.ds(mult(first + quart * quarter + off), n)

        return {
            "y1": at(q, 0, quarter),
            "y2": at(q ^ 3, 0, a),
            "x1": at(q ^ 1, 0, quarter),
            "z1": at(q ^ 2, 0, quarter),
            "d": at(q ^ 3, a, b + d),
            "xs": at(q, 0, quarter),
            "x2": at(q ^ 2, a, b),
            "z2": at(q ^ 1, a + b, d),
        }

    def piece(self, c, what):
        name, first, rows = CHUNKS[c]
        own, land = self.own[name], self.land[name]
        p = self.parts(c)
        if what == "s":
            s = pl.ds(first, rows)
            return self.copy((c, what), own.at[s], land.at[1, s], "c")
        if what in ("y1", "y2"):
            return self.copy((c, what), own.at[p[what]], land.at[2, p[what]], "y")
        if what in ("x1", "z1"):
            return self.copy((c, what), land.at[2, p["xs"]], land.at[2, p["xs"]], what[0])
        if what in ("x2", "z2"):
            return self.copy((c, what), land.at[2, p[what]], land.at[2, p[what]], what[0])
        r = p[what[1:]]
        return self.copy((c, what), land.at[2, r], land.at[3, r], "c")

    def begin(self):
        self.pack("c").start()
        self.pack("y").start()
        for c in range(NCH):
            self.piece(c, "y1").start()
            self.piece(c, "y2").start()
            self.piece(c, "s").start()

    def step(self, n):
        if n == 0:
            self.pack("y").wait_recv()
            self.pack("f").start()
        if n < NCH:
            for w in ("y1", "y2"):
                self.piece(n, w).wait_recv()
            for w in ("x1", "z1", "cy1", "cy2"):
                self.piece(n, w).start()
        if 0 <= n - 1 < NCH:
            for w in ("x1", "z1"):
                self.piece(n - 1, w).wait_recv()
            for w in ("x2", "z2", "cx1", "cz1"):
                self.piece(n - 1, w).start()
        if 0 <= n - 2 < NCH:
            for w in ("x2", "z2"):
                self.piece(n - 2, w).wait_recv()
            self.piece(n - 2, "cd").start()

    def have(self, k, chunks):
        for c in chunks:
            if k == 1:
                self.piece(c, "s").wait_recv()
            if k == 3:
                for w in ("cy1", "cy2", "cx1", "cz1", "cd"):
                    self.piece(c, w).wait_recv()

    def finish(self):
        for w in "cyf":
            self.pack(w).wait_send()
        for c in range(NCH):
            for w in ("s", "y1", "y2", "x1", "z1", "x2", "z2", "cy1", "cy2", "cx1", "cz1", "cd"):
                self.piece(c, w).wait_send()


class Sum:
    def __init__(self, wire, name, send, buf, images):
        self.wire, self.name, self.send, self.buf, self.images = wire, name, send, buf, images
        self.n = send.shape[1]

    def go(self, key, src, dst, dev, do):
        cp = self.wire.copy((self.name, key), src, dst, dev)
        getattr(cp, {"go": "start", "wait": "wait_recv", "end": "wait_send"}[do])()

    def first(self, k, rows, do):
        dev = {1: "c", 2: "y", 3: "yc"}[k]
        dst = self.buf.at[1, pl.ds((k - 1) * self.n + rows.start, rows.size)]
        self.go(("a", k, rows.start), self.send.at[k, rows], dst, dev, do)

    def second(self, do):
        n = self.n
        for j, dev in enumerate("xzd"):
            src, dst = self.buf.at[1, pl.ds(3 * n, n)], self.buf.at[1, pl.ds((4 + j) * n, n)]
            self.go(("b", j), src, dst, dev, do)

    def third(self, level, do):
        n, size = self.n, 1 << level
        start = (self.wire.image >> level) << level
        if do == "wait":
            start = start ^ size
        rows = pl.ds(mult(start * n), size * n)
        self.go(("i", level), self.buf.at[2, rows], self.buf.at[2, rows], f"i{level}", do)

    def fourth(self, do):
        m, t = self.images * RANK, self.wire.t
        for k in (1, 2, 3):
            owner = t if do != "wait" else t ^ k
            part = self.buf.at[3, pl.ds(mult(owner * m), m), pl.ds(0, D // 2)]
            self.go(("r", k), part, part, {1: "c", 2: "y", 3: "yc"}[k], do)

    def finish(self, split):
        for k in (1, 2, 3):
            for rows in split:
                self.first(k, rows, "end")
        self.second("end")
        for b in range(self.wire.levels):
            self.third(b, "end")
        self.fourth("end")

    def part(self, slab, i):
        return self.buf[slab, i * self.n : (i + 1) * self.n, :].astype(F32)

    def add_first(self, split):
        for k in (1, 2, 3):
            for rows in split:
                self.first(k, rows, "wait")
        total = self.send[0].astype(F32) + self.part(1, 0) + self.part(1, 1) + self.part(1, 2)
        self.buf[1, 3 * self.n : 4 * self.n, :] = total.astype(BF)
        self.second("go")

    def add_second(self):
        self.second("wait")
        total = self.part(1, 3) + self.part(1, 4) + self.part(1, 5) + self.part(1, 6)
        self.buf[2, pl.ds(mult(self.wire.image * self.n), self.n), :] = total.astype(BF)
        if self.wire.levels:
            self.third(0, "go")

    def add_third(self):
        for b in range(self.wire.levels):
            self.third(b, "wait")
            if b + 1 < self.wire.levels:
                self.third(b + 1, "go")
        n, m = self.n, self.images * RANK
        for i in range(self.images):
            own = pl.ds(mult(self.wire.t * m + i * RANK), RANK)
            self.buf[3, own, 0 : D // 2] = self.buf[
                2, (i + 1) * n - RANK : (i + 1) * n, 0 : D // 2
            ]
        self.fourth("go")

    def hand_out(self, split_out, whole_out, local):
        self.fourth("wait")
        n, m = self.n, self.images * RANK
        copies = [
            pltpu.make_async_copy(self.buf.at[2, 0 : self.images * n], split_out, local.at[0]),
            pltpu.make_async_copy(self.buf.at[3, 0 : 4 * m, 0 : D // 2], whole_out, local.at[1]),
        ]
        for cp in copies:
            cp.start()
        return copies


def half_of(ref, wire, k):
    s = wire.t ^ k
    return ref[s >> 1, :, pl.ds(mult((s & 1) * (D // 2), 128), D // 2)]


def one_hot(target, count):
    lane = lax.broadcasted_iota(jnp.int32, (target.shape[0], count), 1)
    return jnp.where(lane == target, 1.0, 0.0).astype(BF)


def window_rows(t):
    r = lax.broadcasted_iota(jnp.int32, (R, 1), 0)
    w = jnp.where(r >= PAD, 1, 0)
    i = r - PAD * w
    p = 49 * t + TOK * w + i
    source = jnp.where(i < TOK, jnp.where(p < 343, p, p + (ROWS - 343)), -1)
    slot = lax.rem(lax.axis_index("dp"), GROUP) * WIN_DEV + NW * t + w
    high = (slot * 205) >> 10
    row = (i * 4682) >> 16
    ok = (i < TOK) & (NW * t + w < WIN_DEV) & (slot < GRID * GRID)
    ok = ok & (high * WIN + row < SIDE) & ((slot - GRID * high) * WIN + i - WIN * row < SIDE)
    return source, jnp.where(ok, 1.0, 0.0).astype(F32)


def home_rows(t, mine, fetched):
    r = lax.broadcasted_iota(jnp.int32, (ROWS, 1), 0)
    o = r - 49 * t
    here = jnp.where(o < 0, -1, jnp.where(o < TOK, o, o + PAD - TOK))
    there = jnp.where(o < 0, r + 4 - t, -1)
    here, there = one_hot(here, R), one_hot(there, 160)
    return lambda cols: (nn(here, mine[:, cols]) + nn(there, fetched[:, cols])).astype(BF)


STEPS = NCH + 2


def shifted(values, shift, right):
    for bit in (1, 2, 4, 8):
        moved = pltpu.roll(values, bit if right else 128 - bit, 1)
        values = jnp.where((shift & bit) > 0, moved, values)
    return values


def join_heads(parts):
    lane = lax.broadcasted_iota(jnp.int32, (PAD, 128), 1)
    t0 = jnp.where(lane < 80, parts[0], parts[1][:, :128])
    t1 = jnp.where(
        lane < 32, parts[1][:, 128:], jnp.where(lane < 112, parts[2], parts[3][:, :128])
    )
    return (t0, t1, parts[3][:, 128:])


def head_mask(h, dtype=BF):
    base, width = SPAN[h]
    low = HEAD_DIM * h - base
    lane = lax.broadcasted_iota(jnp.int32, (1, width), 1)
    return jnp.where((lane >= low) & (lane < low + HEAD_DIM), 1.0, 0.0).astype(dtype)


def stats(v):
    mean = jnp.mean(v, axis=-1, keepdims=True)
    cen = v - mean
    inv = lax.rsqrt(jnp.mean(cen * cen, axis=-1, keepdims=True) + EPS)
    return cen * inv, inv


def norm_back(grad, xhat, inv, gain):
    e = grad * gain
    return inv * (
        e
        - jnp.mean(e, axis=-1, keepdims=True)
        - xhat * jnp.mean(e * xhat, axis=-1, keepdims=True)
    )


def row_loop(body, rows=32):
    def one(i, _):
        body(pl.ds(mult(i * rows, 32), rows))
        return 0

    lax.fori_loop(0, R // rows, one, 0)


def ticks(wire, place, index):
    for n, at in place.items():

        @pl.when(index == at)
        def _():
            wire.step(n)


def kernel(
    images,
    x_hbm, g_hbm, wq_hbm, wp_hbm, w1_hbm, w2_hbm, pack_hbm,
    vec_ref, adp_ref, shift_ref, rel_ref, hot_ref, back_ref, key_ref,
    out_hbm, grad_hbm, split_1, whole_1, split_2, whole_2,
    x_s, g_s, wq, wp, w1, w2, pack, xn_s, q_s, k_s, v_s, att_s, p_s, mid_s, acc_a, acc_b,
    datt_s, d1t_s, up2t_s, d1_s, up2_s, d2_s, up1_s, upq_s, dqt_s, valid_ref, sum_1, sum_2,
    rep_s, sems, local, done,
):
    own = {"q": wq_hbm, "p": wp_hbm, "1": w1_hbm, "2": w2_hbm}
    land = {"q": wq, "p": wp, "1": w1, "2": w2}
    wire = Wire(own, land, pack_hbm, pack, sems, images)
    total_1 = Sum(wire, "s1", sum_1, w1, images)
    total_2 = Sum(wire, "s2", sum_2, w2, images)
    t = wire.t
    blank = jnp.zeros((512 - ROWS, D), BF)
    w1[0, ROWS:512, :] = blank
    w2[0, ROWS:512, :] = blank
    wire.barrier()
    for key, src, dst in (("ex", x_hbm, w1), ("eg", g_hbm, w2)):
        wire.edge(key, lambda n: src.at[0:n], lambda n: dst.at[0, ROWS : ROWS + n], False, "go")
        if key == "ex":
            wire.begin()
    pairs = [
        (x_hbm, w1.at[0, 0:ROWS]), (pack_hbm, pack.at[0]), (wq_hbm, wq.at[0]),
        (wp_hbm, wp.at[0]), (g_hbm, w2.at[0, 0:ROWS]), (w1_hbm, w1.at[0]), (w2_hbm, w2.at[0]),
    ]
    loads = [pltpu.make_async_copy(a, b, local.at[i]) for i, (a, b) in enumerate(pairs)]
    for cp in loads[:5]:
        cp.start()
    lane_pad = jnp.zeros((4, R, LP - 256), BF)
    for ref in (q_s, k_s, v_s, att_s):
        ref[:, :, 256:LP] = lane_pad
    datt_s[:, 256:LP] = lane_pad[0]

    gain1, shift1, gain2, shift2 = (vec_ref[i : i + 1, :] for i in range(4))
    bias_p, bias_2 = vec_ref[4:5, :], vec_ref[5:6, :]
    a_q, a_1, b_p, b_2 = (adp_ref[i] for i in range(4))
    lane_e = lax.broadcasted_iota(jnp.int32, (R, EXT), 1)
    source, valid = window_rows(t)
    valid_ref[...] = valid
    pick_rows = one_hot(source, 512)

    loads[0].wait()
    wire.edge("ex", lambda n: x_hbm.at[0:n], lambda n: w1.at[0, ROWS : ROWS + n], False, "wait")
    for n in range(5):
        cols = slice(256 * n, 256 * n + 256)
        x_s[:, cols] = nn(pick_rows, w1[0, 0:512, cols]).astype(BF)
    loads[5].start()

    def norm_one(rows):
        xhat, _ = stats(x_s[rows, :].astype(F32))
        xn_s[rows, :] = (valid_ref[rows, :] * (xhat * gain1 + shift1)).astype(BF)

    row_loop(norm_one)
    loads[1].wait()
    down_q = HALF * nt(xn_s[...], a_q)
    dq_ext = jnp.where(lane_e == RANK, 1.0, down_q).astype(BF)
    d1_s[...] = dq_ext
    dqt_s[...] = down_q.T.astype(BF)
    loads[2].wait()

    def heads_forward(k, _):
        @pl.when(k == 1)
        def _():
            wire.pack("c").wait_recv()
            wire.have(1, range(3))

        @pl.when(k == 2)
        def _():
            for n in range(5):
                wire.step(n)

        @pl.when(k == 3)
        def _():
            wire.pack("f").wait_recv()
            wire.have(3, range(3))

        qkv = nt(xn_s[...], wq[k]) + nn(d1_s[...], pack[k, :, 0 : 3 * LOC])
        q_s[k, :, 0:LOC] = qkv[:, 0:LOC].astype(BF)
        k_s[k, :, 0:LOC] = qkv[:, LOC : 2 * LOC].astype(BF)
        v_s[k, :, 0:LOC] = qkv[:, 2 * LOC : 3 * LOC].astype(BF)

        def window(w, _):
            rows = pl.ds(mult(w * PAD), PAD)
            shift = shift_ref[...]
            lane = lax.broadcasted_iota(jnp.int32, (PAD, 128), 1)
            fine = (lane & 32) > 0
            outs = []
            for h in range(4):
                b, n = SPAN[h]
                lanes = slice(b, b + n)
                qm = q_s[k, rows, lanes] * head_mask(h)
                scores = nt(qm, k_s[k, rows, lanes]) * SCALE
                u = shifted(nt(qm, rel_ref[h, :, lanes]), shift, False)
                rest = u - u.astype(BF).astype(F32)
                u = jnp.where(fine, pltpu.roll(rest, 32, 1), u).astype(BF)
                scores = scores + nn(u, hot_ref[...]) + key_ref[...]
                top = jnp.max(scores, axis=1, keepdims=True)
                e = jnp.exp(scores - top)
                p = (e * (1.0 / jnp.sum(e, axis=1, keepdims=True))).astype(BF)
                p_s[(k * NW + w) * 4 + h] = p
                outs.append(nn(p, v_s[k, rows, lanes]))
            for i, part in enumerate(join_heads(outs)):
                att_s[k, rows, 128 * i : 128 * i + 128] = part.astype(BF)
            return 0

        lax.fori_loop(0, NW, window, 0)
        return 0

    lax.fori_loop(0, 4, heads_forward, 0)

    loads[3].wait()
    wire.have(1, [3])
    wire.step(5)
    wire.have(3, [3])
    down_p = jnp.zeros((R, RANK), F32)
    for k in range(4):
        down_p += nt(att_s[k, :, 0:LOC], pack[k, 16:32, 2304 : 2304 + LOC])
    down_p = HALF * down_p
    dp16 = down_p.astype(BF)
    dpt = down_p.T.astype(BF)
    for n in range(5):
        cols = slice(256 * n, 256 * n + 256)
        total = nn(dp16, b_p[:RANK, cols]) + bias_p[:, cols]
        for k in range(4):
            total += nn(att_s[k, :, 0:LOC], wp[k, :, cols])
        acc_a[:, cols] = total

    def norm_two(rows):
        mid = x_s[rows, :].astype(F32) + valid_ref[rows, :] * acc_a[rows, :]
        mid_s[rows, :] = mid
        xhat, _ = stats(mid)
        xn_s[rows, :] = (xhat * gain2 + shift2).astype(BF)

    row_loop(norm_two)
    down_1 = HALF * nt(xn_s[...], a_1)
    d1_s[...] = jnp.where(lane_e == RANK, 1.0, down_1).astype(BF)
    d1t_s[...] = down_1.T.astype(BF)
    loads[4].wait()
    wire.edge("eg", lambda n: g_hbm.at[0:n], lambda n: w2.at[0, ROWS : ROWS + n], False, "wait")
    pick_rows = one_hot(window_rows(t)[0], 512)
    for n in range(5):
        cols = slice(256 * n, 256 * n + 256)
        g_s[:, cols] = nn(pick_rows, w2[0, 0:512, cols]).astype(BF)
    loads[6].start()
    valid = valid_ref[...]
    up2 = HALF * valid * nt(g_s[...], b_2)
    up2_s[...] = up2.astype(BF)
    up2t_s[...] = up2.T.astype(BF)
    acc_a[...] = jnp.zeros((R, D), F32)
    acc_b[...] = jnp.zeros((R, D), F32)
    d2_s[...] = jnp.zeros((R, EXT), F32)
    up1_s[...] = jnp.zeros((R, EXT), F32)
    loads[5].wait()
    loads[6].wait()

    def hidden(i, _):
        late = i - 10
        k = jnp.where(i < 5, 0, jnp.where(i < 10, 1, 2 + lax.rem(late + 10, 2)))
        c = jnp.where(i < 10, lax.rem(i, 5), (late + 10) // 2 - 5)

        @pl.when(i == 5)
        def _():
            wire.have(1, range(4, NCH))

        ticks(wire, {6: 2, 7: 6, 8: 9, 9: 10, 10: 10, 11: 12, 12: 14, 13: 16, 14: 18}, i)

        @pl.when(i == 11)
        def _():
            wire.have(3, range(4, 8))

        for j in range(5):

            @pl.when(i == 11 + 2 * j)
            def _():
                wire.have(3, [8 + j])

        cols = pl.ds(mult(c * HC, HC), HC)
        pcols = pl.ds(mult(1024 + c * HC, HC), HC)
        acols = pl.ds(mult(2304 + c * HC, HC), HC)
        pre = nn(xn_s[...], w1[k, :, cols]) + nn(d1_s[...], pack[k, :, pcols])
        gauss = jnp.exp(-0.5 * pre * pre)
        t = 1.0 / (1.0 + (ERF_P * 0.5**0.5) * jnp.abs(pre))
        poly = ERF_A[4]
        for a in ERF_A[3::-1]:
            poly = poly * t + a
        tail = (HALF * poly) * t * gauss
        phi = jnp.where(pre >= 0, 1.0 - tail, tail)
        act = (pre * phi).astype(BF)
        slope = phi + pre * gauss * 0.3989422804014327
        a2 = pack[k, :, acols]
        sum_1[k, RANK : 2 * RANK, cols] = nn(up2t_s[...], act)[:RANK].astype(BF)
        d2_s[...] += nt(act, a2)
        dact = valid_ref[...] * nt(g_s[...], w2[k, cols, :]) + nn(up2_s[...], a2)
        dpre = (dact * slope).astype(BF)
        sum_1[k, 0:RANK, cols] = nn(d1t_s[...], dpre)[:RANK].astype(BF)
        up1_s[...] += nt(dpre, pack[k, :, pcols])
        for n in range(5):
            out = slice(256 * n, 256 * n + 256)
            acc_a[:, out] += nn(act, w2[k, cols, out])
            acc_b[:, out] += nt(dpre, w1[k, out, cols])
        return 0

    lax.fori_loop(0, 20, hidden, 0)

    wire.finish()
    wire.edge("ex", lambda n: x_hbm.at[0:n], lambda n: w1.at[0, ROWS : ROWS + n], False, "end")
    wire.edge("eg", lambda n: g_hbm.at[0:n], lambda n: w2.at[0, ROWS : ROWS + n], False, "end")
    wire.ready(done)
    d2 = HALF * d2_s[...]
    d2b = d2.astype(BF)
    up1 = HALF * up1_s[...]
    up1b = up1.astype(BF)
    rep_s[1] = nn((d2 * valid_ref[...]).T.astype(BF), g_s[...])[:RANK].astype(BF)
    rep_s[0] = nn(up1.T.astype(BF), xn_s[...])[:RANK].astype(BF)
    for k in range(4):
        sum_1[k, 2 * RANK :, 0 : D // 2] = half_of(rep_s, wire, k)
        sum_1[k, 2 * RANK :, D // 2 :] = jnp.zeros((RANK, D // 2), BF)
    wire.all_ready(done)
    all_1 = pl.ds(0, 3 * RANK)
    for k in (1, 2, 3):
        total_1.first(k, all_1, "go")
    for n in range(5):
        cols = slice(256 * n, 256 * n + 256)
        acc_a[:, cols] += nn(d2b, b_2[:, cols])
        acc_b[:, cols] += nn(up1b, a_1[:, cols])

    def back_two(rows):
        mid = mid_s[rows, :]
        ok = valid_ref[rows, :]
        x_out = mid + ok * (acc_a[rows, :] + bias_2)
        xhat, inv = stats(mid)
        dmid = g_s[rows, :].astype(F32) + norm_back(acc_b[rows, :], xhat, inv, gain2)
        mid_s[rows, :] = dmid
        g_s[rows, :] = (ok * dmid).astype(BF)
        xn_s[rows, :] = x_out.astype(BF)

    row_loop(back_two)

    def swap_edge(key, src, dst, do):
        to = lambda n: dst.at[0, 512 : 512 + n]
        wire.edge(key, lambda n: src.at[R - n : R], to, True, do)

    swap_edge("eo", xn_s, w1, "go")
    upp = HALF * nt(g_s[...], b_p)
    upp16 = upp[:, :RANK].astype(BF)
    uppt = upp.T.astype(BF)
    rep_s[1] = nn(dpt, g_s[...]).astype(BF)
    acc_a[...] = jnp.zeros((R, D), F32)
    upq_s[...] = jnp.zeros((R, EXT), F32)
    up2_s[:, 0:RANK] = upp16
    up2t_s[...] = uppt

    put_out = pltpu.make_async_copy(w1.at[0, 0:ROWS], out_hbm, local.at[7])

    def heads_backward(step, _):
        k = lax.rem(step + 1, 4)

        @pl.when(step == 1)
        def _():
            total_1.add_first([all_1])
            swap_edge("eo", xn_s, w1, "wait")
            home = home_rows(t, xn_s, w1.at[0, 512:672])
            for n in range(5):
                cols = slice(256 * n, 256 * n + 256)
                w1[0, 0:ROWS, cols] = home(cols)
            put_out.start()

        @pl.when(step == 2)
        def _():
            total_1.add_second()

        @pl.when(step == 3)
        def _():
            total_1.add_third()

        datt = nt(g_s[...], wp[k]) + nn(up2_s[:, 0:RANK], pack[k, 16:32, 2304 : 2304 + LOC])
        datt_s[:, 0:LOC] = datt.astype(BF)
        sum_2[k, 0:RANK, 3 * LOC :] = nn(up2t_s[...], att_s[k, :, 0:LOC])[:RANK].astype(BF)

        def window(w, _):
            rows = pl.ds(mult(w * PAD), PAD)
            shift = shift_ref[...]
            dqs, dks, dvs = [], [], []
            for h in range(4):
                b, n = SPAN[h]
                lanes = slice(b, b + n)
                p = p_s[(k * NW + w) * 4 + h]
                da = datt_s[rows, lanes]
                dprob = nt(da * head_mask(h), v_s[k, rows, lanes])
                dvs.append(tn(p, da))
                pf = p.astype(F32)
                inner = jnp.sum(pf * dprob, axis=1, keepdims=True)
                ds = (pf * (dprob - inner)).astype(BF)
                du = shifted(nn(ds, back_ref[...]), shift, True).astype(BF)
                dqs.append(nn(ds, k_s[k, rows, lanes]) * SCALE + nn(du, rel_ref[h, :, lanes]))
                dks.append(tn(ds, q_s[k, rows, lanes]) * SCALE)
            for ref, parts in ((q_s, dqs), (k_s, dks), (v_s, dvs)):
                for i, part in enumerate(join_heads(parts)):
                    ref[k, rows, 128 * i : 128 * i + 128] = part.astype(BF)
            return 0

        lax.fori_loop(0, NW, window, 0)
        for j, ref in enumerate((q_s, k_s, v_s)):
            d = ref[k, :, 0:LOC]
            b = pack[k, :, j * LOC : (j + 1) * LOC]
            upq_s[...] += nt(d, b)
            sum_2[k, 0:RANK, j * LOC : (j + 1) * LOC] = nn(dqt_s[...], d)[:RANK].astype(BF)
        for n in range(5):
            cols = slice(256 * n, 256 * n + 256)
            total = acc_a[:, cols]
            for j, ref in enumerate((q_s, k_s, v_s)):
                total += nn(ref[k, :, 0:LOC], wq[k, j * LOC : (j + 1) * LOC, cols])
            acc_a[:, cols] = total

        for kk in (1, 2, 3):

            @pl.when(k == kk)
            def _():
                total_2.first(kk, pl.ds(0, RANK), "go")

        return 0

    lax.fori_loop(0, 4, heads_backward, 0)
    puts = total_1.hand_out(split_1, whole_1, local.at[9:11])
    put_out.wait()
    swap_edge("eo", xn_s, w1, "end")

    upq = HALF * upq_s[...]
    upqb = upq.astype(BF)
    upqt = upq.T.astype(BF)
    for n in range(5):
        cols = slice(256 * n, 256 * n + 256)
        acc_a[:, cols] += nn(upqb, a_q[:, cols])

    def back_one(rows):
        ok = valid_ref[rows, :]
        xhat, inv = stats(x_s[rows, :].astype(F32))
        xn_s[rows, :] = (ok * (xhat * gain1 + shift1)).astype(BF)
        back = norm_back(ok * acc_a[rows, :], xhat, inv, gain1)
        g_s[rows, :] = (mid_s[rows, :] + back).astype(BF)

    row_loop(back_one)
    swap_edge("ef", g_s, w2, "go")
    rep_s[0] = nn(upqt, xn_s[...])[:RANK].astype(BF)
    for k in range(4):
        sum_2[k, RANK:, 0 : D // 2] = half_of(rep_s, wire, k)
        sum_2[k, RANK:, D // 2 :] = jnp.zeros((RANK, D // 2), BF)
    low, high = pl.ds(0, RANK), pl.ds(RANK, RANK)
    for k in (1, 2, 3):
        total_2.first(k, high, "go")
    total_2.add_first([low, high])
    swap_edge("ef", g_s, w2, "wait")
    home = home_rows(t, g_s, w2.at[0, 512:672])
    for n in range(5):
        cols = slice(256 * n, 256 * n + 256)
        w2[0, 0:ROWS, cols] = home(cols)
    put_grad = pltpu.make_async_copy(w2.at[0, 0:ROWS], grad_hbm, local.at[8])
    put_grad.start()
    total_2.add_second()
    total_2.add_third()
    puts += total_2.hand_out(split_2, whole_2, local.at[11:13])
    for cp in puts:
        cp.wait()
    put_grad.wait()
    swap_edge("ef", g_s, w2, "end")
    total_1.finish([all_1])
    total_2.finish([low, high])


def tables(rel_pos_h, rel_pos_w):
    flip = np.zeros((2, 128, 2 * WIN - 1), np.float32)
    for i in range(2 * WIN - 1):
        flip[0, i, 2 * WIN - 2 - i] = 1
        flip[1, 64 + i, 2 * WIN - 2 - i] = 1
    rel = jnp.dot(flip[0].astype(BF), rel_pos_h) + jnp.dot(flip[1].astype(BF), rel_pos_w)
    zero = lambda n: jnp.zeros((128, n), BF)
    rel = jnp.stack(
        [
            jnp.concatenate([zero(80 * h), rel, zero(LP - 80 * h - 80)], axis=1)
            for h in range(LOC // HEAD_DIM)
        ]
    )
    tok = np.arange(PAD)
    inside = tok < TOK
    row, col = tok // WIN, tok % WIN
    lane = np.arange(128)[:, None]
    hot = (
        (((lane == row) | (lane == 32 + row)) & inside)
        | (((lane == 64 + col) | (lane == 96 + col)) & inside)
    ).astype(np.float32)
    back = ((lane == row) | (lane == 64 + col)) & inside
    shift = np.where(np.arange(128)[None] < 64, 13 - row[:, None], 13 - col[:, None])
    shift = np.where(inside[:, None], shift, 0).astype(np.int32)
    key = np.where(inside, 0.0, -1e30).astype(np.float32)[None]
    return rel, jnp.asarray(hot, BF), jnp.asarray(back.T, BF), jnp.asarray(shift), jnp.asarray(key)


def call_kernel(images, args):
    any_ = pl.BlockSpec(memory_space=pl.ANY)
    vmem = pl.BlockSpec(memory_space=pltpu.VMEM)
    sds = jax.ShapeDtypeStruct
    V = pltpu.VMEM
    return pl.pallas_call(
        functools.partial(kernel, images),
        out_shape=(
            sds((ROWS, D), BF),
            sds((ROWS, D), BF),
            sds((images * 3 * RANK, D), BF),
            sds((4 * images * RANK, D // 2), BF),
            sds((images * 2 * RANK, D), BF),
            sds((4 * images * RANK, D // 2), BF),
        ),
        in_specs=[any_] * 7 + [vmem] * 7,
        out_specs=(any_,) * 6,
        scratch_shapes=[
            V((R, D), BF),
            V((R, D), BF),
            V((4, 3 * LOC, D), BF),
            V((4, LOC, D), BF),
            V((4, D, HID), BF),
            V((4, HID, D), BF),
            V((4, EXT, PACK), BF),
            V((R, D), BF),
            V((4, R, LP), BF),
            V((4, R, LP), BF),
            V((4, R, LP), BF),
            V((4, R, LP), BF),
            V((4 * NW * 4, PAD, PAD), BF),
            V((R, D), F32),
            V((R, D), F32),
            V((R, D), F32),
            V((R, LP), BF),
            V((EXT, R), BF),
            V((EXT, R), BF),
            V((R, EXT), BF),
            V((R, EXT), BF),
            V((R, EXT), F32),
            V((R, EXT), F32),
            V((R, EXT), F32),
            V((EXT, R), BF),
            V((R, 1), F32),
            V((4, 3 * RANK, D), BF),
            V((4, 2 * RANK, D), BF),
            V((2, RANK, D), BF),
            pltpu.SemaphoreType.DMA((2, 12 * NCH + 60)),
            pltpu.SemaphoreType.DMA((13,)),
            pltpu.SemaphoreType.REGULAR,
        ],
        compiler_params=pltpu.CompilerParams(
            collective_id=0, has_side_effects=True, vmem_limit_bytes=66_500_000
        ),
        name="block",
    )(*args)


def on_device(
    tokens,
    grad_out,
    adapter_index,
    norm1_gain,
    norm1_shift,
    qkv_weight,
    qkv_bias,
    rel_pos_h,
    rel_pos_w,
    proj_weight,
    proj_bias,
    norm2_gain,
    norm2_shift,
    lin1_weight,
    lin1_bias,
    lin2_weight,
    lin2_bias,
    qkv_down,
    qkv_up,
    proj_down,
    proj_up,
    lin1_down,
    lin1_up,
    lin2_down,
    lin2_up,
):
    images = adapter_index.shape[0]
    row_count = tokens.shape[0]
    dp_place = lax.axis_index("dp")
    image = dp_place // GROUP
    pick = jnp.sum(jnp.where(jnp.arange(images) == image, adapter_index, 0))

    def select(table_all):
        return lax.dynamic_index_in_dim(table_all, pick, 0, keepdims=False)

    both = [jnp.pad(v, ((0, ROWS - v.shape[0]), (0, 0))) for v in (tokens, grad_out)]
    wq = jnp.transpose(qkv_weight, (1, 2, 0)).reshape(3 * LOC, D)
    row = lambda v: v.reshape(1, -1)
    bq = jnp.transpose(select(qkv_up), (0, 1, 2)).reshape(RANK, 3 * LOC)
    pad_rows = lambda v, n: jnp.pad(v, ((0, n - v.shape[0]), (0, 0)))
    bq = pad_rows(jnp.concatenate([bq, row(qkv_bias)]), EXT)
    b1 = pad_rows(jnp.concatenate([select(lin1_up), row(lin1_bias)]), EXT)
    low = jnp.concatenate(
        [select(lin2_down).T, jnp.pad(select(proj_down).T, ((0, 0), (0, HID - LOC)))]
    )
    pack = jnp.concatenate([bq, jnp.zeros((EXT, 1024 - 3 * LOC), BF), b1, low], axis=1)
    vecs = jnp.stack([norm1_gain, norm1_shift, norm2_gain, norm2_shift, proj_bias, lin2_bias])
    vecs = jnp.pad(vecs.astype(F32), ((0, 2), (0, 0)))
    adps = jnp.stack([select(qkv_down).T, select(lin1_down).T, select(proj_up), select(lin2_up)])
    adps = jnp.pad(adps, ((0, 0), (0, EXT - RANK), (0, 0)))
    rel, hot, back, shift, key = tables(rel_pos_h, rel_pos_w)
    out, grad, split_1, whole_1, split_2, whole_2 = call_kernel(
        images,
        (*both, wq, proj_weight, lin1_weight, lin2_weight, pack,
         vecs, adps, shift, rel, hot, back, key),
    )

    split_1 = split_1.reshape(images, 3 * RANK, D)
    split_2 = split_2.reshape(images, 2 * RANK, D)
    whole_1, whole_2 = (
        v.reshape(2, 2, images, RANK, D // 2).transpose(0, 2, 3, 1, 4).reshape(2, images, RANK, D)
        for v in (whole_1, whole_2)
    )

    slots = jnp.arange(ADAPTERS)[:, None] == adapter_index[None]

    def to_slots(v):
        v = v.astype(F32)
        total = 0.0
        for i in range(images):
            hit = slots[:, i].reshape((-1,) + (1,) * (v.ndim - 1))
            total = total + jnp.where(hit, v[i][None], 0.0)
        return total

    swap = lambda v: jnp.swapaxes(v, 1, 2)
    up_q = split_2[:, :RANK, : 3 * LOC].reshape(images, RANK, 3, LOC)
    return (
        out[:row_count],
        grad[:row_count],
        swap(to_slots(whole_2[0])),
        to_slots(up_q),
        swap(to_slots(split_2[:, :RANK, 3 * LOC :])),
        to_slots(whole_2[1]),
        swap(to_slots(whole_1[0])),
        to_slots(split_1[:, :RANK]),
        swap(to_slots(split_1[:, RANK : 2 * RANK])),
        to_slots(whole_1[1]),
    )


def solution(mesh):
    placed = (
        P(("dp", "tensor"), None),
        P(("dp", "tensor"), None),
        P(),
        P(),
        P(),
        P(None, None, "tensor"),
        P(None, "tensor"),
        P(),
        P(),
        P("tensor", None),
        P(),
        P(),
        P(),
        P(None, "tensor"),
        P("tensor"),
        P("tensor", None),
        P(),
        P(),
        P(None, None, None, "tensor"),
        P(None, "tensor", None),
        P(),
        P(),
        P(None, None, "tensor"),
        P(None, "tensor", None),
        P(),
    )
    return jax.shard_map(
        on_device,
        mesh=mesh,
        in_specs=placed,
        out_specs=(
            P(("dp", "tensor"), None),
            P(("dp", "tensor"), None),
            P(),
            P(None, None, None, "tensor"),
            P(None, "tensor", None),
            P(),
            P(),
            P(None, None, "tensor"),
            P(None, "tensor", None),
            P(),
        ),
        check_vma=False,
    )
```

```python
import functools

import jax
import jax.numpy as jnp
import numpy as np
from jax import lax
from jax.experimental import pallas as pl
from jax.experimental.pallas import tpu as pltpu
from jax.sharding import PartitionSpec as P

HEAD_DIM = 80
WIN = 14
SIDE = 64
RANK = 16
ADAPTERS = 8
WIN_DEV = 7
GROUP = 4
GRID = 5
TOK = WIN * WIN
PAD = 208
NW = 2
R = NW * PAD
D = 1280
LOC = 320
LP = 384
HID = 1280
HC = 256
PACK_Q = (3 * 32, 320)
PACK_M = (32, 2560)
ROWS = 352
EXT = 32
HALF = 0.5
EPS = 1e-6
SCALE = HEAD_DIM**-0.5
MESH = pl.DeviceIdType.MESH
BF = jnp.bfloat16
F32 = jnp.float32
SPAN = ((0, 128), (0, 256), (128, 128), (128, 256))
ERF_P = 0.3275911
ERF_A = (0.254829592, -0.284496736, 1.421413741, -1.453152027, 1.061405429)

CHUNKS = (
    [("q", 192 * i, 192) for i in range(5)]
    + [("p", 0, 320)]
    + [("1", 320 * i, 320) for i in range(4)]
    + [("2", 256 * i, 256) for i in range(5)]
)
NCH = len(CHUNKS)
OF_Q, OF_P, OF_1, OF_2 = range(5), [5], range(6, 10), range(10, 15)
THIRDS = {
    80: ((2, 2, 1), (2, 1, 2), (1, 2, 2)),
    64: ((2, 1, 1), (1, 2, 1), (1, 1, 2)),
    48: ((1, 1, 1),) * 3,
}


def nn(a, b):
    return jnp.dot(a, b, preferred_element_type=F32)


def nt(a, b):
    return lax.dot_general(a, b, (((1,), (1,)), ((), ())), preferred_element_type=F32)


def tn(a, b):
    return lax.dot_general(a, b, (((0,), (0,)), ((), ())), preferred_element_type=F32)


def mult(v, m=16):
    return v if isinstance(v, int) else pl.multiple_of(v, m)


class Wire:
    def __init__(self, own, land, packs, sems, images):
        self.own, self.land, self.sems = own, land, sems
        self.packs = packs
        dp, t = lax.axis_index("dp"), lax.axis_index("tensor")
        self.q = lax.rem(dp, 4)
        self.t = t
        self.image = dp // GROUP
        self.levels = images.bit_length() - 1
        self.dev = {"x": (dp ^ 1, t), "z": (dp ^ 2, t), "d": (dp ^ 3, t)}
        self.dev |= {"c": (dp, t ^ 1), "y": (dp, t ^ 2), "yc": (dp, t ^ 3)}
        self.dev |= {f"i{b}": (dp ^ (GROUP << b), t) for b in range(self.levels)}
        self.near = {"next": (dp, lax.rem(t + 1, 4)), "prev": (dp, lax.rem(t + 3, 4))}
        self.count = {}

    def barrier(self):
        bar = pltpu.get_barrier_semaphore()
        for d in self.dev.values():
            pl.semaphore_signal(bar, inc=1, device_id=d, device_id_type=MESH)
        pl.semaphore_wait(bar, len(self.dev))

    def copy(self, key, src, dst, dev):
        n = self.count.setdefault(key, len(self.count))
        return pltpu.make_async_remote_copy(
            src_ref=src,
            dst_ref=dst,
            send_sem=self.sems.at[0, n],
            recv_sem=self.sems.at[1, n],
            device_id=(self.dev | self.near)[dev],
            device_id_type=MESH,
        )

    def ready(self, sem):
        for d in self.dev.values():
            pl.semaphore_signal(sem, inc=1, device_id=d, device_id_type=MESH)

    def all_ready(self, sem):
        pl.semaphore_wait(sem, len(self.dev))

    def edge(self, key, src, dst, forward, do):
        for s in range(1, 4):
            n = 16 * -(-49 * s // 16)
            at, to = (s - 1, s) if forward else (s, s - 1)

            @pl.when(self.t == (at if do != "wait" else to))
            def _():
                cp = self.copy((key, s), src(n), dst(n), "next" if forward else "prev")
                getattr(cp, {"go": "start", "wait": "wait_recv", "end": "wait_send"}[do])()

    def pack(self, what, do):
        for i, (own, land) in enumerate(self.packs):
            cp = {
                "c": lambda: self.copy(("pc", i), own, land.at[1], "c"),
                "y": lambda: self.copy(("py", i), own, land.at[2], "y"),
                "f": lambda: self.copy(("pf", i), land.at[2], land.at[3], "c"),
            }[what]()
            getattr(cp, {"go": "start", "wait": "wait_recv", "end": "wait_send"}[do])()

    def parts(self, c):
        name, first, rows = CHUNKS[c]
        quarter = rows // 4
        a, b, d = (16 * v for v in THIRDS[quarter][c % 3])
        q = self.q

        def at(quart, off, n):
            return pl.ds(mult(first + quart * quarter + off), n)

        return {
            "all": pl.ds(first, rows),
            "y1": at(q, 0, quarter),
            "y2": at(q ^ 3, 0, a),
            "x1": at(q ^ 1, 0, quarter),
            "z1": at(q ^ 2, 0, quarter),
            "xs": at(q, 0, quarter),
            "x2": at(q ^ 2, a, b),
            "z2": at(q ^ 1, a + b, d),
        }

    def piece(self, c, what):
        name, first, rows = CHUNKS[c]
        own, land = self.own[name], self.land[name]
        p = self.parts(c)
        if what == "s":
            s = pl.ds(first, rows)
            return self.copy((c, what), own.at[s], land.at[1, s], "c")
        if what in ("y1", "y2"):
            return self.copy((c, what), own.at[p[what]], land.at[2, p[what]], "y")
        if what in ("x1", "z1"):
            return self.copy((c, what), land.at[2, p["xs"]], land.at[2, p["xs"]], what[0])
        if what in ("x2", "z2"):
            return self.copy((c, what), land.at[2, p[what]], land.at[2, p[what]], what[0])
        r = p["all"]
        return self.copy((c, what), land.at[2, r], land.at[3, r], "c")

    def begin(self, after_heads):
        self.pack("c", "go")
        for c in range(NCH):
            if c == OF_P[0]:
                self.pack("y", "go")
                after_heads()
            self.piece(c, "y1").start()
            self.piece(c, "y2").start()
            self.piece(c, "s").start()

    def step(self, what):
        kind, n = what[0], int(what[1:])
        if kind == "P":
            self.pack("y", "wait")
            self.pack("f", "go")
            return
        come, go = {
            "A": (("y1", "y2"), ("x1", "z1")),
            "B": (("x1", "z1"), ("x2", "z2")),
            "C": (("x2", "z2"), ("f",)),
        }[kind]
        for w in come:
            self.piece(n, w).wait_recv()
        for w in go:
            self.piece(n, w).start()

    def have(self, k, chunks):
        for c in chunks:
            if k == 1:
                self.piece(c, "s").wait_recv()
            if k == 3:
                self.piece(c, "f").wait_recv()

    def finish(self):
        for w in "cyf":
            self.pack(w, "end")
        for c in range(NCH):
            for w in ("s", "y1", "y2", "x1", "z1", "x2", "z2", "f"):
                self.piece(c, w).wait_send()


class Sum:
    def __init__(self, wire, name, send, buf, images):
        self.wire, self.name, self.send, self.buf, self.images = wire, name, send, buf, images
        self.n = send.shape[1]

    def go(self, key, src, dst, dev, do):
        cp = self.wire.copy((self.name, key), src, dst, dev)
        getattr(cp, {"go": "start", "wait": "wait_recv", "end": "wait_send"}[do])()

    def first(self, k, rows, do):
        dev = {1: "c", 2: "y", 3: "yc"}[k]
        dst = self.buf.at[1, pl.ds((k - 1) * self.n + rows.start, rows.size)]
        self.go(("a", k, rows.start), self.send.at[k, rows], dst, dev, do)

    def second(self, do):
        n = self.n
        for j, dev in enumerate("xzd"):
            src, dst = self.buf.at[1, pl.ds(3 * n, n)], self.buf.at[1, pl.ds((4 + j) * n, n)]
            self.go(("b", j), src, dst, dev, do)

    def third(self, level, do):
        n, size = self.n, 1 << level
        start = (self.wire.image >> level) << level
        if do == "wait":
            start = start ^ size
        rows = pl.ds(mult(start * n), size * n)
        self.go(("i", level), self.buf.at[2, rows], self.buf.at[2, rows], f"i{level}", do)

    def fourth(self, do):
        m, t = self.images * RANK, self.wire.t
        for k in (1, 2, 3):
            owner = t if do != "wait" else t ^ k
            part = self.buf.at[3, pl.ds(mult(owner * m), m), pl.ds(0, D // 2)]
            self.go(("r", k), part, part, {1: "c", 2: "y", 3: "yc"}[k], do)

    def finish(self, split):
        for k in (1, 2, 3):
            for rows in split:
                self.first(k, rows, "end")
        self.second("end")
        for b in range(self.wire.levels):
            self.third(b, "end")
        self.fourth("end")

    def part(self, slab, i):
        return self.buf[slab, i * self.n : (i + 1) * self.n, :].astype(F32)

    def add_first(self, split):
        for k in (1, 2, 3):
            for rows in split:
                self.first(k, rows, "wait")
        total = self.send[0].astype(F32) + self.part(1, 0) + self.part(1, 1) + self.part(1, 2)
        self.buf[1, 3 * self.n : 4 * self.n, :] = total.astype(BF)
        self.second("go")

    def add_second(self):
        self.second("wait")
        total = self.part(1, 3) + self.part(1, 4) + self.part(1, 5) + self.part(1, 6)
        self.buf[2, pl.ds(mult(self.wire.image * self.n), self.n), :] = total.astype(BF)
        if self.wire.levels:
            self.third(0, "go")

    def add_third(self):
        for b in range(self.wire.levels):
            self.third(b, "wait")
            if b + 1 < self.wire.levels:
                self.third(b + 1, "go")
        n, m = self.n, self.images * RANK
        for i in range(self.images):
            own = pl.ds(mult(self.wire.t * m + i * RANK), RANK)
            self.buf[3, own, 0 : D // 2] = self.buf[
                2, (i + 1) * n - RANK : (i + 1) * n, 0 : D // 2
            ]
        self.fourth("go")

    def hand_out(self, split_out, whole_out, local):
        self.fourth("wait")
        n, m = self.n, self.images * RANK
        copies = [
            pltpu.make_async_copy(self.buf.at[2, 0 : self.images * n], split_out, local.at[0]),
        ]
        for s in range(4):
            row, col = s // 2 * m, s % 2 * (D // 2)
            src = self.buf.at[3, s * m : (s + 1) * m, 0 : D // 2]
            dst = whole_out.at[row : row + m, col : col + D // 2]
            copies.append(pltpu.make_async_copy(src, dst, local.at[1 + s]))
        for cp in copies:
            cp.start()
        return copies


def half_of(ref, wire, k):
    s = wire.t ^ k
    return ref[s >> 1, :, pl.ds(mult((s & 1) * (D // 2), 128), D // 2)]


def one_hot(target, count):
    lane = lax.broadcasted_iota(jnp.int32, (target.shape[0], count), 1)
    return jnp.where(lane == target, 1.0, 0.0).astype(BF)


def window_rows(t):
    r = lax.broadcasted_iota(jnp.int32, (R, 1), 0)
    w = jnp.where(r >= PAD, 1, 0)
    i = r - PAD * w
    p = 49 * t + TOK * w + i
    source = jnp.where(i < TOK, jnp.where(p < 343, p, p + (ROWS - 343)), -1)
    slot = lax.rem(lax.axis_index("dp"), GROUP) * WIN_DEV + NW * t + w
    high = (slot * 205) >> 10
    row = (i * 4682) >> 16
    ok = (i < TOK) & (NW * t + w < WIN_DEV) & (slot < GRID * GRID)
    ok = ok & (high * WIN + row < SIDE) & ((slot - GRID * high) * WIN + i - WIN * row < SIDE)
    return source, jnp.where(ok, 1.0, 0.0).astype(F32)


def home_rows(t, mine, fetched):
    r = lax.broadcasted_iota(jnp.int32, (ROWS, 1), 0)
    o = r - 49 * t
    here = jnp.where(o < 0, -1, jnp.where(o < TOK, o, o + PAD - TOK))
    there = jnp.where(o < 0, r + 4 - t, -1)
    here, there = one_hot(here, R), one_hot(there, 160)
    return lambda cols: (nn(here, mine[:, cols]) + nn(there, fetched[:, cols])).astype(BF)


def shifted(values, shift, right):
    for bit in (1, 2, 4, 8):
        moved = pltpu.roll(values, bit if right else 128 - bit, 1)
        values = jnp.where((shift & bit) > 0, moved, values)
    return values


def join_heads(parts):
    lane = lax.broadcasted_iota(jnp.int32, (PAD, 128), 1)
    t0 = jnp.where(lane < 80, parts[0], parts[1][:, :128])
    t1 = jnp.where(
        lane < 32, parts[1][:, 128:], jnp.where(lane < 112, parts[2], parts[3][:, :128])
    )
    return (t0, t1, parts[3][:, 128:])


def head_mask(h, dtype=BF):
    base, width = SPAN[h]
    low = HEAD_DIM * h - base
    lane = lax.broadcasted_iota(jnp.int32, (1, width), 1)
    return jnp.where((lane >= low) & (lane < low + HEAD_DIM), 1.0, 0.0).astype(dtype)


def stats(v):
    mean = jnp.mean(v, axis=-1, keepdims=True)
    cen = v - mean
    inv = lax.rsqrt(jnp.mean(cen * cen, axis=-1, keepdims=True) + EPS)
    return cen * inv, inv


def norm_back(grad, xhat, inv, gain):
    e = grad * gain
    return inv * (
        e
        - jnp.mean(e, axis=-1, keepdims=True)
        - xhat * jnp.mean(e * xhat, axis=-1, keepdims=True)
    )


def row_loop(body, rows=PAD):
    def one(i, _):
        body(pl.ds(mult(i * rows), rows))
        return 0

    lax.fori_loop(0, R // rows, one, 0)


def ticks(wire, place, index):
    for at, steps in place.items():

        @pl.when(index == at)
        def _():
            for what in steps:
                wire.step(what)


AT_WINDOW = {
    1: ("A0",), 2: ("A1", "B0"), 3: ("A2", "B1", "C0"), 5: ("A5",), 6: ("B5", "A6"), 7: ("C5",),
}
AT_SHARD = {2: ("A3", "B2", "C1", "A4", "B3", "C2", "B4", "C3", "C4")}
AT_HIDDEN = {
    0: ("A7", "B6", "A8"), 1: ("C6", "B7"), 3: ("A9", "B8", "C7"), 5: ("A10", "B9", "C8"),
    7: ("A11", "B10", "C9"), 10: ("A12", "B11", "C10"), 12: ("A13", "B12", "C11"),
    14: ("B13", "C12", "A14"), 16: ("B14", "C13"), 17: ("C14",),
}


def kernel(
    images,
    x_hbm, g_hbm, wq_hbm, wp_hbm, w1_hbm, w2_hbm, pq_hbm, pm_hbm,
    vec_ref, adp_ref, shift_ref, row_ref, col_ref, hot_ref, back_ref, key_ref,
    out_hbm, grad_hbm, split_1, whole_1, split_2, whole_2,
    x_s, g_s, wq, wp, w1, w2, pack_q, pack_m, rel_ref, xn_s, q_s, k_s, v_s, att_s, p_s, mid_s, acc_a, acc_b,
    datt_s, act_s, dpre_s, d1t_s, up2t_s, d1_s, up2_s, d2_s, up1_s, dqt_s, valid_ref, sum_1, sum_2,
    rep_s, sems, local, done,
):
    own = {"q": wq_hbm, "p": wp_hbm, "1": w1_hbm, "2": w2_hbm}
    land = {"q": wq, "p": wp, "1": w1, "2": w2}
    wire = Wire(own, land, [(pq_hbm, pack_q), (pm_hbm, pack_m)], sems, images)
    total_1 = Sum(wire, "s1", sum_1, w1, images)
    total_2 = Sum(wire, "s2", sum_2, w2, images)
    t = wire.t
    blank = jnp.zeros((512 - ROWS, D), BF)
    w1[0, ROWS:512, :] = blank
    w2[0, ROWS:512, :] = blank
    wire.barrier()

    def edge_in(key, src, dst):
        to = lambda n: dst.at[0, ROWS : ROWS + n]
        wire.edge(key, lambda n: src.at[0:n], to, False, "go")

    edge_in("ex", x_hbm, w1)
    wire.begin(lambda: edge_in("eg", g_hbm, w2))
    pairs = [
        (x_hbm, w1.at[0, 0:ROWS]), (pq_hbm, pack_q.at[0]), (wq_hbm, wq.at[0]),
        (wp_hbm, wp.at[0]), (g_hbm, w2.at[0, 0:ROWS]), (w1_hbm, w1.at[0]), (w2_hbm, w2.at[0]),
        (pm_hbm, pack_m.at[0]),
    ]
    loads = [pltpu.make_async_copy(a, b, local.at[i]) for i, (a, b) in enumerate(pairs)]
    for cp in loads[:5] + loads[7:]:
        cp.start()
    lane_pad = jnp.zeros((4, R, LP - 256), BF)
    for ref in (q_s, k_s, v_s, att_s):
        ref[:, :, 256:LP] = lane_pad
    datt_s[:, 256:LP] = lane_pad[0]

    vecs = vec_ref[...].astype(F32)
    gain1, shift1, gain2, shift2, bias_p, bias_2 = (vecs[i : i + 1, :] for i in range(6))

    def factor(i):
        return jnp.concatenate([adp_ref[i], jnp.zeros((EXT - RANK, D), BF)], axis=0)

    lane_e = lax.broadcasted_iota(jnp.int32, (R, EXT), 1)
    line = lax.broadcasted_iota(jnp.int32, (128, 2 * WIN - 1), 0)
    lane = lax.broadcasted_iota(jnp.int32, (128, 2 * WIN - 1), 1)
    rel = nn(jnp.where(line + lane == 2 * WIN - 2, 1.0, 0.0).astype(BF), row_ref[...])
    rel += nn(jnp.where(line + lane == 64 + 2 * WIN - 2, 1.0, 0.0).astype(BF), col_ref[...])
    rel = rel.astype(BF)
    line = lax.broadcasted_iota(jnp.int32, (HEAD_DIM, LP), 0)
    lane = lax.broadcasted_iota(jnp.int32, (HEAD_DIM, LP), 1)
    for h in range(4):
        put = jnp.where(lane == line + HEAD_DIM * h, 1.0, 0.0).astype(BF)
        rel_ref[h] = nn(rel, put).astype(BF)
    source, valid = window_rows(t)
    valid_ref[...] = valid
    pick_rows = one_hot(source, 512)

    loads[0].wait()
    wire.edge("ex", lambda n: x_hbm.at[0:n], lambda n: w1.at[0, ROWS : ROWS + n], False, "wait")
    for n in range(5):
        cols = slice(256 * n, 256 * n + 256)
        x_s[:, cols] = nn(pick_rows, w1[0, 0:512, cols]).astype(BF)
    loads[5].start()

    def norm_one(rows):
        xhat, _ = stats(x_s[rows, :].astype(F32))
        xn_s[rows, :] = (valid_ref[rows, :] * (xhat * gain1 + shift1)).astype(BF)

    row_loop(norm_one)
    loads[1].wait()
    down_q = HALF * nt(xn_s[...], factor(0))
    dq_ext = jnp.where(lane_e == RANK, 1.0, down_q).astype(BF)
    d1_s[...] = dq_ext
    dqt_s[...] = down_q.T.astype(BF)
    loads[2].wait()

    def heads_forward(k, _):
        @pl.when(k == 1)
        def _():
            wire.pack("c", "wait")
            wire.have(1, OF_Q)

        ticks(wire, AT_SHARD, k)

        @pl.when(k == 3)
        def _():
            wire.have(3, OF_Q)

        x_q = nt(xn_s[...], wq[k])

        @pl.when(k == 2)
        def _():
            wire.step("P0")

        @pl.when(k == 3)
        def _():
            wire.pack("f", "wait")

        for j, ref in enumerate((q_s, k_s, v_s)):
            low_rank = nn(d1_s[...], pack_q[k, EXT * j : EXT * j + EXT, 0:LOC])
            ref[k, :, 0:LOC] = (x_q[:, LOC * j : LOC * j + LOC] + low_rank).astype(BF)

        def window(w, _):
            ticks(wire, AT_WINDOW, k * NW + w)
            rows = pl.ds(mult(w * PAD), PAD)
            shift = shift_ref[...]
            lane = lax.broadcasted_iota(jnp.int32, (PAD, 128), 1)
            fine = (lane & 32) > 0
            outs = []
            for h in range(4):
                b, n = SPAN[h]
                lanes = slice(b, b + n)
                qm = q_s[k, rows, lanes] * head_mask(h)
                scores = nt(qm, k_s[k, rows, lanes]) * SCALE
                u = shifted(nt(qm, rel_ref[h, :, lanes]), shift, False)
                rest = u - u.astype(BF).astype(F32)
                u = jnp.where(fine, pltpu.roll(rest, 32, 1), u).astype(BF)
                scores = scores + nn(u, hot_ref[...]) + key_ref[...]
                top = jnp.max(scores, axis=1, keepdims=True)
                e = jnp.exp(scores - top)
                p = (e * (1.0 / jnp.sum(e, axis=1, keepdims=True))).astype(BF)
                p_s[(k * NW + w) * 4 + h] = p
                outs.append(nn(p, v_s[k, rows, lanes]))
            for i, part in enumerate(join_heads(outs)):
                att_s[k, rows, 128 * i : 128 * i + 128] = part.astype(BF)
            return 0

        lax.fori_loop(0, NW, window, 0)
        return 0

    lax.fori_loop(0, 4, heads_forward, 0)

    loads[3].wait()
    wire.have(1, OF_P)
    wire.have(3, OF_P)
    loads[7].wait()
    down_p = jnp.zeros((R, RANK), F32)
    for k in range(4):
        down_p += nt(att_s[k, :, 0:LOC], pack_m[k, 16:32, HID : HID + LOC])
    down_p = HALF * down_p
    dp16 = down_p.astype(BF)
    dpt = down_p.T.astype(BF)
    for n in range(5):
        cols = slice(256 * n, 256 * n + 256)
        total = nn(dp16, adp_ref[2, :, cols]) + bias_p[:, cols]
        for k in range(4):
            total += nn(att_s[k, :, 0:LOC], wp[k, :, cols])
        acc_a[:, cols] = total

    def norm_two(rows):
        mid = x_s[rows, :].astype(F32) + valid_ref[rows, :] * acc_a[rows, :]
        mid_s[rows, :] = mid
        xhat, _ = stats(mid)
        xn_s[rows, :] = (xhat * gain2 + shift2).astype(BF)

    row_loop(norm_two)
    down_1 = HALF * nt(xn_s[...], factor(1))
    d1_s[...] = jnp.where(lane_e == RANK, 1.0, down_1).astype(BF)
    d1t_s[...] = down_1.T.astype(BF)
    loads[4].wait()
    wire.edge("eg", lambda n: g_hbm.at[0:n], lambda n: w2.at[0, ROWS : ROWS + n], False, "wait")
    pick_rows = one_hot(window_rows(t)[0], 512)
    for n in range(5):
        cols = slice(256 * n, 256 * n + 256)
        g_s[:, cols] = nn(pick_rows, w2[0, 0:512, cols]).astype(BF)
    loads[6].start()
    valid = valid_ref[...]
    up2 = HALF * valid * nt(g_s[...], factor(3))
    up2_s[...] = up2.astype(BF)
    up2t_s[...] = up2.T.astype(BF)
    acc_a[...] = jnp.zeros((R, D), F32)
    acc_b[...] = jnp.zeros((R, D), F32)
    d2_s[...] = jnp.zeros((R, EXT), F32)
    up1_s[...] = jnp.zeros((R, EXT), F32)
    loads[5].wait()
    loads[6].wait()

    def slice_of(i):
        k = jnp.where(i < 5, 0, jnp.where(i < 10, 1, 2 + lax.rem(i, 2)))
        c = jnp.where(i < 10, lax.rem(i, 5), i // 2 - 5)
        cols = pl.ds(mult(c * HC, HC), HC)
        return k, cols, pack_m[k, :, pl.ds(mult(HID + c * HC, HC), HC)]

    def hidden_values(i):
        k, cols, a2 = slice_of(i)
        pre = nn(xn_s[...], w1[k, :, cols]) + nn(d1_s[...], pack_m[k, :, cols])
        gauss = jnp.exp(-0.5 * pre * pre)
        t = 1.0 / (1.0 + (ERF_P * 0.5**0.5) * jnp.abs(pre))
        poly = ERF_A[4]
        for a in ERF_A[3::-1]:
            poly = poly * t + a
        tail = (HALF * poly) * t * gauss
        phi = jnp.where(pre >= 0, 1.0 - tail, tail)
        slope = phi + pre * gauss * 0.3989422804014327
        dact = valid_ref[...] * nt(g_s[...], w2[k, cols, :]) + nn(up2_s[...], a2)
        act_s[lax.rem(i, 2)] = (pre * phi).astype(BF)
        dpre_s[lax.rem(i, 2)] = (dact * slope).astype(BF)

    def hidden_sums(i):
        k, cols, a2 = slice_of(i)
        act, dpre = act_s[lax.rem(i, 2)], dpre_s[lax.rem(i, 2)]
        sum_1[k, RANK : 2 * RANK, cols] = nn(up2t_s[...], act)[:RANK].astype(BF)
        sum_1[k, 0:RANK, cols] = nn(d1t_s[...], dpre)[:RANK].astype(BF)
        d2_s[...] += nt(act, a2)
        up1_s[...] += nt(dpre, pack_m[k, :, cols])
        for n in range(5):
            out = slice(256 * n, 256 * n + 256)
            acc_a[:, out] += nn(act, w2[k, cols, out])
            acc_b[:, out] += nt(dpre, w1[k, out, cols])

    def hidden(i, _):
        @pl.when(i == 5)
        def _():
            wire.have(1, [*OF_1, *OF_2])

        ticks(wire, AT_HIDDEN, i)

        @pl.when(i == 11)
        def _():
            wire.have(3, OF_1)

        for j in range(5):

            @pl.when(i == 11 + 2 * j)
            def _():
                wire.have(3, [OF_2[j]])

        hidden_sums(i - 1)
        hidden_values(i)
        return 0

    for what in AT_HIDDEN[0]:
        wire.step(what)
    hidden_values(0)
    lax.fori_loop(1, 20, hidden, 0)
    hidden_sums(19)

    wire.finish()
    wire.edge("ex", lambda n: x_hbm.at[0:n], lambda n: w1.at[0, ROWS : ROWS + n], False, "end")
    wire.edge("eg", lambda n: g_hbm.at[0:n], lambda n: w2.at[0, ROWS : ROWS + n], False, "end")
    wire.ready(done)
    d2 = HALF * d2_s[...]
    d2b = d2[:, :RANK].astype(BF)
    up1 = HALF * up1_s[...]
    up1b = up1[:, :RANK].astype(BF)
    rep_s[1] = nn((d2 * valid_ref[...]).T.astype(BF), g_s[...])[:RANK].astype(BF)
    rep_s[0] = nn(up1.T.astype(BF), xn_s[...])[:RANK].astype(BF)
    for k in range(4):
        sum_1[k, 2 * RANK :, 0 : D // 2] = half_of(rep_s, wire, k)
        sum_1[k, 2 * RANK :, D // 2 :] = jnp.zeros((RANK, D // 2), BF)
    wire.all_ready(done)
    all_1 = pl.ds(0, 3 * RANK)
    for k in (1, 2, 3):
        total_1.first(k, all_1, "go")
    for n in range(5):
        cols = slice(256 * n, 256 * n + 256)
        acc_a[:, cols] += nn(d2b, adp_ref[3, :, cols])
        acc_b[:, cols] += nn(up1b, adp_ref[1, :, cols])

    def back_two(rows):
        mid = mid_s[rows, :]
        ok = valid_ref[rows, :]
        x_out = mid + ok * (acc_a[rows, :] + bias_2)
        xhat, inv = stats(mid)
        dmid = g_s[rows, :].astype(F32) + norm_back(acc_b[rows, :], xhat, inv, gain2)
        mid_s[rows, :] = dmid
        g_s[rows, :] = (ok * dmid).astype(BF)
        xn_s[rows, :] = x_out.astype(BF)

    row_loop(back_two)

    def swap_edge(key, src, dst, do):
        to = lambda n: dst.at[0, 512 : 512 + n]
        wire.edge(key, lambda n: src.at[R - n : R], to, True, do)

    swap_edge("eo", xn_s, w1, "go")
    upp = HALF * nt(g_s[...], factor(2))
    upp16 = upp[:, :RANK].astype(BF)
    uppt = upp.T.astype(BF)
    rep_s[1] = nn(dpt, g_s[...]).astype(BF)
    d2_s[...] = jnp.zeros((R, EXT), F32)
    up2_s[:, 0:RANK] = upp16
    up2t_s[...] = uppt

    put_out = pltpu.make_async_copy(w1.at[0, 0:ROWS], out_hbm, local.at[8])

    def heads_backward(step, _):
        k = lax.rem(step + 1, 4)

        @pl.when(step == 1)
        def _():
            total_1.add_first([all_1])
            swap_edge("eo", xn_s, w1, "wait")
            home = home_rows(t, xn_s, w1.at[0, 512:672])
            for n in range(5):
                cols = slice(256 * n, 256 * n + 256)
                w1[0, 0:ROWS, cols] = home(cols)
            put_out.start()

        @pl.when(step == 2)
        def _():
            total_1.add_second()
            put_out.wait()
            swap_edge("eo", xn_s, w1, "end")
            row_loop(norm_one)

        @pl.when(step == 3)
        def _():
            total_1.add_third()

        datt = nt(g_s[...], wp[k]) + nn(up2_s[:, 0:RANK], pack_m[k, 16:32, HID : HID + LOC])
        datt_s[:, 0:LOC] = datt.astype(BF)
        sum_2[k, 0:RANK, 3 * LOC :] = nn(up2t_s[...], att_s[k, :, 0:LOC])[:RANK].astype(BF)

        def window(w, _):
            rows = pl.ds(mult(w * PAD), PAD)
            shift = shift_ref[...]
            dqs, dks, dvs = [], [], []
            for h in range(4):
                b, n = SPAN[h]
                lanes = slice(b, b + n)
                p = p_s[(k * NW + w) * 4 + h]
                da = datt_s[rows, lanes]
                dprob = nt(da * head_mask(h), v_s[k, rows, lanes])
                dvs.append(tn(p, da))
                pf = p.astype(F32)
                inner = jnp.sum(pf * dprob, axis=1, keepdims=True)
                ds = (pf * (dprob - inner)).astype(BF)
                du = shifted(nn(ds, back_ref[...]), shift, True).astype(BF)
                dqs.append(nn(ds, k_s[k, rows, lanes]) * SCALE + nn(du, rel_ref[h, :, lanes]))
                dks.append(tn(ds, q_s[k, rows, lanes]) * SCALE)
            for ref, parts in ((q_s, dqs), (k_s, dks), (v_s, dvs)):
                for i, part in enumerate(join_heads(parts)):
                    ref[k, rows, 128 * i : 128 * i + 128] = part.astype(BF)
            return 0

        lax.fori_loop(0, NW, window, 0)
        for j, ref in enumerate((q_s, k_s, v_s)):
            d = ref[k, :, 0:LOC]
            b = pack_q[k, EXT * j : EXT * j + EXT, 0:LOC]
            d2_s[...] += nt(d, b)
            sum_2[k, 0:RANK, j * LOC : (j + 1) * LOC] = nn(dqt_s[...], d)[:RANK].astype(BF)
        for kk in (1, 2, 3):

            @pl.when(k == kk)
            def _():
                total_2.first(kk, pl.ds(0, RANK), "go")

        return 0

    lax.fori_loop(0, 4, heads_backward, 0)
    puts = total_1.hand_out(split_1, whole_1, local.at[10:15])

    upq = HALF * d2_s[...]
    upqb = upq[:, :RANK].astype(BF)
    rep_s[0] = nn(upq.T.astype(BF), xn_s[...])[:RANK].astype(BF)
    for k in range(4):
        sum_2[k, RANK:, 0 : D // 2] = half_of(rep_s, wire, k)
        sum_2[k, RANK:, D // 2 :] = jnp.zeros((RANK, D // 2), BF)
    low, high = pl.ds(0, RANK), pl.ds(RANK, RANK)
    for k in (1, 2, 3):
        total_2.first(k, high, "go")

    for n in range(5):
        cols = slice(256 * n, 256 * n + 256)
        total = nn(upqb, adp_ref[0, :, cols])
        for k in range(4):
            for j, ref in enumerate((q_s, k_s, v_s)):
                total += nn(ref[k, :, 0:LOC], wq[k, j * LOC : (j + 1) * LOC, cols])
        acc_a[:, cols] = total
        if n == 1:
            total_2.add_first([low, high])
        if n == 3:
            total_2.add_second()

    def back_one(rows):
        ok = valid_ref[rows, :]
        xhat, inv = stats(x_s[rows, :].astype(F32))
        back = norm_back(ok * acc_a[rows, :], xhat, inv, gain1)
        g_s[rows, :] = (mid_s[rows, :] + back).astype(BF)

    row_loop(back_one)
    swap_edge("ef", g_s, w2, "go")
    total_2.add_third()
    swap_edge("ef", g_s, w2, "wait")
    home = home_rows(t, g_s, w2.at[0, 512:672])
    for n in range(5):
        cols = slice(256 * n, 256 * n + 256)
        w2[0, 0:ROWS, cols] = home(cols)
    put_grad = pltpu.make_async_copy(w2.at[0, 0:ROWS], grad_hbm, local.at[9])
    put_grad.start()
    puts += total_2.hand_out(split_2, whole_2, local.at[15:20])
    for cp in puts:
        cp.wait()
    put_grad.wait()
    swap_edge("ef", g_s, w2, "end")
    total_1.finish([all_1])
    total_2.finish([low, high])


def tables():
    tok = np.arange(PAD)
    inside = tok < TOK
    row, col = tok // WIN, tok % WIN
    lane = np.arange(128)[:, None]
    hot = (
        (((lane == row) | (lane == 32 + row)) & inside)
        | (((lane == 64 + col) | (lane == 96 + col)) & inside)
    ).astype(np.float32)
    back = ((lane == row) | (lane == 64 + col)) & inside
    shift = np.where(np.arange(128)[None] < 64, 13 - row[:, None], 13 - col[:, None])
    shift = np.where(inside[:, None], shift, 0).astype(np.int32)
    key = np.where(inside, 0.0, -1e30).astype(np.float32)[None]
    return jnp.asarray(hot, BF), jnp.asarray(back.T, BF), jnp.asarray(shift), jnp.asarray(key)


def call_kernel(images, args):
    any_ = pl.BlockSpec(memory_space=pl.ANY)
    vmem = pl.BlockSpec(memory_space=pltpu.VMEM)
    sds = jax.ShapeDtypeStruct
    V = pltpu.VMEM
    return pl.pallas_call(
        functools.partial(kernel, images),
        out_shape=(
            sds((ROWS, D), BF),
            sds((ROWS, D), BF),
            sds((images * 3 * RANK, D), BF),
            sds((2 * images * RANK, D), BF),
            sds((images * 2 * RANK, D), BF),
            sds((2 * images * RANK, D), BF),
        ),
        in_specs=[any_] * 8 + [vmem] * 8,
        out_specs=(any_,) * 6,
        scratch_shapes=[
            V((R, D), BF),
            V((R, D), BF),
            V((4, 3 * LOC, D), BF),
            V((4, LOC, D), BF),
            V((4, D, HID), BF),
            V((4, HID, D), BF),
            V((4,) + PACK_Q, BF),
            V((4,) + PACK_M, BF),
            V((4, 128, LP), BF),
            V((R, D), BF),
            V((4, R, LP), BF),
            V((4, R, LP), BF),
            V((4, R, LP), BF),
            V((4, R, LP), BF),
            V((4 * NW * 4, PAD, PAD), BF),
            V((R, D), F32),
            V((R, D), F32),
            V((R, D), F32),
            V((R, LP), BF),
            V((2, R, HC), BF),
            V((2, R, HC), BF),
            V((EXT, R), BF),
            V((EXT, R), BF),
            V((R, EXT), BF),
            V((R, EXT), BF),
            V((R, EXT), F32),
            V((R, EXT), F32),
            V((EXT, R), BF),
            V((R, 1), F32),
            V((4, 3 * RANK, D), BF),
            V((4, 2 * RANK, D), BF),
            V((2, RANK, D), BF),
            pltpu.SemaphoreType.DMA((2, 8 * NCH + 63)),
            pltpu.SemaphoreType.DMA((20,)),
            pltpu.SemaphoreType.REGULAR,
        ],
        compiler_params=pltpu.CompilerParams(
            collective_id=0, has_side_effects=True, vmem_limit_bytes=67_000_000
        ),
        name="block",
    )(*args)


def on_device(
    tokens,
    grad_out,
    adapter_index,
    norm1_gain,
    norm1_shift,
    qkv_weight,
    qkv_bias,
    rel_pos_h,
    rel_pos_w,
    proj_weight,
    proj_bias,
    norm2_gain,
    norm2_shift,
    lin1_weight,
    lin1_bias,
    lin2_weight,
    lin2_bias,
    qkv_down,
    qkv_up,
    proj_down,
    proj_up,
    lin1_down,
    lin1_up,
    lin2_down,
    lin2_up,
):
    images = adapter_index.shape[0]
    row_count = tokens.shape[0]
    dp_place = lax.axis_index("dp")
    image = dp_place // GROUP
    pick = jnp.sum(jnp.where(jnp.arange(images) == image, adapter_index, 0))

    def select(table_all):
        return lax.dynamic_index_in_dim(table_all, pick, 0, keepdims=False)

    both = [jnp.pad(v, ((0, ROWS - v.shape[0]), (0, 0))) for v in (tokens, grad_out)]
    wq = jnp.transpose(qkv_weight, (1, 2, 0)).reshape(3 * LOC, D)
    rows = np.arange(EXT)[:, None]
    pad_rows = lambda v: jnp.pad(v, ((0, EXT - RANK), (0, 0)))
    up = select(jnp.transpose(qkv_up, (0, 2, 1, 3)))
    up = jnp.pad(up, ((0, 0), (0, EXT - RANK), (0, 0)))
    up = jnp.where(rows[None] == RANK, qkv_bias[:, None, :], up)
    pack_q = up.reshape(PACK_Q)
    b1 = jnp.where(rows == RANK, lin1_bias[None], pad_rows(select(lin1_up)))
    low = jnp.pad(select(proj_down).T, ((RANK, 0), (0, HID - LOC)))
    low = jnp.where(rows < RANK, pad_rows(select(lin2_down).T), low)
    pack_m = jnp.concatenate([b1, low], axis=1)
    vecs = jnp.zeros((8, D), BF)
    for i, v in enumerate(
        (norm1_gain, norm1_shift, norm2_gain, norm2_shift, proj_bias, lin2_bias)
    ):
        vecs = jnp.where(rows[:8] == i, v[None], vecs)
    adps = jnp.stack([select(qkv_down).T, select(lin1_down).T, select(proj_up), select(lin2_up)])
    hot, back, shift, key = tables()
    out, grad, split_1, whole_1, split_2, whole_2 = call_kernel(
        images,
        (*both, wq, proj_weight, lin1_weight, lin2_weight, pack_q, pack_m,
         vecs, adps, shift, rel_pos_h, rel_pos_w, hot, back, key),
    )

    split_1 = split_1.reshape(images, 3 * RANK, D)
    split_2 = split_2.reshape(images, 2 * RANK, D)
    whole_1, whole_2 = (v.reshape(2, images, RANK, D) for v in (whole_1, whole_2))

    slots = jnp.arange(ADAPTERS)[:, None] == adapter_index[None]

    def to_slots(v):
        v = v.astype(F32)
        total = 0.0
        for i in range(images):
            hit = slots[:, i].reshape((-1,) + (1,) * (v.ndim - 1))
            total = total + jnp.where(hit, v[i][None], 0.0)
        return total

    swap = lambda v: jnp.swapaxes(v, 1, 2)
    up_q = [split_2[:, :RANK, LOC * j : LOC * j + LOC] for j in range(3)]
    up_q = jnp.stack(up_q, axis=1)
    return (
        out[:row_count],
        grad[:row_count],
        swap(to_slots(whole_2[0])),
        swap(to_slots(up_q)),
        swap(to_slots(split_2[:, :RANK, 3 * LOC :])),
        to_slots(whole_2[1]),
        swap(to_slots(whole_1[0])),
        to_slots(split_1[:, :RANK]),
        swap(to_slots(split_1[:, RANK : 2 * RANK])),
        to_slots(whole_1[1]),
    )


def solution(mesh):
    placed = (
        P(("dp", "tensor"), None),
        P(("dp", "tensor"), None),
        P(),
        P(),
        P(),
        P(None, None, "tensor"),
        P(None, "tensor"),
        P(),
        P(),
        P("tensor", None),
        P(),
        P(),
        P(),
        P(None, "tensor"),
        P("tensor"),
        P("tensor", None),
        P(),
        P(),
        P(None, None, None, "tensor"),
        P(None, "tensor", None),
        P(),
        P(),
        P(None, None, "tensor"),
        P(None, "tensor", None),
        P(),
    )
    return jax.shard_map(
        on_device,
        mesh=mesh,
        in_specs=placed,
        out_specs=(
            P(("dp", "tensor"), None),
            P(("dp", "tensor"), None),
            P(),
            P(None, None, None, "tensor"),
            P(None, "tensor", None),
            P(),
            P(),
            P(None, None, "tensor"),
            P(None, "tensor", None),
            P(),
        ),
        check_vma=False,
    )
```

```python
import functools

import jax
import jax.numpy as jnp
import numpy as np
from jax import lax
from jax.experimental import pallas as pl
from jax.experimental.pallas import tpu as pltpu
from jax.sharding import PartitionSpec as P

HEAD_DIM = 80
WIN = 14
SIDE = 64
RANK = 16
ADAPTERS = 8
WIN_DEV = 7
GROUP = 4
GRID = 5
TOK = WIN * WIN
PAD = 208
NW = 2
R = NW * PAD
D = 1280
LOC = 320
LP = 384
HID = 1280
HC = 256
PACK_Q = (3 * 32, 320)
PACK_M = (32, 2560)
ROWS = 352
EXT = 32
HALF = 0.5
EPS = 1e-6
SCALE = HEAD_DIM**-0.5
MESH = pl.DeviceIdType.MESH
BF = jnp.bfloat16
F32 = jnp.float32
SPAN = ((0, 128), (0, 256), (128, 128), (128, 256))
ERF_P = 0.3275911
ERF_A = (0.254829592, -0.284496736, 1.421413741, -1.453152027, 1.061405429)

CHUNKS = (
    [("q", 192 * i, 192) for i in range(5)]
    + [("p", 0, 320)]
    + [("1", 320 * i, 320) for i in range(4)]
    + [("2", 256 * i, 256) for i in range(5)]
)
NCH = len(CHUNKS)
OF_Q, OF_P, OF_1, OF_2 = range(5), [5], range(6, 10), range(10, 15)
THIRDS = {
    80: ((2, 2, 1), (2, 1, 2), (1, 2, 2)),
    64: ((2, 1, 1), (1, 2, 1), (1, 1, 2)),
    48: ((1, 1, 1),) * 3,
}


def nn(a, b):
    return jnp.dot(a, b, preferred_element_type=F32)


def nt(a, b):
    return lax.dot_general(a, b, (((1,), (1,)), ((), ())), preferred_element_type=F32)


def tn(a, b):
    return lax.dot_general(a, b, (((0,), (0,)), ((), ())), preferred_element_type=F32)


def mult(v, m=16):
    return v if isinstance(v, int) else pl.multiple_of(v, m)


class Wire:
    def __init__(self, own, land, packs, sems, images):
        self.own, self.land, self.sems = own, land, sems
        self.packs = packs
        dp, t = lax.axis_index("dp"), lax.axis_index("tensor")
        self.q = lax.rem(dp, 4)
        self.t = t
        self.image = dp // GROUP
        self.levels = images.bit_length() - 1
        self.dev = {"x": (dp ^ 1, t), "z": (dp ^ 2, t), "d": (dp ^ 3, t)}
        self.dev |= {"c": (dp, t ^ 1), "y": (dp, t ^ 2), "yc": (dp, t ^ 3)}
        self.dev |= {f"i{b}": (dp ^ (GROUP << b), t) for b in range(self.levels)}
        self.near = {"next": (dp, lax.rem(t + 1, 4)), "prev": (dp, lax.rem(t + 3, 4))}
        self.count = {}

    def barrier(self):
        bar = pltpu.get_barrier_semaphore()
        for d in self.dev.values():
            pl.semaphore_signal(bar, inc=1, device_id=d, device_id_type=MESH)
        pl.semaphore_wait(bar, len(self.dev))

    def copy(self, key, src, dst, dev):
        n = self.count.setdefault(key, len(self.count))
        return pltpu.make_async_remote_copy(
            src_ref=src,
            dst_ref=dst,
            send_sem=self.sems.at[0, n],
            recv_sem=self.sems.at[1, n],
            device_id=(self.dev | self.near)[dev],
            device_id_type=MESH,
        )

    def ready(self, sem):
        for d in self.dev.values():
            pl.semaphore_signal(sem, inc=1, device_id=d, device_id_type=MESH)

    def all_ready(self, sem):
        pl.semaphore_wait(sem, len(self.dev))

    def edge(self, key, src, dst, forward, do):
        for s in range(1, 4):
            n = 16 * -(-49 * s // 16)
            at, to = (s - 1, s) if forward else (s, s - 1)

            @pl.when(self.t == (at if do != "wait" else to))
            def _():
                cp = self.copy((key, s), src(n), dst(n), "next" if forward else "prev")
                getattr(cp, {"go": "start", "wait": "wait_recv", "end": "wait_send"}[do])()

    def pack(self, what, do):
        for i, (own, land) in enumerate(self.packs):
            cp = {
                "c": lambda: self.copy(("pc", i), own, land.at[1], "c"),
                "y": lambda: self.copy(("py", i), own, land.at[2], "y"),
                "f": lambda: self.copy(("pf", i), land.at[2], land.at[3], "c"),
            }[what]()
            getattr(cp, {"go": "start", "wait": "wait_recv", "end": "wait_send"}[do])()

    def parts(self, c):
        name, first, rows = CHUNKS[c]
        quarter = rows // 4
        a, b, d = (16 * v for v in THIRDS[quarter][c % 3])
        q = self.q

        def at(quart, off, n):
            return pl.ds(mult(first + quart * quarter + off), n)

        return {
            "all": pl.ds(first, rows),
            "y1": at(q, 0, quarter),
            "y2": at(q ^ 3, 0, a),
            "x1": at(q ^ 1, 0, quarter),
            "z1": at(q ^ 2, 0, quarter),
            "xs": at(q, 0, quarter),
            "x2": at(q ^ 2, a, b),
            "z2": at(q ^ 1, a + b, d),
        }

    def piece(self, c, what):
        name, first, rows = CHUNKS[c]
        own, land = self.own[name], self.land[name]
        p = self.parts(c)
        if what == "s":
            s = pl.ds(first, rows)
            return self.copy((c, what), own.at[s], land.at[1, s], "c")
        if what in ("y1", "y2"):
            return self.copy((c, what), own.at[p[what]], land.at[2, p[what]], "y")
        if what in ("x1", "z1"):
            return self.copy((c, what), land.at[2, p["xs"]], land.at[2, p["xs"]], what[0])
        if what in ("x2", "z2"):
            return self.copy((c, what), land.at[2, p[what]], land.at[2, p[what]], what[0])
        r = p["all"]
        return self.copy((c, what), land.at[2, r], land.at[3, r], "c")

    def begin(self, after_heads):
        self.pack("c", "go")
        for c in range(NCH):
            if c == OF_P[0]:
                self.pack("y", "go")
                after_heads()
            self.piece(c, "y1").start()
            self.piece(c, "y2").start()
            self.piece(c, "s").start()

    def step(self, what):
        kind, n = what[0], int(what[1:])
        if kind == "P":
            self.pack("y", "wait")
            self.pack("f", "go")
            return
        come, go = {
            "A": (("y1", "y2"), ("x1", "z1")),
            "B": (("x1", "z1"), ("x2", "z2")),
            "C": (("x2", "z2"), ("f",)),
        }[kind]
        for w in come:
            self.piece(n, w).wait_recv()
        for w in go:
            self.piece(n, w).start()

    def have(self, k, chunks):
        for c in chunks:
            if k == 1:
                self.piece(c, "s").wait_recv()
            if k == 3:
                self.piece(c, "f").wait_recv()

    def finish(self):
        for w in "cyf":
            self.pack(w, "end")
        for c in range(NCH):
            for w in ("s", "y1", "y2", "x1", "z1", "x2", "z2", "f"):
                self.piece(c, w).wait_send()


class Sum:
    def __init__(self, wire, name, send, buf, images):
        self.wire, self.name, self.send, self.buf, self.images = wire, name, send, buf, images
        self.n = send.shape[1]

    def go(self, key, src, dst, dev, do):
        cp = self.wire.copy((self.name, key), src, dst, dev)
        getattr(cp, {"go": "start", "wait": "wait_recv", "end": "wait_send"}[do])()

    def first(self, k, rows, do):
        dev = {1: "c", 2: "y", 3: "yc"}[k]
        dst = self.buf.at[1, pl.ds((k - 1) * self.n + rows.start, rows.size)]
        self.go(("a", k, rows.start), self.send.at[k, rows], dst, dev, do)

    def second(self, do):
        n = self.n
        for j, dev in enumerate("xzd"):
            src, dst = self.buf.at[1, pl.ds(3 * n, n)], self.buf.at[1, pl.ds((4 + j) * n, n)]
            self.go(("b", j), src, dst, dev, do)

    def third(self, level, do):
        n, size = self.n, 1 << level
        start = (self.wire.image >> level) << level
        if do == "wait":
            start = start ^ size
        rows = pl.ds(mult(start * n), size * n)
        self.go(("i", level), self.buf.at[2, rows], self.buf.at[2, rows], f"i{level}", do)

    def fourth(self, do):
        m, t = self.images * RANK, self.wire.t
        for k in (1, 2, 3):
            owner = t if do != "wait" else t ^ k
            part = self.buf.at[3, pl.ds(mult(owner * m), m), pl.ds(0, D // 2)]
            self.go(("r", k), part, part, {1: "c", 2: "y", 3: "yc"}[k], do)

    def finish(self, split):
        for k in (1, 2, 3):
            for rows in split:
                self.first(k, rows, "end")
        self.second("end")
        for b in range(self.wire.levels):
            self.third(b, "end")
        self.fourth("end")

    def part(self, slab, i):
        return self.buf[slab, i * self.n : (i + 1) * self.n, :].astype(F32)

    def add_first(self, split):
        for k in (1, 2, 3):
            for rows in split:
                self.first(k, rows, "wait")
        total = self.send[0].astype(F32) + self.part(1, 0) + self.part(1, 1) + self.part(1, 2)
        self.buf[1, 3 * self.n : 4 * self.n, :] = total.astype(BF)
        self.second("go")

    def add_second(self):
        self.second("wait")
        total = self.part(1, 3) + self.part(1, 4) + self.part(1, 5) + self.part(1, 6)
        self.buf[2, pl.ds(mult(self.wire.image * self.n), self.n), :] = total.astype(BF)
        if self.wire.levels:
            self.third(0, "go")

    def add_third(self):
        for b in range(self.wire.levels):
            self.third(b, "wait")
            if b + 1 < self.wire.levels:
                self.third(b + 1, "go")
        n, m = self.n, self.images * RANK
        for i in range(self.images):
            own = pl.ds(mult(self.wire.t * m + i * RANK), RANK)
            self.buf[3, own, 0 : D // 2] = self.buf[
                2, (i + 1) * n - RANK : (i + 1) * n, 0 : D // 2
            ]
        self.fourth("go")

    def hand_out(self, split_out, whole_out, local):
        self.fourth("wait")
        n, m = self.n, self.images * RANK
        copies = [
            pltpu.make_async_copy(self.buf.at[2, 0 : self.images * n], split_out, local.at[0]),
        ]
        for s in range(4):
            row, col = s // 2 * m, s % 2 * (D // 2)
            src = self.buf.at[3, s * m : (s + 1) * m, 0 : D // 2]
            dst = whole_out.at[row : row + m, col : col + D // 2]
            copies.append(pltpu.make_async_copy(src, dst, local.at[1 + s]))
        for cp in copies:
            cp.start()
        return copies


def half_of(ref, wire, k):
    s = wire.t ^ k
    return ref[s >> 1, :, pl.ds(mult((s & 1) * (D // 2), 128), D // 2)]


def one_hot(target, count):
    lane = lax.broadcasted_iota(jnp.int32, (target.shape[0], count), 1)
    return jnp.where(lane == target, 1.0, 0.0).astype(BF)


def window_rows(t):
    r = lax.broadcasted_iota(jnp.int32, (R, 1), 0)
    w = jnp.where(r >= PAD, 1, 0)
    i = r - PAD * w
    p = 49 * t + TOK * w + i
    source = jnp.where(i < TOK, jnp.where(p < 343, p, p + (ROWS - 343)), -1)
    slot = lax.rem(lax.axis_index("dp"), GROUP) * WIN_DEV + NW * t + w
    high = (slot * 205) >> 10
    row = (i * 4682) >> 16
    ok = (i < TOK) & (NW * t + w < WIN_DEV) & (slot < GRID * GRID)
    ok = ok & (high * WIN + row < SIDE) & ((slot - GRID * high) * WIN + i - WIN * row < SIDE)
    return source, jnp.where(ok, 1.0, 0.0).astype(F32)


def home_rows(t, mine, fetched):
    r = lax.broadcasted_iota(jnp.int32, (ROWS, 1), 0)
    o = r - 49 * t
    here = jnp.where(o < 0, -1, jnp.where(o < TOK, o, o + PAD - TOK))
    there = jnp.where(o < 0, r + 4 - t, -1)
    here, there = one_hot(here, R), one_hot(there, 160)
    return lambda cols: (nn(here, mine[:, cols]) + nn(there, fetched[:, cols])).astype(BF)


def shifted(values, shift, right):
    for bit in (1, 2, 4, 8):
        moved = pltpu.roll(values, bit if right else 128 - bit, 1)
        values = jnp.where((shift & bit) > 0, moved, values)
    return values


def join_heads(parts):
    lane = lax.broadcasted_iota(jnp.int32, (PAD, 128), 1)
    t0 = jnp.where(lane < 80, parts[0], parts[1][:, :128])
    t1 = jnp.where(
        lane < 32, parts[1][:, 128:], jnp.where(lane < 112, parts[2], parts[3][:, :128])
    )
    return (t0, t1, parts[3][:, 128:])


def head_mask(h, dtype=BF):
    base, width = SPAN[h]
    low = HEAD_DIM * h - base
    lane = lax.broadcasted_iota(jnp.int32, (1, width), 1)
    return jnp.where((lane >= low) & (lane < low + HEAD_DIM), 1.0, 0.0).astype(dtype)


def stats(v):
    mean = jnp.mean(v, axis=-1, keepdims=True)
    cen = v - mean
    inv = lax.rsqrt(jnp.mean(cen * cen, axis=-1, keepdims=True) + EPS)
    return cen * inv, inv


def norm_back(grad, xhat, inv, gain):
    e = grad * gain
    return inv * (
        e
        - jnp.mean(e, axis=-1, keepdims=True)
        - xhat * jnp.mean(e * xhat, axis=-1, keepdims=True)
    )


def row_loop(body, rows=PAD):
    def one(i, _):
        body(pl.ds(mult(i * rows), rows))
        return 0

    lax.fori_loop(0, R // rows, one, 0)


def ticks(wire, place, index):
    for at, steps in place.items():

        @pl.when(index == at)
        def _():
            for what in steps:
                wire.step(what)


AT_WINDOW = {1: ('A0',), 2: ('A1', 'B0'), 3: ('A2', 'B1', 'C0'), 5: ('A5',), 6: ('B5', 'A6'), 7: ('C5',)}
AT_SHARD = {2: ('A3', 'B2', 'C1', 'A4', 'B3', 'C2', 'B4', 'C3', 'C4')}
AT_HIDDEN = {0: ('C6', 'B7', 'A8'), 2: ('A9', 'B8', 'C7'), 4: ('A10', 'B9', 'C8'), 6: ('A11', 'B10', 'C9'), 8: ('A12', 'B11', 'C10'), 10: ('A13', 'B12', 'C11'), 12: ('A14', 'B13', 'C12'), 14: ('B14', 'C13'), 16: ('C14',)}


def kernel(
    images,
    x_hbm, g_hbm, wq_hbm, wp_hbm, w1_hbm, w2_hbm, pq_hbm, pm_hbm,
    vec_ref, adp_ref, shift_ref, row_ref, col_ref, hot_ref, back_ref, key_ref,
    out_hbm, grad_hbm, split_1, whole_1, split_2, whole_2,
    x_s, g_s, wq, wp, w1, w2, pack_q, pack_m, rel_ref, xn_s, q_s, k_s, v_s, att_s, p_s, mid_s, acc_a, acc_b,
    datt_s, act_s, dpre_s, d1t_s, up2t_s, d1_s, up2_s, d2_s, up1_s, dqt_s, valid_ref, sum_1, sum_2,
    rep_s, sems, local, done,
):
    own = {"q": wq_hbm, "p": wp_hbm, "1": w1_hbm, "2": w2_hbm}
    land = {"q": wq, "p": wp, "1": w1, "2": w2}
    wire = Wire(own, land, [(pq_hbm, pack_q), (pm_hbm, pack_m)], sems, images)
    total_1 = Sum(wire, "s1", sum_1, w1, images)
    total_2 = Sum(wire, "s2", sum_2, w2, images)
    t = wire.t
    blank = jnp.zeros((512 - ROWS, D), BF)
    w1[0, ROWS:512, :] = blank
    w2[0, ROWS:512, :] = blank
    wire.barrier()

    def edge_in(key, src, dst):
        to = lambda n: dst.at[0, ROWS : ROWS + n]
        wire.edge(key, lambda n: src.at[0:n], to, False, "go")

    edge_in("ex", x_hbm, w1)
    wire.begin(lambda: edge_in("eg", g_hbm, w2))
    pairs = [
        (x_hbm, w1.at[0, 0:ROWS]), (pq_hbm, pack_q.at[0]), (wq_hbm, wq.at[0]),
        (wp_hbm, wp.at[0]), (g_hbm, w2.at[0, 0:ROWS]), (w1_hbm, w1.at[0]), (w2_hbm, w2.at[0]),
        (pm_hbm, pack_m.at[0]),
    ]
    loads = [pltpu.make_async_copy(a, b, local.at[i]) for i, (a, b) in enumerate(pairs)]
    for cp in loads[:5] + loads[7:]:
        cp.start()
    lane_pad = jnp.zeros((4, R, LP - 256), BF)
    for ref in (q_s, k_s, v_s, att_s):
        ref[:, :, 256:LP] = lane_pad
    datt_s[:, 256:LP] = lane_pad[0]

    vecs = vec_ref[...].astype(F32)
    gain1, shift1, gain2, shift2, bias_p, bias_2 = (vecs[i : i + 1, :] for i in range(6))

    def factor(i):
        return jnp.concatenate([adp_ref[i], jnp.zeros((EXT - RANK, D), BF)], axis=0)

    lane_e = lax.broadcasted_iota(jnp.int32, (R, EXT), 1)
    line = lax.broadcasted_iota(jnp.int32, (128, 2 * WIN - 1), 0)
    lane = lax.broadcasted_iota(jnp.int32, (128, 2 * WIN - 1), 1)
    rel = nn(jnp.where(line + lane == 2 * WIN - 2, 1.0, 0.0).astype(BF), row_ref[...])
    rel += nn(jnp.where(line + lane == 64 + 2 * WIN - 2, 1.0, 0.0).astype(BF), col_ref[...])
    rel = rel.astype(BF)
    line = lax.broadcasted_iota(jnp.int32, (HEAD_DIM, LP), 0)
    lane = lax.broadcasted_iota(jnp.int32, (HEAD_DIM, LP), 1)
    for h in range(4):
        put = jnp.where(lane == line + HEAD_DIM * h, 1.0, 0.0).astype(BF)
        rel_ref[h] = nn(rel, put).astype(BF)
    source, valid = window_rows(t)
    valid_ref[...] = valid
    pick_rows = one_hot(source, 512)

    loads[0].wait()
    wire.edge("ex", lambda n: x_hbm.at[0:n], lambda n: w1.at[0, ROWS : ROWS + n], False, "wait")
    for n in range(5):
        cols = slice(256 * n, 256 * n + 256)
        x_s[:, cols] = nn(pick_rows, w1[0, 0:512, cols]).astype(BF)
    loads[5].start()

    def norm_one(rows):
        xhat, _ = stats(x_s[rows, :].astype(F32))
        xn_s[rows, :] = (valid_ref[rows, :] * (xhat * gain1 + shift1)).astype(BF)

    row_loop(norm_one)
    loads[1].wait()
    down_q = HALF * nt(xn_s[...], factor(0))
    dq_ext = jnp.where(lane_e == RANK, 1.0, down_q).astype(BF)
    d1_s[...] = dq_ext
    dqt_s[...] = down_q.T.astype(BF)
    loads[2].wait()

    def heads_forward(k, _):
        @pl.when(k == 1)
        def _():
            wire.pack("c", "wait")
            wire.have(1, OF_Q)

        ticks(wire, AT_SHARD, k)

        @pl.when(k == 3)
        def _():
            wire.have(3, OF_Q)

        x_q = nt(xn_s[...], wq[k])

        @pl.when(k == 2)
        def _():
            wire.step("P0")

        @pl.when(k == 3)
        def _():
            wire.pack("f", "wait")

        for j, ref in enumerate((q_s, k_s, v_s)):
            low_rank = nn(d1_s[...], pack_q[k, EXT * j : EXT * j + EXT, 0:LOC])
            ref[k, :, 0:LOC] = (x_q[:, LOC * j : LOC * j + LOC] + low_rank).astype(BF)

        def window(w, _):
            ticks(wire, AT_WINDOW, k * NW + w)
            rows = pl.ds(mult(w * PAD), PAD)
            shift = shift_ref[...]
            lane = lax.broadcasted_iota(jnp.int32, (PAD, 128), 1)
            fine = (lane & 32) > 0
            outs = []
            for h in range(4):
                b, n = SPAN[h]
                lanes = slice(b, b + n)
                qm = q_s[k, rows, lanes] * head_mask(h)
                scores = nt(qm, k_s[k, rows, lanes]) * SCALE
                u = shifted(nt(qm, rel_ref[h, :, lanes]), shift, False)
                rest = u - u.astype(BF).astype(F32)
                u = jnp.where(fine, pltpu.roll(rest, 32, 1), u).astype(BF)
                scores = scores + nn(u, hot_ref[...]) + key_ref[...]
                top = jnp.max(scores, axis=1, keepdims=True)
                e = jnp.exp(scores - top)
                p = (e * (1.0 / jnp.sum(e, axis=1, keepdims=True))).astype(BF)
                p_s[(k * NW + w) * 4 + h] = p
                outs.append(nn(p, v_s[k, rows, lanes]))
            for i, part in enumerate(join_heads(outs)):
                att_s[k, rows, 128 * i : 128 * i + 128] = part.astype(BF)
            return 0

        lax.fori_loop(0, NW, window, 0)
        return 0

    lax.fori_loop(0, 4, heads_forward, 0)

    loads[3].wait()
    wire.have(1, OF_P)
    wire.have(3, OF_P)
    wire.step("A7")
    wire.step("B6")
    loads[7].wait()
    down_p = jnp.zeros((R, RANK), F32)
    for k in range(4):
        down_p += nt(att_s[k, :, 0:LOC], pack_m[k, 16:32, HID : HID + LOC])
    down_p = HALF * down_p
    dp16 = down_p.astype(BF)
    dpt = down_p.T.astype(BF)
    for n in range(5):
        cols = slice(256 * n, 256 * n + 256)
        total = nn(dp16, adp_ref[2, :, cols]) + bias_p[:, cols]
        for k in range(4):
            total += nn(att_s[k, :, 0:LOC], wp[k, :, cols])
        acc_a[:, cols] = total


    def norm_two(rows):
        mid = x_s[rows, :].astype(F32) + valid_ref[rows, :] * acc_a[rows, :]
        mid_s[rows, :] = mid
        xhat, _ = stats(mid)
        xn_s[rows, :] = (xhat * gain2 + shift2).astype(BF)

    row_loop(norm_two)
    down_1 = HALF * nt(xn_s[...], factor(1))
    d1_s[...] = jnp.where(lane_e == RANK, 1.0, down_1).astype(BF)
    d1t_s[...] = down_1.T.astype(BF)
    loads[4].wait()
    wire.edge("eg", lambda n: g_hbm.at[0:n], lambda n: w2.at[0, ROWS : ROWS + n], False, "wait")
    pick_rows = one_hot(window_rows(t)[0], 512)
    for n in range(5):
        cols = slice(256 * n, 256 * n + 256)
        g_s[:, cols] = nn(pick_rows, w2[0, 0:512, cols]).astype(BF)
    loads[6].start()
    valid = valid_ref[...]
    up2 = HALF * valid * nt(g_s[...], factor(3))
    up2_s[...] = up2.astype(BF)
    up2t_s[...] = up2.T.astype(BF)
    acc_a[...] = jnp.zeros((R, D), F32)
    acc_b[...] = jnp.zeros((R, D), F32)
    d2_s[...] = jnp.zeros((R, EXT), F32)
    up1_s[...] = jnp.zeros((R, EXT), F32)
    loads[5].wait()
    loads[6].wait()

    def slice_of(i):
        k = jnp.where(i < 5, 0, jnp.where(i < 10, 1, 2 + lax.rem(i, 2)))
        c = jnp.where(i < 10, lax.rem(i, 5), i // 2 - 5)
        cols = pl.ds(mult(c * HC, HC), HC)
        return k, cols, pack_m[k, :, pl.ds(mult(HID + c * HC, HC), HC)]

    def hidden_values(i):
        k, cols, a2 = slice_of(i)
        pre = nn(xn_s[...], w1[k, :, cols]) + nn(d1_s[...], pack_m[k, :, cols])
        gauss = jnp.exp(-0.5 * pre * pre)
        t = 1.0 / (1.0 + (ERF_P * 0.5**0.5) * jnp.abs(pre))
        poly = ERF_A[4]
        for a in ERF_A[3::-1]:
            poly = poly * t + a
        tail = (HALF * poly) * t * gauss
        phi = jnp.where(pre >= 0, 1.0 - tail, tail)
        slope = phi + pre * gauss * 0.3989422804014327
        dact = valid_ref[...] * nt(g_s[...], w2[k, cols, :]) + nn(up2_s[...], a2)
        act_s[lax.rem(i, 2)] = (pre * phi).astype(BF)
        dpre_s[lax.rem(i, 2)] = (dact * slope).astype(BF)

    def hidden_sums(i):
        k, cols, a2 = slice_of(i)
        act, dpre = act_s[lax.rem(i, 2)], dpre_s[lax.rem(i, 2)]
        sum_1[k, RANK : 2 * RANK, cols] = nn(up2t_s[...], act)[:RANK].astype(BF)
        sum_1[k, 0:RANK, cols] = nn(d1t_s[...], dpre)[:RANK].astype(BF)
        d2_s[...] += nt(act, a2)
        up1_s[...] += nt(dpre, pack_m[k, :, cols])
        for n in range(5):
            out = slice(256 * n, 256 * n + 256)
            acc_a[:, out] += nn(act, w2[k, cols, out])
            acc_b[:, out] += nt(dpre, w1[k, out, cols])

    def hidden(i, _):
        @pl.when(i == 5)
        def _():
            wire.have(1, [*OF_1, *OF_2])

        ticks(wire, AT_HIDDEN, i)

        @pl.when(i == 11)
        def _():
            wire.have(3, OF_1)

        for j in range(5):

            @pl.when(i == 11 + 2 * j)
            def _():
                wire.have(3, [OF_2[j]])

        hidden_sums(i - 1)
        hidden_values(i)
        return 0

    for what in AT_HIDDEN[0]:
        wire.step(what)
    hidden_values(0)
    lax.fori_loop(1, 20, hidden, 0)
    hidden_sums(19)

    wire.finish()
    wire.edge("ex", lambda n: x_hbm.at[0:n], lambda n: w1.at[0, ROWS : ROWS + n], False, "end")
    wire.edge("eg", lambda n: g_hbm.at[0:n], lambda n: w2.at[0, ROWS : ROWS + n], False, "end")
    wire.ready(done)
    d2 = HALF * d2_s[...]
    d2b = d2[:, :RANK].astype(BF)
    up1 = HALF * up1_s[...]
    up1b = up1[:, :RANK].astype(BF)
    rep_s[1] = nn((d2 * valid_ref[...]).T.astype(BF), g_s[...])[:RANK].astype(BF)
    rep_s[0] = nn(up1.T.astype(BF), xn_s[...])[:RANK].astype(BF)
    for k in range(4):
        sum_1[k, 2 * RANK :, 0 : D // 2] = half_of(rep_s, wire, k)
        sum_1[k, 2 * RANK :, D // 2 :] = jnp.zeros((RANK, D // 2), BF)
    wire.all_ready(done)
    all_1 = pl.ds(0, 3 * RANK)
    for k in (1, 2, 3):
        total_1.first(k, all_1, "go")
    for n in range(5):
        cols = slice(256 * n, 256 * n + 256)
        acc_a[:, cols] += nn(d2b, adp_ref[3, :, cols])
        acc_b[:, cols] += nn(up1b, adp_ref[1, :, cols])

    def back_two(rows):
        mid = mid_s[rows, :]
        ok = valid_ref[rows, :]
        x_out = mid + ok * (acc_a[rows, :] + bias_2)
        xhat, inv = stats(mid)
        dmid = g_s[rows, :].astype(F32) + norm_back(acc_b[rows, :], xhat, inv, gain2)
        mid_s[rows, :] = dmid
        g_s[rows, :] = (ok * dmid).astype(BF)
        xn_s[rows, :] = x_out.astype(BF)

    row_loop(back_two)

    def swap_edge(key, src, dst, do):
        to = lambda n: dst.at[0, 512 : 512 + n]
        wire.edge(key, lambda n: src.at[R - n : R], to, True, do)

    swap_edge("eo", xn_s, w1, "go")
    upp = HALF * nt(g_s[...], factor(2))
    upp16 = upp[:, :RANK].astype(BF)
    uppt = upp.T.astype(BF)
    rep_s[1] = nn(dpt, g_s[...]).astype(BF)
    d2_s[...] = jnp.zeros((R, EXT), F32)
    up2_s[:, 0:RANK] = upp16
    up2t_s[...] = uppt

    put_out = pltpu.make_async_copy(w1.at[0, 0:ROWS], out_hbm, local.at[8])

    def heads_backward(step, _):
        k = lax.rem(step + 1, 4)

        @pl.when(step == 1)
        def _():
            total_1.add_first([all_1])
            swap_edge("eo", xn_s, w1, "wait")
            home = home_rows(t, xn_s, w1.at[0, 512:672])
            for n in range(5):
                cols = slice(256 * n, 256 * n + 256)
                w1[0, 0:ROWS, cols] = home(cols)
            put_out.start()

        @pl.when(step == 2)
        def _():
            total_1.add_second()
            put_out.wait()
            swap_edge("eo", xn_s, w1, "end")
            row_loop(norm_one)

        @pl.when(step == 3)
        def _():
            total_1.add_third()

        datt = nt(g_s[...], wp[k]) + nn(up2_s[:, 0:RANK], pack_m[k, 16:32, HID : HID + LOC])
        datt_s[:, 0:LOC] = datt.astype(BF)
        sum_2[k, 0:RANK, 3 * LOC :] = nn(up2t_s[...], att_s[k, :, 0:LOC])[:RANK].astype(BF)

        def window(w, _):
            rows = pl.ds(mult(w * PAD), PAD)
            shift = shift_ref[...]
            dqs, dks, dvs = [], [], []
            for h in range(4):
                b, n = SPAN[h]
                lanes = slice(b, b + n)
                p = p_s[(k * NW + w) * 4 + h]
                da = datt_s[rows, lanes]
                dprob = nt(da * head_mask(h), v_s[k, rows, lanes])
                dvs.append(tn(p, da))
                pf = p.astype(F32)
                inner = jnp.sum(pf * dprob, axis=1, keepdims=True)
                ds = (pf * (dprob - inner)).astype(BF)
                du = shifted(nn(ds, back_ref[...]), shift, True).astype(BF)
                dqs.append(nn(ds, k_s[k, rows, lanes]) * SCALE + nn(du, rel_ref[h, :, lanes]))
                dks.append(tn(ds, q_s[k, rows, lanes]) * SCALE)
            for ref, parts in ((q_s, dqs), (k_s, dks), (v_s, dvs)):
                for i, part in enumerate(join_heads(parts)):
                    ref[k, rows, 128 * i : 128 * i + 128] = part.astype(BF)
            return 0

        lax.fori_loop(0, NW, window, 0)
        for j, ref in enumerate((q_s, k_s, v_s)):
            d = ref[k, :, 0:LOC]
            b = pack_q[k, EXT * j : EXT * j + EXT, 0:LOC]
            d2_s[...] += nt(d, b)
            sum_2[k, 0:RANK, j * LOC : (j + 1) * LOC] = nn(dqt_s[...], d)[:RANK].astype(BF)
        for kk in (1, 2, 3):

            @pl.when(k == kk)
            def _():
                total_2.first(kk, pl.ds(0, RANK), "go")

        return 0

    lax.fori_loop(0, 4, heads_backward, 0)
    puts = total_1.hand_out(split_1, whole_1, local.at[10:15])

    upq = HALF * d2_s[...]
    upqb = upq[:, :RANK].astype(BF)
    rep_s[0] = nn(upq.T.astype(BF), xn_s[...])[:RANK].astype(BF)
    for k in range(4):
        sum_2[k, RANK:, 0 : D // 2] = half_of(rep_s, wire, k)
        sum_2[k, RANK:, D // 2 :] = jnp.zeros((RANK, D // 2), BF)
    low, high = pl.ds(0, RANK), pl.ds(RANK, RANK)
    for k in (1, 2, 3):
        total_2.first(k, high, "go")

    for n in range(5):
        cols = slice(256 * n, 256 * n + 256)
        total = nn(upqb, adp_ref[0, :, cols])
        for k in range(4):
            for j, ref in enumerate((q_s, k_s, v_s)):
                total += nn(ref[k, :, 0:LOC], wq[k, j * LOC : (j + 1) * LOC, cols])
        acc_a[:, cols] = total
        if n == 1:
            total_2.add_first([low, high])
        if n == 3:
            total_2.add_second()

    def back_one(rows):
        ok = valid_ref[rows, :]
        xhat, inv = stats(x_s[rows, :].astype(F32))
        back = norm_back(ok * acc_a[rows, :], xhat, inv, gain1)
        g_s[rows, :] = (mid_s[rows, :] + back).astype(BF)

    row_loop(back_one)
    swap_edge("ef", g_s, w2, "go")
    total_2.add_third()
    swap_edge("ef", g_s, w2, "wait")
    home = home_rows(t, g_s, w2.at[0, 512:672])
    for n in range(5):
        cols = slice(256 * n, 256 * n + 256)
        w2[0, 0:ROWS, cols] = home(cols)
    put_grad = pltpu.make_async_copy(w2.at[0, 0:ROWS], grad_hbm, local.at[9])
    put_grad.start()
    puts += total_2.hand_out(split_2, whole_2, local.at[15:20])
    for cp in puts:
        cp.wait()
    put_grad.wait()
    swap_edge("ef", g_s, w2, "end")
    total_1.finish([all_1])
    total_2.finish([low, high])


def tables():
    tok = np.arange(PAD)
    inside = tok < TOK
    row, col = tok // WIN, tok % WIN
    lane = np.arange(128)[:, None]
    hot = (
        (((lane == row) | (lane == 32 + row)) & inside)
        | (((lane == 64 + col) | (lane == 96 + col)) & inside)
    ).astype(np.float32)
    back = ((lane == row) | (lane == 64 + col)) & inside
    shift = np.where(np.arange(128)[None] < 64, 13 - row[:, None], 13 - col[:, None])
    shift = np.where(inside[:, None], shift, 0).astype(np.int32)
    key = np.where(inside, 0.0, -1e30).astype(np.float32)[None]
    return jnp.asarray(hot, BF), jnp.asarray(back.T, BF), jnp.asarray(shift), jnp.asarray(key)


def call_kernel(images, args):
    any_ = pl.BlockSpec(memory_space=pl.ANY)
    vmem = pl.BlockSpec(memory_space=pltpu.VMEM)
    sds = jax.ShapeDtypeStruct
    V = pltpu.VMEM
    return pl.pallas_call(
        functools.partial(kernel, images),
        out_shape=(
            sds((ROWS, D), BF),
            sds((ROWS, D), BF),
            sds((images * 3 * RANK, D), BF),
            sds((2 * images * RANK, D), BF),
            sds((images * 2 * RANK, D), BF),
            sds((2 * images * RANK, D), BF),
        ),
        in_specs=[any_] * 8 + [vmem] * 8,
        out_specs=(any_,) * 6,
        scratch_shapes=[
            V((R, D), BF),
            V((R, D), BF),
            V((4, 3 * LOC, D), BF),
            V((4, LOC, D), BF),
            V((4, D, HID), BF),
            V((4, HID, D), BF),
            V((4,) + PACK_Q, BF),
            V((4,) + PACK_M, BF),
            V((4, 128, LP), BF),
            V((R, D), BF),
            V((4, R, LP), BF),
            V((4, R, LP), BF),
            V((4, R, LP), BF),
            V((4, R, LP), BF),
            V((4 * NW * 4, PAD, PAD), BF),
            V((R, D), F32),
            V((R, D), F32),
            V((R, D), F32),
            V((R, LP), BF),
            V((2, R, HC), BF),
            V((2, R, HC), BF),
            V((EXT, R), BF),
            V((EXT, R), BF),
            V((R, EXT), BF),
            V((R, EXT), BF),
            V((R, EXT), F32),
            V((R, EXT), F32),
            V((EXT, R), BF),
            V((R, 1), F32),
            V((4, 3 * RANK, D), BF),
            V((4, 2 * RANK, D), BF),
            V((2, RANK, D), BF),
            pltpu.SemaphoreType.DMA((2, 8 * NCH + 63)),
            pltpu.SemaphoreType.DMA((20,)),
            pltpu.SemaphoreType.REGULAR,
        ],
        compiler_params=pltpu.CompilerParams(
            collective_id=0, has_side_effects=True, vmem_limit_bytes=67_000_000
        ),
        name="block",
    )(*args)


def before_kernel(
    pick, x_ref, g_ref, q_down, q_up, p_down, p_up, down_1, up_1, down_2, up_2, q_bias, vec_ref,
    x_out, g_out, pack_q, pack_m, adp_ref,
):
    rows = x_ref.shape[0]
    for src, dst in ((x_ref, x_out), (g_ref, g_out)):
        dst[0:rows, :] = src[...]
        dst[rows:, :] = jnp.zeros((ROWS - rows, D), BF)
    for i, ref in enumerate((q_down, down_1, p_up, up_2)):
        adp_ref[i] = ref[0]
    line = lax.broadcasted_iota(jnp.int32, (RANK, 1), 0)

    def bias_rows(bias):
        return jnp.where(line == 0, bias, 0.0).astype(BF)

    biases, vecs = q_bias[...].astype(F32), vec_ref[...].astype(F32)
    for j in range(3):
        pack_q[EXT * j : EXT * j + RANK, :] = q_up[0, j]
        pack_q[EXT * j + RANK : EXT * j + EXT, :] = bias_rows(biases[j : j + 1, :])
    pack_m[0:RANK, 0:HID] = up_1[0]
    pack_m[RANK:EXT, 0:HID] = bias_rows(vecs[6:7, :])
    pack_m[0:RANK, HID:] = down_2[0]
    pack_m[RANK:EXT, HID : HID + LOC] = p_down[0]
    pack_m[RANK:EXT, HID + LOC :] = jnp.zeros((RANK, HID - LOC), BF)


def call_before(pick, args):
    sds = jax.ShapeDtypeStruct

    def spec(v):
        if v.ndim > 2:
            return pl.BlockSpec(
                (1,) + v.shape[1:], lambda i, p: (p[0],) + (0,) * (v.ndim - 1)
            )
        return pl.BlockSpec(v.shape, lambda i, p: (0, 0))

    outs = (
        sds((ROWS, D), BF), sds((ROWS, D), BF), sds(PACK_Q, BF), sds(PACK_M, BF),
        sds((4, RANK, D), BF),
    )
    return pl.pallas_call(
        before_kernel,
        out_shape=outs,
        grid_spec=pltpu.PrefetchScalarGridSpec(
            num_scalar_prefetch=1,
            grid=(1,),
            in_specs=[spec(v) for v in args],
            out_specs=tuple(
                pl.BlockSpec(v.shape, lambda i, p, n=len(v.shape): (0,) * n) for v in outs
            ),
        ),
        compiler_params=pltpu.CompilerParams(vmem_limit_bytes=66_500_000),
        name="before",
    )(pick, *args)


def after_kernel(
    images, pick, out_ref, grad_ref, split_1, whole_1, split_2, whole_2,
    out, grad, q_down, q_up, p_down, p_up, down_1, up_1, down_2, up_2,
):
    out[...] = out_ref[0 : out.shape[0], :]
    grad[...] = grad_ref[0 : out.shape[0], :]

    def slot(a, _):
        hits = [jnp.where(pick[i] == a, 1.0, 0.0) for i in range(images)]

        def total(ref, first, step, cols=slice(None)):
            v = 0.0
            for i in range(images):
                at = first + i * step
                v = v + hits[i] * ref[at : at + RANK, cols].astype(F32)
            return v

        up_1[a] = total(split_1, 0, 3 * RANK)
        down_2[a] = total(split_1, RANK, 3 * RANK)
        down_1[a] = total(whole_1, 0, RANK)
        up_2[a] = total(whole_1, images * RANK, RANK)
        q_down[a] = total(whole_2, 0, RANK)
        p_up[a] = total(whole_2, images * RANK, RANK)
        for j in range(3):
            q_up[a, j] = total(split_2, 0, 2 * RANK, slice(LOC * j, LOC * j + LOC))
        p_down[a] = total(split_2, 0, 2 * RANK, slice(3 * LOC, 4 * LOC))
        return 0

    lax.fori_loop(0, ADAPTERS, slot, 0)


def call_after(images, row_count, pick, args):
    sds = jax.ShapeDtypeStruct
    full = sds((ADAPTERS, RANK, D), F32)
    vmem = pl.BlockSpec(memory_space=pltpu.VMEM)
    return pl.pallas_call(
        functools.partial(after_kernel, images),
        out_shape=(
            sds((row_count, D), BF), sds((row_count, D), BF),
            full, sds((ADAPTERS, 3, RANK, LOC), F32), sds((ADAPTERS, RANK, LOC), F32), full,
            full, full, full, full,
        ),
        in_specs=[pl.BlockSpec(memory_space=pltpu.SMEM)] + [vmem] * 6,
        out_specs=(vmem,) * 10,
        compiler_params=pltpu.CompilerParams(vmem_limit_bytes=66_500_000),
        name="after",
    )(pick, *args)


def on_device(
    tokens,
    grad_out,
    adapter_index,
    norm1_gain,
    norm1_shift,
    qkv_weight,
    qkv_bias,
    rel_pos_h,
    rel_pos_w,
    proj_weight,
    proj_bias,
    norm2_gain,
    norm2_shift,
    lin1_weight,
    lin1_bias,
    lin2_weight,
    lin2_bias,
    qkv_down,
    qkv_up,
    proj_down,
    proj_up,
    lin1_down,
    lin1_up,
    lin2_down,
    lin2_up,
):
    images = adapter_index.shape[0]
    row_count = tokens.shape[0]
    dp_place = lax.axis_index("dp")
    image = dp_place // GROUP
    pick = lax.dynamic_slice_in_dim(adapter_index, image, 1)

    wq = jnp.transpose(qkv_weight, (1, 2, 0)).reshape(3 * LOC, D)
    vecs = jnp.zeros((8, D), BF)
    for i, v in enumerate(
        (norm1_gain, norm1_shift, norm2_gain, norm2_shift, proj_bias, lin2_bias, lin1_bias)
    ):
        vecs = jnp.where(np.arange(8)[:, None] == i, v[None], vecs)
    swap = lambda v: jnp.swapaxes(v, 1, 2)
    x, g, pack_q, pack_m, adps = call_before(
        pick,
        (tokens, grad_out, swap(qkv_down), swap(qkv_up), swap(proj_down), proj_up,
         swap(lin1_down), lin1_up, swap(lin2_down), lin2_up, qkv_bias, vecs),
    )
    hot, back, shift, key = tables()
    out, grad, split_1, whole_1, split_2, whole_2 = call_kernel(
        images,
        (x, g, wq, proj_weight, lin1_weight, lin2_weight, pack_q, pack_m,
         vecs, adps, shift, rel_pos_h, rel_pos_w, hot, back, key),
    )

    (out, grad, q_down, q_up, p_down, p_up, down_1, up_1, down_2, up_2) = call_after(
        images, row_count, adapter_index, (out, grad, split_1, whole_1, split_2, whole_2)
    )
    return (
        out,
        grad,
        swap(q_down),
        swap(q_up),
        swap(p_down),
        p_up,
        swap(down_1),
        up_1,
        swap(down_2),
        up_2,
    )


def solution(mesh):
    placed = (
        P(("dp", "tensor"), None),
        P(("dp", "tensor"), None),
        P(),
        P(),
        P(),
        P(None, None, "tensor"),
        P(None, "tensor"),
        P(),
        P(),
        P("tensor", None),
        P(),
        P(),
        P(),
        P(None, "tensor"),
        P("tensor"),
        P("tensor", None),
        P(),
        P(),
        P(None, None, None, "tensor"),
        P(None, "tensor", None),
        P(),
        P(),
        P(None, None, "tensor"),
        P(None, "tensor", None),
        P(),
    )
    return jax.shard_map(
        on_device,
        mesh=mesh,
        in_specs=placed,
        out_specs=(
            P(("dp", "tensor"), None),
            P(("dp", "tensor"), None),
            P(),
            P(None, None, None, "tensor"),
            P(None, "tensor", None),
            P(),
            P(),
            P(None, None, "tensor"),
            P(None, "tensor", None),
            P(),
        ),
        check_vma=False,
    )
```

```python
import functools

import jax
import jax.numpy as jnp
import numpy as np
from jax import lax
from jax.experimental import pallas as pl
from jax.experimental.pallas import tpu as pltpu
from jax.sharding import PartitionSpec as P

HEAD_DIM = 80
WIN = 14
SIDE = 64
RANK = 16
ADAPTERS = 8
WIN_DEV = 7
GROUP = 4
GRID = 5
TOK = WIN * WIN
PAD = 208
NW = 2
R = NW * PAD
D = 1280
LOC = 320
LP = 384
HID = 1280
HC = 256
PACK_Q = (3 * 32, 320)
PACK_M = (32, 2560)
ROWS = 352
EXT = 32
HALF = 0.5
EPS = 1e-6
SCALE = HEAD_DIM**-0.5
MESH = pl.DeviceIdType.MESH
BF = jnp.bfloat16
F32 = jnp.float32
SPAN = ((0, 128), (0, 256), (128, 128), (128, 256))
ERF_P = 0.3275911
ERF_A = (0.254829592, -0.284496736, 1.421413741, -1.453152027, 1.061405429)

CHUNKS = (
    [("q", 192 * i, 192) for i in range(5)]
    + [("p", 0, 320)]
    + [("1", 320 * i, 320) for i in range(4)]
    + [("2", 256 * i, 256) for i in range(5)]
)
NCH = len(CHUNKS)
OF_Q, OF_P, OF_1, OF_2 = range(5), [5], range(6, 10), range(10, 15)
THIRDS = {
    80: ((2, 2, 1), (2, 1, 2), (1, 2, 2)),
    64: ((2, 1, 1), (1, 2, 1), (1, 1, 2)),
    48: ((1, 1, 1),) * 3,
}


def nn(a, b):
    return jnp.dot(a, b, preferred_element_type=F32)


def nt(a, b):
    return lax.dot_general(a, b, (((1,), (1,)), ((), ())), preferred_element_type=F32)


def tn(a, b):
    return lax.dot_general(a, b, (((0,), (0,)), ((), ())), preferred_element_type=F32)


def mult(v, m=16):
    return v if isinstance(v, int) else pl.multiple_of(v, m)


class Wire:
    def __init__(self, own, land, packs, sems, images):
        self.own, self.land, self.sems = own, land, sems
        self.packs = packs
        dp, t = lax.axis_index("dp"), lax.axis_index("tensor")
        self.q = lax.rem(dp, 4)
        self.t = t
        self.image = dp // GROUP
        self.levels = images.bit_length() - 1
        self.dev = {"x": (dp ^ 1, t), "z": (dp ^ 2, t), "d": (dp ^ 3, t)}
        self.dev |= {"c": (dp, t ^ 1), "y": (dp, t ^ 2), "yc": (dp, t ^ 3)}
        self.dev |= {f"i{b}": (dp ^ (GROUP << b), t) for b in range(self.levels)}
        self.near = {"next": (dp, lax.rem(t + 1, 4)), "prev": (dp, lax.rem(t + 3, 4))}
        self.count = {}

    def barrier(self):
        bar = pltpu.get_barrier_semaphore()
        for d in self.dev.values():
            pl.semaphore_signal(bar, inc=1, device_id=d, device_id_type=MESH)
        pl.semaphore_wait(bar, len(self.dev))

    def copy(self, key, src, dst, dev):
        n = self.count.setdefault(key, len(self.count))
        return pltpu.make_async_remote_copy(
            src_ref=src,
            dst_ref=dst,
            send_sem=self.sems.at[0, n],
            recv_sem=self.sems.at[1, n],
            device_id=(self.dev | self.near)[dev],
            device_id_type=MESH,
        )

    def ready(self, sem):
        for d in self.dev.values():
            pl.semaphore_signal(sem, inc=1, device_id=d, device_id_type=MESH)

    def all_ready(self, sem):
        pl.semaphore_wait(sem, len(self.dev))

    def edge(self, key, src, dst, forward, do):
        for s in range(1, 4):
            n = 16 * -(-49 * s // 16)
            at, to = (s - 1, s) if forward else (s, s - 1)

            @pl.when(self.t == (at if do != "wait" else to))
            def _():
                cp = self.copy((key, s), src(n), dst(n), "next" if forward else "prev")
                getattr(cp, {"go": "start", "wait": "wait_recv", "end": "wait_send"}[do])()

    def pack(self, what, do):
        for i, (own, land) in enumerate(self.packs):
            cp = {
                "c": lambda: self.copy(("pc", i), own, land.at[1], "c"),
                "y": lambda: self.copy(("py", i), own, land.at[2], "y"),
                "f": lambda: self.copy(("pf", i), land.at[2], land.at[3], "c"),
            }[what]()
            getattr(cp, {"go": "start", "wait": "wait_recv", "end": "wait_send"}[do])()

    def parts(self, c):
        name, first, rows = CHUNKS[c]
        quarter = rows // 4
        a, b, d = (16 * v for v in THIRDS[quarter][c % 3])
        q = self.q

        def at(quart, off, n):
            return pl.ds(mult(first + quart * quarter + off), n)

        return {
            "all": pl.ds(first, rows),
            "y1": at(q, 0, quarter),
            "y2": at(q ^ 3, 0, a),
            "x1": at(q ^ 1, 0, quarter),
            "z1": at(q ^ 2, 0, quarter),
            "xs": at(q, 0, quarter),
            "x2": at(q ^ 2, a, b),
            "z2": at(q ^ 1, a + b, d),
        }

    def piece(self, c, what):
        name, first, rows = CHUNKS[c]
        own, land = self.own[name], self.land[name]
        p = self.parts(c)
        if what == "s":
            s = pl.ds(first, rows)
            return self.copy((c, what), own.at[s], land.at[1, s], "c")
        if what in ("y1", "y2"):
            return self.copy((c, what), own.at[p[what]], land.at[2, p[what]], "y")
        if what in ("x1", "z1"):
            return self.copy((c, what), land.at[2, p["xs"]], land.at[2, p["xs"]], what[0])
        if what in ("x2", "z2"):
            return self.copy((c, what), land.at[2, p[what]], land.at[2, p[what]], what[0])
        r = p["all"]
        return self.copy((c, what), land.at[2, r], land.at[3, r], "c")

    def begin(self, after_heads):
        self.pack("c", "go")
        for c in range(NCH):
            if c == OF_P[0]:
                after_heads()
                self.pack("y", "go")
            self.piece(c, "y1").start()
            self.piece(c, "y2").start()
            self.piece(c, "s").start()

    def step(self, what):
        kind, n = what[0], int(what[1:])
        if kind == "P":
            self.pack("y", "wait")
            self.pack("f", "go")
            return
        come, go = {
            "A": (("y1", "y2"), ("x1", "z1")),
            "B": (("x1", "z1"), ("x2", "z2")),
            "C": (("x2", "z2"), ("f",)),
        }[kind]
        for w in come:
            self.piece(n, w).wait_recv()
        for w in go:
            self.piece(n, w).start()

    def have(self, k, chunks):
        for c in chunks:
            if k == 1:
                self.piece(c, "s").wait_recv()
            if k == 3:
                self.piece(c, "f").wait_recv()

    def finish(self):
        for w in "cyf":
            self.pack(w, "end")
        for c in range(NCH):
            for w in ("s", "y1", "y2", "x1", "z1", "x2", "z2", "f"):
                self.piece(c, w).wait_send()


class Sum:
    def __init__(self, wire, name, send, buf, images):
        self.wire, self.name, self.send, self.buf, self.images = wire, name, send, buf, images
        self.n = send.shape[1]

    def go(self, key, src, dst, dev, do):
        cp = self.wire.copy((self.name, key), src, dst, dev)
        getattr(cp, {"go": "start", "wait": "wait_recv", "end": "wait_send"}[do])()

    def first(self, k, rows, do):
        dev = {1: "c", 2: "y", 3: "yc"}[k]
        dst = self.buf.at[1, pl.ds((k - 1) * self.n + rows.start, rows.size)]
        self.go(("a", k, rows.start), self.send.at[k, rows], dst, dev, do)

    def second(self, do):
        n = self.n
        for j, dev in enumerate("xzd"):
            src, dst = self.buf.at[1, pl.ds(3 * n, n)], self.buf.at[1, pl.ds((4 + j) * n, n)]
            self.go(("b", j), src, dst, dev, do)

    def third(self, level, do):
        n, size = self.n, 1 << level
        start = (self.wire.image >> level) << level
        if do == "wait":
            start = start ^ size
        rows = pl.ds(mult(start * n), size * n)
        self.go(("i", level), self.buf.at[2, rows], self.buf.at[2, rows], f"i{level}", do)

    def fourth(self, do):
        m, t = self.images * RANK, self.wire.t
        for k in (1, 2, 3):
            owner = t if do != "wait" else t ^ k
            part = self.buf.at[3, pl.ds(mult(owner * m), m), pl.ds(0, D // 2)]
            self.go(("r", k), part, part, {1: "c", 2: "y", 3: "yc"}[k], do)

    def finish(self, split):
        for k in (1, 2, 3):
            for rows in split:
                self.first(k, rows, "end")
        self.second("end")
        for b in range(self.wire.levels):
            self.third(b, "end")
        self.fourth("end")

    def part(self, slab, i):
        return self.buf[slab, i * self.n : (i + 1) * self.n, :].astype(F32)

    def add_first(self, split):
        for k in (1, 2, 3):
            for rows in split:
                self.first(k, rows, "wait")
        total = self.send[0].astype(F32) + self.part(1, 0) + self.part(1, 1) + self.part(1, 2)
        self.buf[1, 3 * self.n : 4 * self.n, :] = total.astype(BF)
        self.second("go")

    def add_second(self):
        self.second("wait")
        total = self.part(1, 3) + self.part(1, 4) + self.part(1, 5) + self.part(1, 6)
        self.buf[2, pl.ds(mult(self.wire.image * self.n), self.n), :] = total.astype(BF)
        if self.wire.levels:
            self.third(0, "go")

    def add_third(self):
        for b in range(self.wire.levels):
            self.third(b, "wait")
            if b + 1 < self.wire.levels:
                self.third(b + 1, "go")
        n, m = self.n, self.images * RANK
        for i in range(self.images):
            own = pl.ds(mult(self.wire.t * m + i * RANK), RANK)
            self.buf[3, own, 0 : D // 2] = self.buf[
                2, (i + 1) * n - RANK : (i + 1) * n, 0 : D // 2
            ]
        self.fourth("go")

    def hand_out(self, split_out, whole_out, local):
        self.fourth("wait")
        n, m = self.n, self.images * RANK
        copies = [
            pltpu.make_async_copy(self.buf.at[2, 0 : self.images * n], split_out, local.at[0]),
        ]
        for s in range(4):
            row, col = s // 2 * m, s % 2 * (D // 2)
            src = self.buf.at[3, s * m : (s + 1) * m, 0 : D // 2]
            dst = whole_out.at[row : row + m, col : col + D // 2]
            copies.append(pltpu.make_async_copy(src, dst, local.at[1 + s]))
        for cp in copies:
            cp.start()
        return copies


def half_of(ref, wire, k):
    s = wire.t ^ k
    return ref[s >> 1, :, pl.ds(mult((s & 1) * (D // 2), 128), D // 2)]


def one_hot(target, count):
    lane = lax.broadcasted_iota(jnp.int32, (target.shape[0], count), 1)
    return jnp.where(lane == target, 1.0, 0.0).astype(BF)


def window_rows(t):
    r = lax.broadcasted_iota(jnp.int32, (R, 1), 0)
    w = jnp.where(r >= PAD, 1, 0)
    i = r - PAD * w
    p = 49 * t + TOK * w + i
    source = jnp.where(i < TOK, jnp.where(p < 343, p, p + (ROWS - 343)), -1)
    slot = lax.rem(lax.axis_index("dp"), GROUP) * WIN_DEV + NW * t + w
    high = (slot * 205) >> 10
    row = (i * 4682) >> 16
    ok = (i < TOK) & (NW * t + w < WIN_DEV) & (slot < GRID * GRID)
    ok = ok & (high * WIN + row < SIDE) & ((slot - GRID * high) * WIN + i - WIN * row < SIDE)
    return source, jnp.where(ok, 1.0, 0.0).astype(F32)


def home_rows(t, mine, fetched):
    r = lax.broadcasted_iota(jnp.int32, (ROWS, 1), 0)
    o = r - 49 * t
    here = jnp.where(o < 0, -1, jnp.where(o < TOK, o, o + PAD - TOK))
    there = jnp.where(o < 0, r + 4 - t, -1)
    here, there = one_hot(here, R), one_hot(there, 160)
    return lambda cols: (nn(here, mine[:, cols]) + nn(there, fetched[:, cols])).astype(BF)


def shifted(values, shift, right):
    for bit in (1, 2, 4, 8):
        moved = pltpu.roll(values, bit if right else 128 - bit, 1)
        values = jnp.where((shift & bit) > 0, moved, values)
    return values


def join_heads(parts):
    lane = lax.broadcasted_iota(jnp.int32, (PAD, 128), 1)
    t0 = jnp.where(lane < 80, parts[0], parts[1][:, :128])
    t1 = jnp.where(
        lane < 32, parts[1][:, 128:], jnp.where(lane < 112, parts[2], parts[3][:, :128])
    )
    return (t0, t1, parts[3][:, 128:])


def head_mask(h, dtype=BF):
    base, width = SPAN[h]
    low = HEAD_DIM * h - base
    lane = lax.broadcasted_iota(jnp.int32, (1, width), 1)
    return jnp.where((lane >= low) & (lane < low + HEAD_DIM), 1.0, 0.0).astype(dtype)


def stats(v):
    mean = jnp.mean(v, axis=-1, keepdims=True)
    cen = v - mean
    inv = lax.rsqrt(jnp.mean(cen * cen, axis=-1, keepdims=True) + EPS)
    return cen * inv, inv


def norm_back(grad, xhat, inv, gain):
    e = grad * gain
    return inv * (
        e
        - jnp.mean(e, axis=-1, keepdims=True)
        - xhat * jnp.mean(e * xhat, axis=-1, keepdims=True)
    )


def row_loop(body, rows=PAD):
    def one(i, _):
        body(pl.ds(mult(i * rows), rows))
        return 0

    lax.fori_loop(0, R // rows, one, 0)


def ticks(wire, place, index):
    for at, steps in place.items():

        @pl.when(index == at)
        def _():
            for what in steps:
                wire.step(what)


AT_WINDOW = {1: ('A0',), 2: ('A1', 'B0'), 3: ('A2', 'B1', 'C0'), 5: ('A5',), 6: ('B5', 'A6'), 7: ('C5',)}
AT_SHARD = {2: ("A3", "B2", "C1", "A4", "B3", "C2")}
AFTER_GRADIENT = ("B4", "C3", "C4")
AT_HIDDEN = {0: ('C6', 'B7', 'A8'), 2: ('A9', 'B8', 'C7'), 4: ('A10', 'B9', 'C8'), 6: ('A11', 'B10', 'C9'), 8: ('A12', 'B11', 'C10'), 10: ('A13', 'B12', 'C11'), 12: ('A14', 'B13', 'C12'), 14: ('B14', 'C13'), 16: ('C14',)}


def kernel(
    images,
    x_hbm, g_hbm, wq_hbm, wp_hbm, w1_hbm, w2_hbm, pq_hbm, pm_hbm,
    vec_ref, adp_ref, shift_ref, row_ref, col_ref, hot_ref, back_ref, key_ref,
    out_hbm, grad_hbm, split_1, whole_1, split_2, whole_2,
    x_s, g_s, wq, wp, w1, w2, pack_q, pack_m, rel_ref, xn_s, q_s, k_s, v_s, att_s, p_s, mid_s, acc_a, acc_b,
    datt_s, act_s, dpre_s, d1t_s, up2t_s, d1_s, up2_s, d2_s, up1_s, dqt_s, valid_ref, sum_1, sum_2,
    rep_s, sems, local, done,
):
    own = {"q": wq_hbm, "p": wp_hbm, "1": w1_hbm, "2": w2_hbm}
    land = {"q": wq, "p": wp, "1": w1, "2": w2}
    wire = Wire(own, land, [(pq_hbm, pack_q), (pm_hbm, pack_m)], sems, images)
    total_1 = Sum(wire, "s1", sum_1, w1, images)
    total_2 = Sum(wire, "s2", sum_2, w2, images)
    t = wire.t
    blank = jnp.zeros((512 - ROWS, D), BF)
    w1[0, ROWS:512, :] = blank
    w2[0, ROWS:512, :] = blank
    wire.barrier()

    def edge_in(key, src, dst):
        to = lambda n: dst.at[0, ROWS : ROWS + n]
        wire.edge(key, lambda n: src.at[0:n], to, False, "go")

    edge_in("ex", x_hbm, w1)
    wire.begin(lambda: edge_in("eg", g_hbm, w2))
    pairs = [
        (x_hbm, w1.at[0, 0:ROWS]), (pq_hbm, pack_q.at[0]), (wq_hbm, wq.at[0]),
        (wp_hbm, wp.at[0]), (g_hbm, w2.at[0, 0:ROWS]), (w1_hbm, w1.at[0]), (w2_hbm, w2.at[0]),
        (pm_hbm, pack_m.at[0]),
    ]
    loads = [pltpu.make_async_copy(a, b, local.at[i]) for i, (a, b) in enumerate(pairs)]
    for cp in loads[:5] + loads[7:]:
        cp.start()
    lane_pad = jnp.zeros((4, R, LP - 256), BF)
    for ref in (q_s, k_s, v_s, att_s):
        ref[:, :, 256:LP] = lane_pad
    datt_s[:, 256:LP] = lane_pad[0]

    vecs = vec_ref[...].astype(F32)
    gain1, shift1, gain2, shift2, bias_p, bias_2 = (vecs[i : i + 1, :] for i in range(6))

    def factor(i):
        return jnp.concatenate([adp_ref[i], jnp.zeros((EXT - RANK, D), BF)], axis=0)

    lane_e = lax.broadcasted_iota(jnp.int32, (R, EXT), 1)
    line = lax.broadcasted_iota(jnp.int32, (128, 2 * WIN - 1), 0)
    lane = lax.broadcasted_iota(jnp.int32, (128, 2 * WIN - 1), 1)
    rel = nn(jnp.where(line + lane == 2 * WIN - 2, 1.0, 0.0).astype(BF), row_ref[...])
    rel += nn(jnp.where(line + lane == 64 + 2 * WIN - 2, 1.0, 0.0).astype(BF), col_ref[...])
    rel = rel.astype(BF)
    line = lax.broadcasted_iota(jnp.int32, (HEAD_DIM, LP), 0)
    lane = lax.broadcasted_iota(jnp.int32, (HEAD_DIM, LP), 1)
    for h in range(4):
        put = jnp.where(lane == line + HEAD_DIM * h, 1.0, 0.0).astype(BF)
        rel_ref[h] = nn(rel, put).astype(BF)
    source, valid = window_rows(t)
    valid_ref[...] = valid
    pick_rows = one_hot(source, 512)

    loads[0].wait()
    wire.edge("ex", lambda n: x_hbm.at[0:n], lambda n: w1.at[0, ROWS : ROWS + n], False, "wait")
    for n in range(5):
        cols = slice(256 * n, 256 * n + 256)
        x_s[:, cols] = nn(pick_rows, w1[0, 0:512, cols]).astype(BF)
    loads[5].start()

    def norm_one(rows):
        xhat, _ = stats(x_s[rows, :].astype(F32))
        xn_s[rows, :] = (valid_ref[rows, :] * (xhat * gain1 + shift1)).astype(BF)

    row_loop(norm_one)
    loads[1].wait()
    down_q = HALF * nt(xn_s[...], factor(0))
    dq_ext = jnp.where(lane_e == RANK, 1.0, down_q).astype(BF)
    d1_s[...] = dq_ext
    dqt_s[...] = down_q.T.astype(BF)
    loads[2].wait()

    def output_gradient():
        loads[4].wait()
        wire.edge("eg", lambda n: g_hbm.at[0:n], lambda n: w2.at[0, ROWS : ROWS + n], False, "wait")
        picks = one_hot(window_rows(t)[0], 512)
        for n in range(5):
            cols = slice(256 * n, 256 * n + 256)
            g_s[:, cols] = nn(picks, w2[0, 0:512, cols]).astype(BF)
        loads[6].start()
        ok = valid_ref[...]
        up2 = HALF * ok * nt(g_s[...], factor(3))
        up2_s[...] = up2.astype(BF)
        up2t_s[...] = up2.T.astype(BF)
        acc_b[...] = jnp.zeros((R, D), F32)
        d2_s[...] = jnp.zeros((R, EXT), F32)
        up1_s[...] = jnp.zeros((R, EXT), F32)

    def heads_forward(k, _):
        @pl.when(k == 1)
        def _():
            wire.pack("c", "wait")
            wire.have(1, OF_Q)

        ticks(wire, AT_SHARD, k)

        @pl.when(k == 2)
        def _():
            output_gradient()
            for what in AFTER_GRADIENT:
                wire.step(what)

        @pl.when(k == 3)
        def _():
            wire.have(3, OF_Q)

        x_q = nt(xn_s[...], wq[k])

        @pl.when(k == 2)
        def _():
            wire.step("P0")

        @pl.when(k == 3)
        def _():
            wire.pack("f", "wait")

        for j, ref in enumerate((q_s, k_s, v_s)):
            low_rank = nn(d1_s[...], pack_q[k, EXT * j : EXT * j + EXT, 0:LOC])
            ref[k, :, 0:LOC] = (x_q[:, LOC * j : LOC * j + LOC] + low_rank).astype(BF)

        def window(w, _):
            ticks(wire, AT_WINDOW, k * NW + w)
            rows = pl.ds(mult(w * PAD), PAD)
            shift = shift_ref[...]
            lane = lax.broadcasted_iota(jnp.int32, (PAD, 128), 1)
            fine = (lane & 32) > 0
            outs = []
            for h in range(4):
                b, n = SPAN[h]
                lanes = slice(b, b + n)
                qm = q_s[k, rows, lanes] * head_mask(h)
                scores = nt(qm, k_s[k, rows, lanes]) * SCALE
                u = shifted(nt(qm, rel_ref[h, :, lanes]), shift, False)
                rest = u - u.astype(BF).astype(F32)
                u = jnp.where(fine, pltpu.roll(rest, 32, 1), u).astype(BF)
                scores = scores + nn(u, hot_ref[...]) + key_ref[...]
                top = jnp.max(scores, axis=1, keepdims=True)
                e = jnp.exp(scores - top)
                p = (e * (1.0 / jnp.sum(e, axis=1, keepdims=True))).astype(BF)
                p_s[(k * NW + w) * 4 + h] = p
                outs.append(nn(p, v_s[k, rows, lanes]))
            for i, part in enumerate(join_heads(outs)):
                att_s[k, rows, 128 * i : 128 * i + 128] = part.astype(BF)
            return 0

        lax.fori_loop(0, NW, window, 0)
        return 0

    lax.fori_loop(0, 4, heads_forward, 0)

    loads[3].wait()
    wire.have(1, OF_P)
    wire.have(3, OF_P)
    wire.step("A7")
    wire.step("B6")
    loads[7].wait()
    down_p = jnp.zeros((R, RANK), F32)
    for k in range(4):
        down_p += nt(att_s[k, :, 0:LOC], pack_m[k, 16:32, HID : HID + LOC])
    down_p = HALF * down_p
    dp16 = down_p.astype(BF)
    dpt = down_p.T.astype(BF)
    for n in range(5):
        cols = slice(256 * n, 256 * n + 256)
        total = nn(dp16, adp_ref[2, :, cols]) + bias_p[:, cols]
        for k in range(4):
            total += nn(att_s[k, :, 0:LOC], wp[k, :, cols])
        acc_a[:, cols] = total


    def norm_two(rows):
        mid = x_s[rows, :].astype(F32) + valid_ref[rows, :] * acc_a[rows, :]
        mid_s[rows, :] = mid
        xhat, _ = stats(mid)
        xn_s[rows, :] = (xhat * gain2 + shift2).astype(BF)

    row_loop(norm_two)
    down_1 = HALF * nt(xn_s[...], factor(1))
    d1_s[...] = jnp.where(lane_e == RANK, 1.0, down_1).astype(BF)
    d1t_s[...] = down_1.T.astype(BF)
    acc_a[...] = jnp.zeros((R, D), F32)
    loads[5].wait()
    loads[6].wait()

    def slice_of(i):
        k = jnp.where(i < 5, 0, jnp.where(i < 10, 1, 2 + lax.rem(i, 2)))
        c = jnp.where(i < 10, lax.rem(i, 5), i // 2 - 5)
        cols = pl.ds(mult(c * HC, HC), HC)
        return k, cols, pack_m[k, :, pl.ds(mult(HID + c * HC, HC), HC)]

    def hidden_values(i):
        k, cols, a2 = slice_of(i)
        pre = nn(xn_s[...], w1[k, :, cols]) + nn(d1_s[...], pack_m[k, :, cols])
        gauss = jnp.exp(-0.5 * pre * pre)
        t = 1.0 / (1.0 + (ERF_P * 0.5**0.5) * jnp.abs(pre))
        poly = ERF_A[4]
        for a in ERF_A[3::-1]:
            poly = poly * t + a
        tail = (HALF * poly) * t * gauss
        phi = jnp.where(pre >= 0, 1.0 - tail, tail)
        slope = phi + pre * gauss * 0.3989422804014327
        dact = valid_ref[...] * nt(g_s[...], w2[k, cols, :]) + nn(up2_s[...], a2)
        act_s[lax.rem(i, 2)] = (pre * phi).astype(BF)
        dpre_s[lax.rem(i, 2)] = (dact * slope).astype(BF)

    def hidden_sums(i):
        k, cols, a2 = slice_of(i)
        act, dpre = act_s[lax.rem(i, 2)], dpre_s[lax.rem(i, 2)]
        sum_1[k, RANK : 2 * RANK, cols] = nn(up2t_s[...], act)[:RANK].astype(BF)
        sum_1[k, 0:RANK, cols] = nn(d1t_s[...], dpre)[:RANK].astype(BF)
        d2_s[...] += nt(act, a2)
        up1_s[...] += nt(dpre, pack_m[k, :, cols])
        for n in range(5):
            out = slice(256 * n, 256 * n + 256)
            acc_a[:, out] += nn(act, w2[k, cols, out])
            acc_b[:, out] += nt(dpre, w1[k, out, cols])

    def hidden(i, _):
        @pl.when(i == 5)
        def _():
            wire.have(1, [*OF_1, *OF_2])

        ticks(wire, AT_HIDDEN, i)

        @pl.when(i == 11)
        def _():
            wire.have(3, OF_1)

        for j in range(5):

            @pl.when(i == 11 + 2 * j)
            def _():
                wire.have(3, [OF_2[j]])

        hidden_sums(i - 1)
        hidden_values(i)
        return 0

    for what in AT_HIDDEN[0]:
        wire.step(what)
    hidden_values(0)
    lax.fori_loop(1, 20, hidden, 0)
    hidden_sums(19)

    wire.finish()
    wire.edge("ex", lambda n: x_hbm.at[0:n], lambda n: w1.at[0, ROWS : ROWS + n], False, "end")
    wire.edge("eg", lambda n: g_hbm.at[0:n], lambda n: w2.at[0, ROWS : ROWS + n], False, "end")
    wire.ready(done)
    d2 = HALF * d2_s[...]
    d2b = d2[:, :RANK].astype(BF)
    up1 = HALF * up1_s[...]
    up1b = up1[:, :RANK].astype(BF)
    rep_s[1] = nn((d2 * valid_ref[...]).T.astype(BF), g_s[...])[:RANK].astype(BF)
    rep_s[0] = nn(up1.T.astype(BF), xn_s[...])[:RANK].astype(BF)
    for k in range(4):
        sum_1[k, 2 * RANK :, 0 : D // 2] = half_of(rep_s, wire, k)
        sum_1[k, 2 * RANK :, D // 2 :] = jnp.zeros((RANK, D // 2), BF)
    wire.all_ready(done)
    all_1 = pl.ds(0, 3 * RANK)
    for k in (1, 2, 3):
        total_1.first(k, all_1, "go")
    for n in range(5):
        cols = slice(256 * n, 256 * n + 256)
        acc_a[:, cols] += nn(d2b, adp_ref[3, :, cols])
        acc_b[:, cols] += nn(up1b, adp_ref[1, :, cols])

    def back_two(rows):
        mid = mid_s[rows, :]
        ok = valid_ref[rows, :]
        x_out = mid + ok * (acc_a[rows, :] + bias_2)
        xhat, inv = stats(mid)
        dmid = g_s[rows, :].astype(F32) + norm_back(acc_b[rows, :], xhat, inv, gain2)
        mid_s[rows, :] = dmid
        g_s[rows, :] = (ok * dmid).astype(BF)
        xn_s[rows, :] = x_out.astype(BF)

    row_loop(back_two)

    def swap_edge(key, src, dst, do):
        to = lambda n: dst.at[0, 512 : 512 + n]
        wire.edge(key, lambda n: src.at[R - n : R], to, True, do)

    swap_edge("eo", xn_s, w1, "go")
    upp = HALF * nt(g_s[...], factor(2))
    upp16 = upp[:, :RANK].astype(BF)
    uppt = upp.T.astype(BF)
    rep_s[1] = nn(dpt, g_s[...]).astype(BF)
    d2_s[...] = jnp.zeros((R, EXT), F32)
    up2_s[:, 0:RANK] = upp16
    up2t_s[...] = uppt

    put_out = pltpu.make_async_copy(w1.at[0, 0:ROWS], out_hbm, local.at[8])

    def heads_backward(step, _):
        k = lax.rem(step + 1, 4)

        @pl.when(step == 1)
        def _():
            total_1.add_first([all_1])
            swap_edge("eo", xn_s, w1, "wait")
            home = home_rows(t, xn_s, w1.at[0, 512:672])
            for n in range(5):
                cols = slice(256 * n, 256 * n + 256)
                w1[0, 0:ROWS, cols] = home(cols)
            put_out.start()

        @pl.when(step == 2)
        def _():
            total_1.add_second()
            put_out.wait()
            swap_edge("eo", xn_s, w1, "end")
            row_loop(norm_one)

        @pl.when(step == 3)
        def _():
            total_1.add_third()

        datt = nt(g_s[...], wp[k]) + nn(up2_s[:, 0:RANK], pack_m[k, 16:32, HID : HID + LOC])
        datt_s[:, 0:LOC] = datt.astype(BF)
        sum_2[k, 0:RANK, 3 * LOC :] = nn(up2t_s[...], att_s[k, :, 0:LOC])[:RANK].astype(BF)

        def window(w, _):
            rows = pl.ds(mult(w * PAD), PAD)
            shift = shift_ref[...]
            dqs, dks, dvs = [], [], []
            for h in range(4):
                b, n = SPAN[h]
                lanes = slice(b, b + n)
                p = p_s[(k * NW + w) * 4 + h]
                da = datt_s[rows, lanes]
                dprob = nt(da * head_mask(h), v_s[k, rows, lanes])
                dvs.append(tn(p, da))
                pf = p.astype(F32)
                inner = jnp.sum(pf * dprob, axis=1, keepdims=True)
                ds = (pf * (dprob - inner)).astype(BF)
                du = shifted(nn(ds, back_ref[...]), shift, True).astype(BF)
                dqs.append(nn(ds, k_s[k, rows, lanes]) * SCALE + nn(du, rel_ref[h, :, lanes]))
                dks.append(tn(ds, q_s[k, rows, lanes]) * SCALE)
            for ref, parts in ((q_s, dqs), (k_s, dks), (v_s, dvs)):
                for i, part in enumerate(join_heads(parts)):
                    ref[k, rows, 128 * i : 128 * i + 128] = part.astype(BF)
            return 0

        lax.fori_loop(0, NW, window, 0)
        for j, ref in enumerate((q_s, k_s, v_s)):
            d = ref[k, :, 0:LOC]
            b = pack_q[k, EXT * j : EXT * j + EXT, 0:LOC]
            d2_s[...] += nt(d, b)
            sum_2[k, 0:RANK, j * LOC : (j + 1) * LOC] = nn(dqt_s[...], d)[:RANK].astype(BF)
        for kk in (1, 2, 3):

            @pl.when(k == kk)
            def _():
                total_2.first(kk, pl.ds(0, RANK), "go")

        return 0

    lax.fori_loop(0, 4, heads_backward, 0)
    puts = total_1.hand_out(split_1, whole_1, local.at[10:15])

    upq = HALF * d2_s[...]
    upqb = upq[:, :RANK].astype(BF)
    rep_s[0] = nn(upq.T.astype(BF), xn_s[...])[:RANK].astype(BF)
    for k in range(4):
        sum_2[k, RANK:, 0 : D // 2] = half_of(rep_s, wire, k)
        sum_2[k, RANK:, D // 2 :] = jnp.zeros((RANK, D // 2), BF)
    low, high = pl.ds(0, RANK), pl.ds(RANK, RANK)
    for k in (1, 2, 3):
        total_2.first(k, high, "go")

    for n in range(5):
        cols = slice(256 * n, 256 * n + 256)
        total = nn(upqb, adp_ref[0, :, cols])
        for k in range(4):
            for j, ref in enumerate((q_s, k_s, v_s)):
                total += nn(ref[k, :, 0:LOC], wq[k, j * LOC : (j + 1) * LOC, cols])
        acc_a[:, cols] = total
        if n == 1:
            total_2.add_first([low, high])
        if n == 3:
            total_2.add_second()

    def back_one(rows):
        ok = valid_ref[rows, :]
        xhat, inv = stats(x_s[rows, :].astype(F32))
        back = norm_back(ok * acc_a[rows, :], xhat, inv, gain1)
        g_s[rows, :] = (mid_s[rows, :] + back).astype(BF)

    row_loop(back_one)
    swap_edge("ef", g_s, w2, "go")
    total_2.add_third()
    swap_edge("ef", g_s, w2, "wait")
    home = home_rows(t, g_s, w2.at[0, 512:672])
    for n in range(5):
        cols = slice(256 * n, 256 * n + 256)
        w2[0, 0:ROWS, cols] = home(cols)
    put_grad = pltpu.make_async_copy(w2.at[0, 0:ROWS], grad_hbm, local.at[9])
    put_grad.start()
    puts += total_2.hand_out(split_2, whole_2, local.at[15:20])
    for cp in puts:
        cp.wait()
    put_grad.wait()
    swap_edge("ef", g_s, w2, "end")
    total_1.finish([all_1])
    total_2.finish([low, high])


def tables():
    tok = np.arange(PAD)
    inside = tok < TOK
    row, col = tok // WIN, tok % WIN
    lane = np.arange(128)[:, None]
    hot = (
        (((lane == row) | (lane == 32 + row)) & inside)
        | (((lane == 64 + col) | (lane == 96 + col)) & inside)
    ).astype(np.float32)
    back = ((lane == row) | (lane == 64 + col)) & inside
    shift = np.where(np.arange(128)[None] < 64, 13 - row[:, None], 13 - col[:, None])
    shift = np.where(inside[:, None], shift, 0).astype(np.int32)
    key = np.where(inside, 0.0, -1e30).astype(np.float32)[None]
    return jnp.asarray(hot, BF), jnp.asarray(back.T, BF), jnp.asarray(shift), jnp.asarray(key)


def call_kernel(images, args):
    any_ = pl.BlockSpec(memory_space=pl.ANY)
    vmem = pl.BlockSpec(memory_space=pltpu.VMEM)
    sds = jax.ShapeDtypeStruct
    V = pltpu.VMEM
    return pl.pallas_call(
        functools.partial(kernel, images),
        out_shape=(
            sds((ROWS, D), BF),
            sds((ROWS, D), BF),
            sds((images * 3 * RANK, D), BF),
            sds((2 * images * RANK, D), BF),
            sds((images * 2 * RANK, D), BF),
            sds((2 * images * RANK, D), BF),
        ),
        in_specs=[any_] * 8 + [vmem] * 8,
        out_specs=(any_,) * 6,
        scratch_shapes=[
            V((R, D), BF),
            V((R, D), BF),
            V((4, 3 * LOC, D), BF),
            V((4, LOC, D), BF),
            V((4, D, HID), BF),
            V((4, HID, D), BF),
            V((4,) + PACK_Q, BF),
            V((4,) + PACK_M, BF),
            V((4, 128, LP), BF),
            V((R, D), BF),
            V((4, R, LP), BF),
            V((4, R, LP), BF),
            V((4, R, LP), BF),
            V((4, R, LP), BF),
            V((4 * NW * 4, PAD, PAD), BF),
            V((R, D), F32),
            V((R, D), F32),
            V((R, D), F32),
            V((R, LP), BF),
            V((2, R, HC), BF),
            V((2, R, HC), BF),
            V((EXT, R), BF),
            V((EXT, R), BF),
            V((R, EXT), BF),
            V((R, EXT), BF),
            V((R, EXT), F32),
            V((R, EXT), F32),
            V((EXT, R), BF),
            V((R, 1), F32),
            V((4, 3 * RANK, D), BF),
            V((4, 2 * RANK, D), BF),
            V((2, RANK, D), BF),
            pltpu.SemaphoreType.DMA((2, 8 * NCH + 63)),
            pltpu.SemaphoreType.DMA((20,)),
            pltpu.SemaphoreType.REGULAR,
        ],
        compiler_params=pltpu.CompilerParams(
            collective_id=0, has_side_effects=True, vmem_limit_bytes=67_000_000
        ),
        name="block",
    )(*args)


def before_kernel(
    pick, x_ref, g_ref, q_down, q_up, p_down, p_up, down_1, up_1, down_2, up_2, q_bias, vec_ref,
    x_out, g_out, pack_q, pack_m, adp_ref,
):
    rows = x_ref.shape[0]
    for src, dst in ((x_ref, x_out), (g_ref, g_out)):
        dst[0:rows, :] = src[...]
        dst[rows:, :] = jnp.zeros((ROWS - rows, D), BF)
    for i, ref in enumerate((q_down, down_1, p_up, up_2)):
        adp_ref[i] = ref[0]
    line = lax.broadcasted_iota(jnp.int32, (RANK, 1), 0)

    def bias_rows(bias):
        return jnp.where(line == 0, bias, 0.0).astype(BF)

    biases, vecs = q_bias[...].astype(F32), vec_ref[...].astype(F32)
    for j in range(3):
        pack_q[EXT * j : EXT * j + RANK, :] = q_up[0, j]
        pack_q[EXT * j + RANK : EXT * j + EXT, :] = bias_rows(biases[j : j + 1, :])
    pack_m[0:RANK, 0:HID] = up_1[0]
    pack_m[RANK:EXT, 0:HID] = bias_rows(vecs[6:7, :])
    pack_m[0:RANK, HID:] = down_2[0]
    pack_m[RANK:EXT, HID : HID + LOC] = p_down[0]
    pack_m[RANK:EXT, HID + LOC :] = jnp.zeros((RANK, HID - LOC), BF)


def call_before(pick, args):
    sds = jax.ShapeDtypeStruct

    def spec(v):
        if v.ndim > 2:
            return pl.BlockSpec(
                (1,) + v.shape[1:], lambda i, p: (p[0],) + (0,) * (v.ndim - 1)
            )
        return pl.BlockSpec(v.shape, lambda i, p: (0, 0))

    outs = (
        sds((ROWS, D), BF), sds((ROWS, D), BF), sds(PACK_Q, BF), sds(PACK_M, BF),
        sds((4, RANK, D), BF),
    )
    return pl.pallas_call(
        before_kernel,
        out_shape=outs,
        grid_spec=pltpu.PrefetchScalarGridSpec(
            num_scalar_prefetch=1,
            grid=(1,),
            in_specs=[spec(v) for v in args],
            out_specs=tuple(
                pl.BlockSpec(v.shape, lambda i, p, n=len(v.shape): (0,) * n) for v in outs
            ),
        ),
        compiler_params=pltpu.CompilerParams(vmem_limit_bytes=66_500_000),
        name="before",
    )(pick, *args)


def after_kernel(
    images, pick, out_ref, grad_ref, split_1, whole_1, split_2, whole_2,
    out, grad, q_down, q_up, p_down, p_up, down_1, up_1, down_2, up_2,
):
    out[...] = out_ref[0 : out.shape[0], :]
    grad[...] = grad_ref[0 : out.shape[0], :]

    def slot(a, _):
        hits = [jnp.where(pick[i] == a, 1.0, 0.0) for i in range(images)]

        def total(ref, first, step, cols=slice(None)):
            v = 0.0
            for i in range(images):
                at = first + i * step
                v = v + hits[i] * ref[at : at + RANK, cols].astype(F32)
            return v

        up_1[a] = total(split_1, 0, 3 * RANK)
        down_2[a] = total(split_1, RANK, 3 * RANK)
        down_1[a] = total(whole_1, 0, RANK)
        up_2[a] = total(whole_1, images * RANK, RANK)
        q_down[a] = total(whole_2, 0, RANK)
        p_up[a] = total(whole_2, images * RANK, RANK)
        for j in range(3):
            q_up[a, j] = total(split_2, 0, 2 * RANK, slice(LOC * j, LOC * j + LOC))
        p_down[a] = total(split_2, 0, 2 * RANK, slice(3 * LOC, 4 * LOC))
        return 0

    lax.fori_loop(0, ADAPTERS, slot, 0)


def call_after(images, row_count, pick, args):
    sds = jax.ShapeDtypeStruct
    full = sds((ADAPTERS, RANK, D), F32)
    vmem = pl.BlockSpec(memory_space=pltpu.VMEM)
    return pl.pallas_call(
        functools.partial(after_kernel, images),
        out_shape=(
            sds((row_count, D), BF), sds((row_count, D), BF),
            full, sds((ADAPTERS, 3, RANK, LOC), F32), sds((ADAPTERS, RANK, LOC), F32), full,
            full, full, full, full,
        ),
        in_specs=[pl.BlockSpec(memory_space=pltpu.SMEM)] + [vmem] * 6,
        out_specs=(vmem,) * 10,
        compiler_params=pltpu.CompilerParams(vmem_limit_bytes=66_500_000),
        name="after",
    )(pick, *args)


def on_device(
    tokens,
    grad_out,
    adapter_index,
    norm1_gain,
    norm1_shift,
    qkv_weight,
    qkv_bias,
    rel_pos_h,
    rel_pos_w,
    proj_weight,
    proj_bias,
    norm2_gain,
    norm2_shift,
    lin1_weight,
    lin1_bias,
    lin2_weight,
    lin2_bias,
    qkv_down,
    qkv_up,
    proj_down,
    proj_up,
    lin1_down,
    lin1_up,
    lin2_down,
    lin2_up,
):
    images = adapter_index.shape[0]
    row_count = tokens.shape[0]
    dp_place = lax.axis_index("dp")
    image = dp_place // GROUP
    pick = lax.dynamic_slice_in_dim(adapter_index, image, 1)

    wq = jnp.transpose(qkv_weight, (1, 2, 0)).reshape(3 * LOC, D)
    vecs = jnp.zeros((8, D), BF)
    for i, v in enumerate(
        (norm1_gain, norm1_shift, norm2_gain, norm2_shift, proj_bias, lin2_bias, lin1_bias)
    ):
        vecs = jnp.where(np.arange(8)[:, None] == i, v[None], vecs)
    swap = lambda v: jnp.swapaxes(v, 1, 2)
    x, g, pack_q, pack_m, adps = call_before(
        pick,
        (tokens, grad_out, swap(qkv_down), swap(qkv_up), swap(proj_down), proj_up,
         swap(lin1_down), lin1_up, swap(lin2_down), lin2_up, qkv_bias, vecs),
    )
    hot, back, shift, key = tables()
    out, grad, split_1, whole_1, split_2, whole_2 = call_kernel(
        images,
        (x, g, wq, proj_weight, lin1_weight, lin2_weight, pack_q, pack_m,
         vecs, adps, shift, rel_pos_h, rel_pos_w, hot, back, key),
    )

    (out, grad, q_down, q_up, p_down, p_up, down_1, up_1, down_2, up_2) = call_after(
        images, row_count, adapter_index, (out, grad, split_1, whole_1, split_2, whole_2)
    )
    return (
        out,
        grad,
        swap(q_down),
        swap(q_up),
        swap(p_down),
        p_up,
        swap(down_1),
        up_1,
        swap(down_2),
        up_2,
    )


def solution(mesh):
    placed = (
        P(("dp", "tensor"), None),
        P(("dp", "tensor"), None),
        P(),
        P(),
        P(),
        P(None, None, "tensor"),
        P(None, "tensor"),
        P(),
        P(),
        P("tensor", None),
        P(),
        P(),
        P(),
        P(None, "tensor"),
        P("tensor"),
        P("tensor", None),
        P(),
        P(),
        P(None, None, None, "tensor"),
        P(None, "tensor", None),
        P(),
        P(),
        P(None, None, "tensor"),
        P(None, "tensor", None),
        P(),
    )
    return jax.shard_map(
        on_device,
        mesh=mesh,
        in_specs=placed,
        out_specs=(
            P(("dp", "tensor"), None),
            P(("dp", "tensor"), None),
            P(),
            P(None, None, None, "tensor"),
            P(None, "tensor", None),
            P(),
            P(),
            P(None, None, "tensor"),
            P(None, "tensor", None),
            P(),
        ),
        check_vma=False,
    )
```
